128 devices in a mesh: tm: 8 (over x, z_lo), height: 8 (over z_hi, y), heads: 2 (over core).
Axes of the slice: x: 4, y: 4, z: 4 (z_hi: 2, z_lo: 2; z = z_hi * 2 + z_lo), core: 2. Of those that a mesh axis runs over, the one named last changes fastest.
Arguments:
- query_latent: bfloat16 [8, 8, 4, 128, 1536], P('tm', 'height', None, None, 'heads'), may hold values from -19 to 19
- key_latent: bfloat16 [8, 8, 4, 128, 1536], P('tm', 'height', None, None, 'heads'), may hold values from -19 to 19
- value_latent: bfloat16 [8, 8, 4, 128, 1536], P('tm', 'height', None, None, 'heads'), may hold values from -6 to 6
- grad_latent: bfloat16 [8, 8, 4, 128, 1536], P('tm', 'height', None, None, 'heads'), may hold values from -6 to 6
- tile_lists: int32 [8, 8, 4, 27], P('tm', 'height'), may hold values from -1 to 255, as said below
- text_query: bfloat16 [256, 1536], P(None, 'heads'), may hold values from -19 to 19
- text_key: bfloat16 [256, 1536], P(None, 'heads'), may hold values from -6 to 6
- text_value: bfloat16 [256, 1536], P(None, 'heads'), may hold values from -6 to 6
- grad_text: bfloat16 [256, 1536], P(None, 'heads'), may hold values from -6 to 6
- text_mask: int32 [256], replicated, may hold values 0 or 1
Outputs:
- out_latent: bfloat16 [8, 8, 4, 128, 1536], P('tm', 'height', None, None, 'heads')
- grad_q_latent: bfloat16 [8, 8, 4, 128, 1536], P('tm', 'height', None, None, 'heads')
- grad_k_latent: bfloat16 [8, 8, 4, 128, 1536], P('tm', 'height', None, None, 'heads')
- grad_v_latent: bfloat16 [8, 8, 4, 128, 1536], P('tm', 'height', None, None, 'heads')
- out_text: bfloat16 [256, 1536], P(None, 'heads')
- grad_q_text: bfloat16 [256, 1536], P(None, 'heads')
- grad_k_text: bfloat16 [256, 1536], P(None, 'heads')
- grad_v_text: bfloat16 [256, 1536], P(None, 'heads')
The draws below stay inside these ranges and needn't reach their ends.
Inputs may be any that keep to these rules, and one draw needn't show every extreme that they name: `tile_lists`: entry 9 * a + 3 * b + c of query tile (f, r, w), a, b, c in 0..2, is -1 if frame tile f + a - 1 or row tile r + b - 1 lies outside the grid, else the index of tile (f + a - 1, r + b - 1, s + c), where s is an integer with max(0, w - 2) <= s <= min(w, 1) chosen per query tile and pair (a, b).
All inputs are finite; a program needn't handle non-finite values.
Results may differ from the reference program's by a relative error of at most 0.04.
Values may be sent and summed in bfloat16 or wider, within the bound.
A program may use at most 192 MiB of HBM per device.

```python
import math
import jax
import jax.numpy as jnp
from jax import lax

HEADS = 12
HD = 128
TILE = 128
TEXT = 256
TT_DEV = 1
HT_DEV = 1
NWT = 4
NTT = 8
NHT = 8
N_TM = 8
N_HEIGHT = 8


def draw_query_latent(key, part):
    key = jax.random.fold_in(key, 11)
    drawn = 2.0 * jax.random.truncated_normal(key, -4.0, 4.0, (NTT, NHT, NWT, TILE, HEADS * HD), jnp.float32)
    return jnp.clip(drawn, -19.0, 19.0).astype(jnp.bfloat16)


def draw_key_latent(key, part):
    key = jax.random.fold_in(key, 12)
    drawn = jax.random.truncated_normal(key, -4.0, 4.0, (NTT, NHT, NWT, TILE, HEADS * HD), jnp.float32)
    return jnp.clip(drawn, -19.0, 19.0).astype(jnp.bfloat16)


def draw_text_query(key, part):
    key = jax.random.fold_in(key, 13)
    drawn = 2.0 * jax.random.truncated_normal(key, -4.0, 4.0, (TEXT // 32, 32, HEADS * HD), jnp.float32)
    return jnp.clip(drawn, -19.0, 19.0).reshape(TEXT, HEADS * HD).astype(jnp.bfloat16)


def draw_tile_lists(key, part):
    key = jax.random.fold_in(key, 15)
    offsets = jax.random.randint(key, (NTT, NHT, NWT, 3, 3), 0, 3)
    frame_tile = jnp.arange(NTT)[:, None, None, None, None, None] + jnp.arange(3)[None, None, None, :, None, None] - 1
    row_tile = jnp.arange(NHT)[None, :, None, None, None, None] + jnp.arange(3)[None, None, None, None, :, None] - 1
    column = jnp.arange(NWT)[None, None, :, None, None, None]
    start = jnp.clip(column - offsets[..., None], 0, NWT - 3)
    columns = start + jnp.arange(3)[None, None, None, None, None, :]
    inside = (frame_tile >= 0) & (frame_tile < NTT) & (row_tile >= 0) & (row_tile < NHT)
    index = (frame_tile * NHT + row_tile) * NWT + columns
    index = jnp.where(inside, index, -1)
    return jnp.broadcast_to(index, (NTT, NHT, NWT, 3, 3, 3)).reshape(NTT, NHT, NWT, 27).astype(jnp.int32)


def place_ends(drawn, own_key, smallest, high):
    shape = drawn.shape
    spot = [jax.random.randint(jax.random.fold_in(own_key, axis), (), 0, shape[axis]) for axis in range(len(shape))]
    drawn = drawn.at[tuple(spot)].set(smallest)
    longest = shape.index(max(shape))
    spot[longest] = (spot[longest] + 1) % shape[longest]
    return drawn.at[tuple(spot)].set(high)


def block_scale(key, extent, shards, low, largest):
    gain = 1.0
    for axis_at, shards_of in shards:
        draws = jax.random.uniform(jax.random.fold_in(jax.random.fold_in(key, 6), axis_at), (shards_of,), jnp.float32, low / len(shards), largest / len(shards))
        gain = gain * jnp.repeat(jnp.exp(draws), extent[axis_at] // shards_of).reshape((-1,) + (1,) * (len(extent) - 1 - axis_at))
    return gain


def bell_draw(own_key, extent, width, reach, shards=(), kind=jnp.bfloat16):
    factor_of = block_scale(own_key, extent, shards, -0.22, 0.18) if shards else 1.0
    values = jax.random.normal(own_key, extent, jnp.float32) * width * factor_of
    return jnp.minimum(jnp.maximum(values, -reach), reach).astype(kind)


def setup_inputs(seed: int = 0) -> dict:
    arg_keys = jax.random.split(jax.random.key(seed), 11)
    return {
        "query_latent": draw_query_latent(jax.random.fold_in(arg_keys[10], 71), 0),
        "key_latent": draw_key_latent(jax.random.fold_in(arg_keys[10], 71), 0),
        "value_latent": bell_draw(arg_keys[2], (NTT, NHT, NWT, TILE, HEADS * HD), 1.0, 6.0, ((0, 8), (1, 8), (4, 2))),
        "grad_latent": bell_draw(arg_keys[3], (NTT, NHT, NWT, TILE, HEADS * HD), 1.0, 6.0, ((0, 8), (1, 8), (4, 2))),
        "tile_lists": draw_tile_lists(jax.random.fold_in(arg_keys[10], 71), 0),
        "text_query": draw_text_query(jax.random.fold_in(arg_keys[10], 71), 0),
        "text_key": bell_draw(arg_keys[6], (TEXT, HEADS * HD), 1.0, 6.0, ((1, 2),)),
        "text_value": bell_draw(arg_keys[7], (TEXT, HEADS * HD), 1.0, 6.0, ((1, 2),)),
        "grad_text": bell_draw(arg_keys[8], (TEXT, HEADS * HD), 1.0, 6.0, ((1, 2),)),
        "text_mask": place_ends((jax.random.randint(arg_keys[9], (TEXT,), 0, 2) < 1).astype(jnp.int32), jax.random.fold_in(arg_keys[9], 1), 0, 1),
    }


def window_slots(tile_lists, start_t, start_h, rows_tiles, width_tiles, pad_rows):
    frame_tile = tile_lists // (rows_tiles * width_tiles)
    row_tile = tile_lists // width_tiles % rows_tiles
    column_tile = tile_lists % width_tiles
    local = ((frame_tile - start_t + 1) * pad_rows + (row_tile - start_h + 1)) * width_tiles + column_tile
    present = tile_lists >= 0
    return (jnp.where(present, local, 0).astype(jnp.int32), present)

def group_latent(query, padded, tile_lists, key_text, value_text, text_on, grad_out, start_t, start_h, rows_tiles, head_dim, score_scale):
    frames, rows, width_tiles, tile, channels = query.shape
    heads = channels // head_dim
    flat_keys = padded[0].reshape(-1, tile, channels)
    flat_values = padded[1].reshape(-1, tile, channels)
    slots, present = window_slots(tile_lists, start_t, start_h, rows_tiles, width_tiles, rows + 2)
    count_pairs = frames * rows * width_tiles // 2
    query_rows = query.reshape(count_pairs, 2, tile, heads, head_dim)
    grad_rows = grad_out.reshape(count_pairs, 2, tile, heads, head_dim)
    slot_rows = slots.reshape(count_pairs, -1)
    on_rows = present.reshape(count_pairs, 2, -1)
    key_t32 = key_text.astype(jnp.float32)
    value_t32 = value_text.astype(jnp.float32)

    def one_pair(carry, inputs):
        totals, text_dk, text_dv = carry
        query_part, grad_part, slot_part, on_part = inputs
        keys = flat_keys[slot_part].reshape(2, -1, heads, head_dim).astype(jnp.float32)
        values = flat_values[slot_part].reshape(2, -1, heads, head_dim).astype(jnp.float32)
        key_on = jnp.repeat(on_part, tile, axis=1)
        query32 = query_part.astype(jnp.float32)
        grad32 = grad_part.astype(jnp.float32)
        score_window = jnp.einsum('aihd,ajhd->ahij', query32, keys) * score_scale
        score_window = jnp.where(key_on[:, None, None, :], score_window, -jnp.inf)
        score_words = jnp.einsum('aihd,jhd->ahij', query32, key_t32) * score_scale
        score_words = jnp.where(text_on[None, None, None, :], score_words, -jnp.inf)
        peak = jnp.maximum(lax.optimization_barrier(jnp.max(score_window, -1)), lax.optimization_barrier(jnp.max(score_words, -1)))
        total = lax.optimization_barrier(jnp.sum(jnp.exp(score_window - peak[..., None]), -1)) + lax.optimization_barrier(jnp.sum(jnp.exp(score_words - peak[..., None]), -1))
        log_total = (peak + jnp.log(total))[..., None]
        prob_window = jnp.exp(score_window - log_total)
        prob_words = jnp.exp(score_words - log_total)
        weight_window = prob_window.astype(jnp.bfloat16).astype(jnp.float32)
        weight_words = prob_words.astype(jnp.bfloat16).astype(jnp.float32)
        result = jnp.einsum('ahij,ajhd->aihd', weight_window, values) + jnp.einsum('ahij,jhd->aihd', weight_words, value_t32)
        result = result.astype(jnp.bfloat16)
        row_delta = jnp.transpose(lax.optimization_barrier(jnp.sum(grad32 * result.astype(jnp.float32), -1)), (0, 2, 1))[..., None]
        dscore_window = (prob_window * (jnp.einsum('aihd,ajhd->ahij', grad32, values) - row_delta)).astype(jnp.bfloat16).astype(jnp.float32)
        dscore_words = (prob_words * (jnp.einsum('aihd,jhd->ahij', grad32, value_t32) - row_delta)).astype(jnp.bfloat16).astype(jnp.float32)
        grad_query = (jnp.einsum('ahij,ajhd->aihd', dscore_window, keys) + jnp.einsum('ahij,jhd->aihd', dscore_words, key_t32)) * score_scale
        grad_keys = jnp.einsum('ahij,aihd->ajhd', dscore_window, query32) * score_scale
        grad_values = jnp.einsum('ahij,aihd->ajhd', weight_window, grad32)
        totals = totals.at[0, slot_part].add(grad_keys.reshape(-1, tile, channels))
        totals = totals.at[1, slot_part].add(grad_values.reshape(-1, tile, channels))
        text_dk = text_dk + jnp.einsum('ahij,aihd->jhd', dscore_words, query32) * score_scale
        text_dv = text_dv + jnp.einsum('ahij,aihd->jhd', weight_words, grad32)
        outputs = (result.reshape(2, tile, channels), grad_query.astype(jnp.bfloat16).reshape(2, tile, channels))
        return ((totals, text_dk, text_dv), outputs)
    zero_pad = jnp.zeros((2, flat_keys.shape[0], tile, channels), jnp.float32)
    zero_text = jnp.zeros(key_text.shape, jnp.float32)
    carry, stacked = lax.scan(one_pair, (zero_pad, zero_text, zero_text), (query_rows, grad_rows, slot_rows, on_rows))
    totals, text_dk, text_dv = carry
    totals = totals.reshape((2, frames + 2, rows + 2, width_tiles, tile, channels))
    return (totals, text_dk, text_dv, stacked[0].reshape(query.shape), stacked[1].reshape(query.shape))

def text_heads(text_query, text_key, text_value, grad_text, key_latent, value_latent, text_on, heads, head_dim, score_scale):

    def pick(array, head):
        return lax.dynamic_index_in_dim(array.reshape(array.shape[0], heads, head_dim), head, 1, keepdims=False)

    def one_head(head):
        query = pick(text_query, head)
        grad_head = pick(grad_text, head)
        key_all = pick(key_latent, head)
        value_all = pick(value_latent, head)
        key_words = pick(text_key, head)
        value_words = pick(text_value, head)
        score_all = jnp.dot(query, key_all.T, preferred_element_type=jnp.float32) * score_scale
        score_words = jnp.dot(query, key_words.T, preferred_element_type=jnp.float32) * score_scale
        score_words = jnp.where(text_on[None, :], score_words, -jnp.inf)
        peak = jnp.maximum(lax.optimization_barrier(jnp.max(score_all, -1)), lax.optimization_barrier(jnp.max(score_words, -1)))
        total = lax.optimization_barrier(jnp.sum(jnp.exp(score_all - peak[:, None]), -1)) + lax.optimization_barrier(jnp.sum(jnp.exp(score_words - peak[:, None]), -1))
        log_total = (peak + jnp.log(total))[:, None]
        prob_all = jnp.exp(score_all - log_total)
        prob_words = jnp.exp(score_words - log_total)
        weight_all = prob_all.astype(jnp.bfloat16)
        weight_words = prob_words.astype(jnp.bfloat16)
        result = jnp.dot(weight_all, value_all, preferred_element_type=jnp.float32) + jnp.dot(weight_words, value_words, preferred_element_type=jnp.float32)
        result = result.astype(jnp.bfloat16)
        row_delta = lax.optimization_barrier(jnp.sum(grad_head.astype(jnp.float32) * result.astype(jnp.float32), -1))[:, None]
        dscore_all = (prob_all * (jnp.dot(grad_head, value_all.T, preferred_element_type=jnp.float32) - row_delta)).astype(jnp.bfloat16)
        dscore_words = (prob_words * (jnp.dot(grad_head, value_words.T, preferred_element_type=jnp.float32) - row_delta)).astype(jnp.bfloat16)
        grad_query = (jnp.dot(dscore_all, key_all, preferred_element_type=jnp.float32) + jnp.dot(dscore_words, key_words, preferred_element_type=jnp.float32)) * score_scale
        grad_key_all = jnp.dot(dscore_all.T, query, preferred_element_type=jnp.float32) * score_scale
        grad_value_all = jnp.dot(weight_all.T, grad_head, preferred_element_type=jnp.float32)
        grad_key_words = jnp.dot(dscore_words.T, query, preferred_element_type=jnp.float32) * score_scale
        grad_value_words = jnp.dot(weight_words.T, grad_head, preferred_element_type=jnp.float32)
        return (result, grad_query, grad_key_all, grad_value_all, grad_key_words, grad_value_words)
    return lax.map(one_head, jnp.arange(heads, dtype=jnp.int32))

def merge_heads(stacked):
    return jnp.transpose(stacked, (1, 0, 2)).reshape(stacked.shape[1], -1)

def reference(query_latent, key_latent, value_latent, grad_latent, tile_lists, text_query, text_key, text_value, grad_text, text_mask):
    frames_all, rows_all, width_tiles, tile, channels = query_latent.shape
    head_dim = HD
    heads = channels // head_dim
    score_scale = 1.0 / math.sqrt(head_dim)
    text_on = text_mask > 0
    both = jnp.stack([key_latent, value_latent])
    padded_all = jnp.pad(both, ((0, 0), (1, 1), (1, 1), (0, 0), (0, 0), (0, 0)))
    key_text = text_key.reshape(-1, heads, head_dim)
    value_text = text_value.reshape(-1, heads, head_dim)

    def one_group(carry, index):
        totals, text_dk, text_dv = carry
        start_t = index // N_HEIGHT * TT_DEV
        start_h = index % N_HEIGHT * HT_DEV
        zero = jnp.int32(0)
        query = lax.dynamic_slice(query_latent, (start_t, start_h, zero, zero, zero), (TT_DEV, HT_DEV, width_tiles, tile, channels))
        grad_out = lax.dynamic_slice(grad_latent, (start_t, start_h, zero, zero, zero), (TT_DEV, HT_DEV, width_tiles, tile, channels))
        lists = lax.dynamic_slice(tile_lists, (start_t, start_h, zero, zero), (TT_DEV, HT_DEV, width_tiles, tile_lists.shape[3]))
        window = lax.dynamic_slice(padded_all, (zero, start_t, start_h, zero, zero, zero), (2, TT_DEV + 2, HT_DEV + 2, width_tiles, tile, channels))
        share, part_dk, part_dv, result, grad_query = group_latent(query, window, lists, key_text, value_text, text_on, grad_out, start_t, start_h, rows_all, head_dim, score_scale)
        rounded = lax.optimization_barrier(share.astype(jnp.bfloat16)).astype(jnp.float32)
        current = lax.dynamic_slice(totals, (zero, start_t, start_h, zero, zero, zero), rounded.shape)
        totals = lax.dynamic_update_slice(totals, current + rounded, (zero, start_t, start_h, zero, zero, zero))
        return ((totals, text_dk + part_dk, text_dv + part_dv), (result, grad_query))
    zero_all = jnp.zeros((2, frames_all + 2, rows_all + 2, width_tiles, tile, channels), jnp.float32)
    zero_text = jnp.zeros(key_text.shape, jnp.float32)
    carry, stacked = lax.scan(one_group, (zero_all, zero_text, zero_text), jnp.arange(N_TM * N_HEIGHT, dtype=jnp.int32))
    totals, text_dk, text_dv = carry

    def regroup(array):
        shaped = array.reshape(N_TM, N_HEIGHT, TT_DEV, HT_DEV, width_tiles, tile, channels)
        return jnp.transpose(shaped, (0, 2, 1, 3, 4, 5, 6)).reshape(query_latent.shape)
    out_latent = regroup(stacked[0])
    grad_q_latent = regroup(stacked[1])
    flat_keys = key_latent.reshape(-1, channels)
    flat_values = value_latent.reshape(-1, channels)
    result, grad_query, grad_key_all, grad_value_all, grad_key_words, grad_value_words = text_heads(text_query, text_key, text_value, grad_text, flat_keys, flat_values, text_on, heads, head_dim, score_scale)
    latent_dk = totals[0, 1:-1, 1:-1] + merge_heads(grad_key_all).reshape(query_latent.shape)
    latent_dv = totals[1, 1:-1, 1:-1] + merge_heads(grad_value_all).reshape(query_latent.shape)
    out_text = merge_heads(result)
    grad_q_text = merge_heads(grad_query).astype(jnp.bfloat16)
    grad_k_text = (text_dk.reshape(-1, channels) + merge_heads(grad_key_words)).astype(jnp.bfloat16)
    grad_v_text = (text_dv.reshape(-1, channels) + merge_heads(grad_value_words)).astype(jnp.bfloat16)
    return (out_latent, grad_q_latent, latent_dk.astype(jnp.bfloat16), latent_dv.astype(jnp.bfloat16), out_text, grad_q_text, grad_k_text, grad_v_text)
```

```python
import functools
import math

import jax
import jax.numpy as jnp
from jax import lax
from jax.experimental import pallas as pl
from jax.experimental.pallas import tpu as pltpu
from jax.sharding import PartitionSpec as P

HD = 128
NEG = -1e30
F32 = jnp.float32
BF16 = jnp.bfloat16
MESH = pl.DeviceIdType.MESH


def mm_nt(a, b):
    return lax.dot_general(a, b, (((1,), (1,)), ((), ())), preferred_element_type=F32)


def mm_tn(a, b):
    return lax.dot_general(a, b, (((0,), (0,)), ((), ())), preferred_element_type=F32)


def mm_nn(a, b):
    return jnp.dot(a, b, preferred_element_type=F32)


def window_kernel(
    nx,
    ny,
    q_ref,
    k_ref,
    v_ref,
    g_ref,
    mask_ref,
    tk_ref,
    tv_ref,
    tm_ref,
    out_ref,
    dq_ref,
    dk_ref,
    dv_ref,
    td_ref,
    kv,
    qg,
    mask,
    p_mid,
    p_side,
    p_text,
    m_saved,
    m_run,
    l_run,
    d_row,
    o_t,
    dq_t,
    share,
    g1r,
    g2r,
    fin,
    sem_loc,
    sem_r1s,
    sem_r1r,
    sem_mask,
    sem_r2s,
    sem_r2r,
    sem_r3s,
    sem_r3r,
    sem_g1s,
    sem_g1r,
    sem_g2s,
    sem_g2r,
    sem_g3s,
    sem_g3r,
    sem_out,
):
    bq = q_ref.shape[0]
    tile = bq // 4
    heads = q_ref.shape[1] // HD
    nh = heads // 2
    both = 2 * bq
    scale = 1.0 / math.sqrt(HD)
    c2 = scale * math.log2(math.e)

    t = lax.axis_index("tm")
    h = lax.axis_index("height")
    c = lax.axis_index("heads")
    x = t // 2
    zl = t % 2
    zh = h // ny
    half = (zl + zh) % 2
    other = 1 - half
    rows_all = 2 * ny

    def at_height(hh):
        return (2 * x + (half + hh // ny) % 2, hh, c)

    partner = (2 * x + 1 - zl, h, c)
    left = (t - 2, h, c)
    right = (t + 2, h, c)
    up = at_height(h - 1)
    down = at_height(h + 1)
    has_left = x > 0
    has_right = x < nx - 1
    has_up = h > 0
    has_down = h < rows_all - 1

    barrier = pltpu.get_barrier_semaphore()
    greet = [
        (None, partner),
        (has_left, left),
        (has_right, right),
        (has_up, up),
        (has_down, down),
    ]
    for cond, dev in greet:
        def hello(dev=dev):
            pl.semaphore_signal(barrier, inc=1, device_id=dev, device_id_type=MESH)

        if cond is None:
            hello()
        else:
            pl.when(cond)(hello)
    count = (
        1
        + has_left.astype(jnp.int32)
        + has_right.astype(jnp.int32)
        + has_up.astype(jnp.int32)
        + has_down.astype(jnp.int32)
    )
    pl.semaphore_wait(barrier, count)

    def remote(src, dst, ssem, rsem, dev):
        return pltpu.make_async_remote_copy(
            src_ref=src, dst_ref=dst, send_sem=ssem, recv_sem=rsem,
            device_id=dev, device_id_type=MESH,
        )

    def head_cols(which, i):
        return pl.ds(pl.multiple_of((which * nh + i) * HD, HD), HD)

    ins = (q_ref, k_ref, v_ref, g_ref)
    outs = (out_ref, dq_ref, dk_ref, dv_ref)

    def landing(i, j):
        if j == 0:
            return qg.at[i, 0, pl.ds(pl.multiple_of(zl * bq, bq), bq)]
        if j == 3:
            return qg.at[i, 1, pl.ds(pl.multiple_of(zl * bq, bq), bq)]
        return kv.at[i, j - 1, 1, 1 + zl]

    def r1(i, j):
        return remote(
            ins[j].at[:, head_cols(other, i)], landing(i, j),
            sem_r1s.at[i, j], sem_r1r.at[i, j], partner,
        )

    def local_in(i, j):
        return pltpu.make_async_copy(
            ins[j].at[:, head_cols(half, i)], landing(i, j), sem_loc.at[i, j]
        )

    mask_cols = pl.ds(pl.multiple_of(zl * bq, bq), bq)
    mask_out = remote(mask_ref, mask.at[:, mask_cols], sem_mask.at[0], sem_mask.at[1], partner)
    mask_own = pltpu.make_async_copy(mask_ref, mask.at[:, mask_cols], sem_mask.at[2])

    def r2(i, d):
        return remote(
            kv.at[i, :, 1, pl.ds(1, 2)], kv.at[i, :, 2 - 2 * d, pl.ds(1, 2)],
            sem_r2s.at[i, d], sem_r2r.at[i, d], (up, down)[d],
        )

    def r3(i, r, d):
        return remote(
            kv.at[i, :, r, 1 + d], kv.at[i, :, r, 3 - 3 * d],
            sem_r3s.at[i, r, d], sem_r3r.at[i, r, d], (left, right)[d],
        )

    def g1(i, r, d):
        return remote(
            share.at[i, :, r, 3 * d], g1r.at[i, d, :, r],
            sem_g1s.at[i, r, d], sem_g1r.at[i, r, d], (left, right)[d],
        )

    def g2(i, d):
        return remote(
            share.at[i, :, 2 * d, pl.ds(1, 2)], g2r.at[i, d],
            sem_g2s.at[i, d], sem_g2r.at[i, d], (up, down)[d],
        )

    def g3(i, j):
        return remote(
            fin.at[i, j, pl.ds(pl.multiple_of((1 - zl) * bq, bq), bq)],
            outs[j].at[:, head_cols(half, i)],
            sem_g3s.at[i, j], sem_g3r.at[i, j], partner,
        )

    def local_out(i, j):
        return pltpu.make_async_copy(
            fin.at[i, j, pl.ds(pl.multiple_of(zl * bq, bq), bq)],
            outs[j].at[:, head_cols(half, i)], sem_out.at[i, j],
        )

    def row_on(r):
        return (h + r - 1 >= 0) & (h + r - 1 < rows_all)

    side_on = (has_left, has_right)
    vert_on = (has_up, has_down)

    def wait_r1(i):
        for j in range(4):
            local_in(i, j).wait()
            r1(i, j).wait_recv()

    def start_r2(i):
        for d in range(2):
            pl.when(vert_on[d])(lambda d=d: r2(i, d).start())

    def wait_r2(i):
        for d in range(2):
            pl.when(vert_on[1 - d])(lambda d=d: r2(i, d).wait_recv())

    def for_sides(i, rows, act, flip):
        for r in rows:
            for d in range(2):
                on = side_on[1 - d] if flip else side_on[d]
                if r != 1:
                    on = on & row_on(r)
                pl.when(on)(lambda r=r, d=d: act(i, r, d))

    def start_r3(i, rows):
        for_sides(i, rows, lambda i, r, d: r3(i, r, d).start(), False)

    def wait_r3(i):
        for_sides(i, (0, 1, 2), lambda i, r, d: r3(i, r, d).wait_recv(), True)

    @pl.loop(0, nh)
    def _(i):
        for j in range(4):
            r1(i, j).start()
            local_in(i, j).start()

    mask_out.start()
    mask_own.start()

    @pl.loop(0, nh)
    def _(i):
        @pl.when(jnp.logical_not(has_right))
        def _():
            g1r[i, 0] = jnp.zeros(g1r.shape[2:], BF16)

        @pl.when(jnp.logical_not(has_left))
        def _():
            g1r[i, 1] = jnp.zeros(g1r.shape[2:], BF16)

        @pl.when(jnp.logical_not(has_down))
        def _():
            g2r[i, 0] = jnp.zeros(g2r.shape[2:], BF16)

        @pl.when(jnp.logical_not(has_up))
        def _():
            g2r[i, 1] = jnp.zeros(g2r.shape[2:], BF16)

    mask_own.wait()
    mask_out.wait_recv()
    wait_r1(0)
    start_r2(0)
    start_r3(0, (1,))

    def online(s, v, save, qs, keep):
        m_old = m_run[0:1, qs]
        m_new = jnp.maximum(m_old, jnp.max(s, 0, keepdims=True))
        alpha = jnp.exp2(m_old - m_new)
        e = jnp.exp2(s - m_new)
        l_run[0:1, qs] = l_run[0:1, qs] * alpha + jnp.sum(e, 0, keepdims=True)
        m_run[0:1, qs] = m_new
        m_saved[pl.ds(save, 1), qs] = m_new
        w = e.astype(BF16)
        keep(w)
        o_t[:, qs] = o_t[:, qs] * alpha + mm_tn(v, w)

    def fwd(i, row, col, qs, keep):
        s = mm_nt(kv[i, 0, row, col], qg[i, 0, qs]) * c2
        at = (col * 3 + row) * 2
        first = mask[pl.ds(at, 1), qs]
        last = mask[pl.ds(at + 1, 1), qs]
        s = jnp.concatenate(
            [
                jnp.where(first > 0.5, s[:tile], NEG),
                s[tile : 3 * tile],
                jnp.where(last > 0.5, s[3 * tile :], NEG),
            ],
            axis=0,
        )
        online(s, kv[i, 1, row, col], col * 3 + row, qs, keep)

    def fwd_mid(i, row, col):
        def keep(w):
            p_mid[row, col - 1] = w

        fwd(i, row, col, pl.ds(0, both), keep)

    def fwd_side(i, row, d):
        def keep(w):
            p_side[row, d] = w

        fwd(i, row, 3 * d, pl.ds(d * bq, bq), keep)

    def back(w0, k, v, q, g, save, qs):
        f = jnp.exp2(m_saved[pl.ds(save, 1), qs] - m_run[0:1, qs]) * l_run[0:1, qs]
        dp = mm_nt(v, g)
        w = w0.astype(F32) * f
        ds = (w * (dp - d_row[0:1, qs])).astype(BF16)
        d_k = mm_nn(ds, q) * scale
        d_v = mm_nn(w.astype(BF16), g)
        dq_t[:, qs] += mm_tn(k, ds)
        return d_k, d_v

    def bwd(i, row, col, qs, w0):
        d_k, d_v = back(
            w0, kv[i, 0, row, col], kv[i, 1, row, col], qg[i, 0, qs], qg[i, 1, qs],
            col * 3 + row, qs,
        )
        share[i, 0, row, col] = d_k.astype(BF16)
        share[i, 1, row, col] = d_v.astype(BF16)

    def add_g1(i):
        for_sides(i, (0, 1, 2), lambda i, r, d: g1(i, r, d).wait_recv(), True)
        for r in (0, 2):
            @pl.when(row_on(r))
            def _(r=r):
                for a in range(2):
                    for d in range(2):
                        col = 2 - d
                        share[i, a, r, col] = (
                            share[i, a, r, col].astype(F32) + g1r[i, d, a, r].astype(F32)
                        ).astype(BF16)
        for d in range(2):
            pl.when(vert_on[d])(lambda d=d: g2(i, d).start())

    def add_g2(i):
        for d in range(2):
            pl.when(vert_on[1 - d])(lambda d=d: g2(i, d).wait_recv())
        for a in range(2):
            for s in range(2):
                total = (
                    share[i, a, 1, 1 + s].astype(F32)
                    + g1r[i, 1 - s, a, 1].astype(F32)
                    + g2r[i, 0, a, s].astype(F32)
                    + g2r[i, 1, a, s].astype(F32)
                )
                fin[i, 2 + a, s * bq : (s + 1) * bq] = total.astype(BF16)
        for j in (2, 3):
            g3(i, j).start()
            local_out(i, j).start()

    @pl.loop(0, nh)
    def _(i):
        m_run[0:1, :] = jnp.full((1, both), NEG, F32)
        l_run[0:1, :] = jnp.zeros((1, both), F32)
        o_t[...] = jnp.zeros(o_t.shape, F32)
        dq_t[...] = jnp.zeros(dq_t.shape, F32)

        @pl.loop(1, 3)
        def _(col):
            fwd_mid(i, 1, col)

        @pl.when(i == 0)
        def _():
            wait_r1(1)
            start_r2(1)
            start_r3(1, (1,))
            wait_r2(0)
            start_r3(0, (0, 2))

        @pl.loop(0, 4)
        def _(n):
            row = (n // 2) * 2

            @pl.when(row_on(row))
            def _():
                fwd_mid(i, row, 1 + n % 2)

        @pl.when(i == 0)
        def _():
            wait_r1(2)
            start_r2(2)
            start_r3(2, (1,))

        @pl.when(i < nh - 1)
        def _():
            wait_r2(i + 1)
            start_r3(i + 1, (0, 2))

        words = head_cols(half, i)
        s_text = jnp.where(
            tm_ref[:, 0:1] > 0.5, mm_nt(tk_ref[:, words], qg[i, 0]) * c2, NEG
        )

        def keep_text(w):
            p_text[...] = w

        online(s_text, tv_ref[:, words], 12, pl.ds(0, both), keep_text)

        @pl.when(i > 0)
        def _():
            add_g1(i - 1)

        wait_r3(i)
        for d in range(2):
            @pl.when(side_on[d])
            def _(d=d):
                @pl.loop(0, 3)
                def _(row):
                    @pl.when(row_on(row))
                    def _():
                        fwd_side(i, row, d)

        inv = 1.0 / l_run[0:1, :]
        l_run[0:1, :] = inv
        o_round = (o_t[...] * inv).astype(BF16).astype(F32)
        fin[i, 0] = o_round.T.astype(BF16)
        g_t = qg[i, 1].astype(F32).T
        d_row[0:1, :] = jnp.sum(o_round * g_t, 0, keepdims=True)
        g3(i, 0).start()
        local_out(i, 0).start()

        d_k, d_v = back(
            p_text[...], tk_ref[:, words], tv_ref[:, words], qg[i, 0], qg[i, 1],
            12, pl.ds(0, both),
        )
        td_ref[i, 0] = d_k
        td_ref[i, 1] = d_v

        for d in range(2):
            @pl.when(side_on[d])
            def _(d=d):
                @pl.loop(0, 3)
                def _(row):
                    @pl.when(row_on(row))
                    def _():
                        bwd(i, row, 3 * d, pl.ds(d * bq, bq), p_side[row, d])
                        g1(i, row, d).start()

        @pl.when(i > 0)
        def _():
            add_g2(i - 1)

        @pl.loop(0, 6)
        def _(n):
            row = n // 2
            col = 1 + n % 2

            @pl.when(row_on(row))
            def _():
                bwd(i, row, col, pl.ds(0, both), p_mid[row, col - 1])

        fin[i, 1] = (dq_t[...] * scale).T.astype(BF16)
        g3(i, 1).start()
        local_out(i, 1).start()

    add_g1(nh - 1)
    add_g2(nh - 1)

    mask_out.wait_send()

    @pl.loop(0, nh)
    def _(i):
        for j in range(4):
            r1(i, j).wait_send()
            g3(i, j).wait_send()
            g3(i, j).wait_recv()
            local_out(i, j).wait()
        for d in range(2):
            @pl.when(vert_on[d])
            def _(d=d):
                r2(i, d).wait_send()
                g2(i, d).wait_send()
        for_sides(i, (0, 1, 2), lambda i, r, d: r3(i, r, d).wait_send(), False)
        for_sides(i, (0, 1, 2), lambda i, r, d: g1(i, r, d).wait_send(), False)


def window_pass(query, key, value, grad, mask, text_key, text_value, text_mask):
    nx = lax.axis_size("tm") // 2
    ny = lax.axis_size("height") // 2
    bq, channels = query.shape
    nh = channels // HD // 2
    words = text_key.shape[0]
    both = 2 * bq
    sds = jax.ShapeDtypeStruct
    hbm = pl.BlockSpec(memory_space=pl.ANY)
    vmem = pl.BlockSpec(memory_space=pltpu.VMEM)
    dma = pltpu.SemaphoreType.DMA
    return pl.pallas_call(
        functools.partial(window_kernel, nx, ny),
        out_shape=[sds((bq, channels), BF16)] * 4 + [sds((nh, 2, words, HD), F32)],
        in_specs=[hbm, hbm, hbm, hbm, vmem, vmem, vmem, vmem],
        out_specs=[hbm] * 4 + [vmem],
        scratch_shapes=[
            pltpu.VMEM((nh, 2, 3, 4, bq, HD), BF16),
            pltpu.VMEM((nh, 2, both, HD), BF16),
            pltpu.VMEM((24, both), F32),
            pltpu.VMEM((3, 2, bq, both), BF16),
            pltpu.VMEM((3, 2, bq, bq), BF16),
            pltpu.VMEM((words, both), BF16),
            pltpu.VMEM((16, both), F32),
            pltpu.VMEM((8, both), F32),
            pltpu.VMEM((8, both), F32),
            pltpu.VMEM((8, both), F32),
            pltpu.VMEM((HD, both), F32),
            pltpu.VMEM((HD, both), F32),
            pltpu.VMEM((nh, 2, 3, 4, bq, HD), BF16),
            pltpu.VMEM((nh, 2, 2, 3, bq, HD), BF16),
            pltpu.VMEM((nh, 2, 2, 2, bq, HD), BF16),
            pltpu.VMEM((nh, 4, both, HD), BF16),
            dma((nh, 4)),
            dma((nh, 4)),
            dma((nh, 4)),
            dma((3,)),
            dma((nh, 2)),
            dma((nh, 2)),
            dma((nh, 3, 2)),
            dma((nh, 3, 2)),
            dma((nh, 3, 2)),
            dma((nh, 3, 2)),
            dma((nh, 2)),
            dma((nh, 2)),
            dma((nh, 4)),
            dma((nh, 4)),
            dma((nh, 4)),
        ],
        compiler_params=pltpu.CompilerParams(
            collective_id=0, has_side_effects=True, vmem_limit_bytes=62 * 2**20
        ),
        name="window",
    )(query, key, value, grad, mask, text_key, text_value, text_mask)


def edge_mask(tile_lists, tile, slot):
    lists = tile_lists.reshape(4, 3, 3, 3)
    rows = []
    for col in (0, 3):
        on = jnp.any((lists >= 0) & (lists % 4 == col), axis=-1)
        rows.append(on)
    on = jnp.stack(rows, -1)
    on = jnp.transpose(on, (1, 2, 3, 0)).reshape(18, 4).astype(F32)
    on = jnp.repeat(on, tile, axis=1)
    pad = jnp.zeros((6, on.shape[1]), F32)
    return jnp.where(
        slot == 0, jnp.concatenate([on, pad]), jnp.concatenate([pad, on])
    )


def body(
    query_latent,
    key_latent,
    value_latent,
    grad_latent,
    tile_lists,
    text_query,
    text_key,
    text_value,
    grad_text,
    text_mask,
):
    frames, rows, width_tiles, tile, channels = query_latent.shape
    head_dim = HD
    heads = channels // head_dim
    nh = heads // 2
    score_scale = 1.0 / math.sqrt(head_dim)
    text_on = text_mask > 0
    key_text = text_key.reshape(-1, heads, head_dim)
    value_text = text_value.reshape(-1, heads, head_dim)
    query_text = text_query.reshape(-1, heads, head_dim)
    grad_words = grad_text.reshape(-1, heads, head_dim)
    t = lax.axis_index("tm")
    h = lax.axis_index("height")
    half = (t % 2 + h // (lax.axis_size("height") // 2)) % 2
    flat = [
        a.reshape(width_tiles * tile, channels)
        for a in (query_latent, key_latent, value_latent, grad_latent)
    ]
    mask = edge_mask(tile_lists, tile, t % 2)
    tm_cols = jnp.broadcast_to(text_on.astype(F32)[:, None], (text_on.shape[0], HD))
    out_latent, grad_q_latent, win_dk, win_dv, td = window_pass(
        *flat, mask, text_key, text_value, tm_cols
    )
    td = jnp.transpose(td, (1, 2, 0, 3)).reshape(2, -1, nh * head_dim)
    wide = jnp.zeros((2, td.shape[1], channels), F32)
    wide = lax.dynamic_update_slice(
        wide, td, (jnp.int32(0), jnp.int32(0), (half * nh * head_dim).astype(jnp.int32))
    )
    text_dk, text_dv = wide[0], wide[1]

    own_keys = key_latent.reshape(-1, heads, head_dim)
    own_values = value_latent.reshape(-1, heads, head_dim)
    score_own = (
        jnp.einsum("ihd,jhd->hij", query_text, own_keys, preferred_element_type=F32) * score_scale
    )
    score_words = (
        jnp.einsum("ihd,jhd->hij", query_text, key_text, preferred_element_type=F32) * score_scale
    )
    score_words = jnp.where(text_on[None, None, :], score_words, -jnp.inf)
    local_peak = jnp.max(score_own, -1)
    peak = lax.pmax(local_peak, ("tm", "height"))
    peak = jnp.maximum(peak, jnp.max(score_words, -1))
    local_total = jnp.sum(jnp.exp(score_own - peak[..., None]), -1)
    total = lax.psum(local_total, ("tm", "height"))
    total = total + jnp.sum(jnp.exp(score_words - peak[..., None]), -1)
    log_total = (peak + jnp.log(total))[..., None]
    prob_own = jnp.exp(score_own - log_total)
    prob_words = jnp.exp(score_words - log_total)
    weight_own = prob_own.astype(BF16)
    weight_words = prob_words.astype(BF16)
    numer = jnp.einsum(
        "hij,jhd->ihd", weight_own, own_values, preferred_element_type=F32
    ).reshape(-1, channels)
    numer = lax.psum(numer, ("tm", "height"))
    words_part = jnp.einsum(
        "hij,jhd->ihd", weight_words, value_text, preferred_element_type=F32
    ).reshape(-1, channels)
    out_text = (numer + words_part).astype(BF16)
    row_delta = jnp.transpose(
        jnp.sum(grad_words.astype(F32) * out_text.reshape(-1, heads, head_dim).astype(F32), -1),
        (1, 0),
    )[..., None]
    dscore_own = (
        prob_own
        * (
            jnp.einsum("ihd,jhd->hij", grad_words, own_values, preferred_element_type=F32)
            - row_delta
        )
    ).astype(BF16)
    dscore_words = (
        prob_words
        * (
            jnp.einsum("ihd,jhd->hij", grad_words, value_text, preferred_element_type=F32)
            - row_delta
        )
    ).astype(BF16)
    query_part = (
        jnp.einsum("hij,jhd->ihd", dscore_own, own_keys, preferred_element_type=F32) * score_scale
    )
    own_dk = (
        jnp.einsum("hij,ihd->jhd", dscore_own, query_text, preferred_element_type=F32)
        * score_scale
    )
    own_dv = jnp.einsum("hij,ihd->jhd", weight_own, grad_words, preferred_element_type=F32)
    summed_q, summed_k, summed_v = lax.psum(
        (query_part.reshape(-1, channels), text_dk, text_dv), ("tm", "height")
    )
    words_q = (
        jnp.einsum("hij,jhd->ihd", dscore_words, key_text, preferred_element_type=F32)
        * score_scale
    )
    words_k = (
        jnp.einsum("hij,ihd->jhd", dscore_words, query_text, preferred_element_type=F32)
        * score_scale
    )
    words_v = jnp.einsum("hij,ihd->jhd", weight_words, grad_words, preferred_element_type=F32)
    grad_q_text = (summed_q + words_q.reshape(-1, channels)).astype(BF16)
    grad_k_text = (summed_k + words_k.reshape(-1, channels)).astype(BF16)
    grad_v_text = (summed_v + words_v.reshape(-1, channels)).astype(BF16)
    shape = query_latent.shape
    grad_k_latent = (win_dk.astype(F32) + own_dk.reshape(win_dk.shape)).astype(BF16)
    grad_v_latent = (win_dv.astype(F32) + own_dv.reshape(win_dv.shape)).astype(BF16)
    return (
        out_latent.reshape(shape),
        grad_q_latent.reshape(shape),
        grad_k_latent.reshape(shape),
        grad_v_latent.reshape(shape),
        out_text,
        grad_q_text,
        grad_k_text,
        grad_v_text,
    )


def solution(mesh):
    latent = P("tm", "height", None, None, "heads")
    text = P(None, "heads")
    in_specs = (latent,) * 4 + (P("tm", "height", None, None),) + (text,) * 4 + (P(),)
    out_specs = (latent,) * 4 + (text,) * 4
    return jax.shard_map(body, mesh=mesh, in_specs=in_specs, out_specs=out_specs, check_vma=False)
```

```python
import functools
import math

import jax
import jax.numpy as jnp
from jax import lax
from jax.experimental import pallas as pl
from jax.experimental.pallas import tpu as pltpu
from jax.sharding import PartitionSpec as P

HD = 128
NEG = -1e30
F32 = jnp.float32
BF16 = jnp.bfloat16
MESH = pl.DeviceIdType.MESH


def mm_nt(a, b):
    return lax.dot_general(a, b, (((1,), (1,)), ((), ())), preferred_element_type=F32)


def mm_tn(a, b):
    return lax.dot_general(a, b, (((0,), (0,)), ((), ())), preferred_element_type=F32)


def mm_nn(a, b):
    return jnp.dot(a, b, preferred_element_type=F32)


def window_kernel(
    nx,
    ny,
    q_ref,
    k_ref,
    v_ref,
    g_ref,
    mask_ref,
    tq_ref,
    tk_ref,
    tv_ref,
    tg_ref,
    tm_ref,
    out_ref,
    dq_ref,
    dk_ref,
    dv_ref,
    tout_ref,
    tdq_ref,
    tdk_ref,
    tdv_ref,
    kv,
    qg,
    mask,
    p_mid,
    p_side,
    p_text,
    m_saved,
    m_run,
    l_run,
    d_row,
    o_t,
    dq_t,
    share,
    g1r,
    g2r,
    fin,
    st,
    st_in,
    lse,
    part,
    from_z,
    from_y,
    from_x,
    whole,
    t_kv,
    t_fin,
    sem_loc,
    sem_r1s,
    sem_r1r,
    sem_mask,
    sem_r2s,
    sem_r2r,
    sem_r3s,
    sem_r3r,
    sem_g1s,
    sem_g1r,
    sem_g2s,
    sem_g2r,
    sem_g3s,
    sem_g3r,
    sem_out,
    sem_sts,
    sem_str,
    sem_ars,
    sem_arr,
    sem_tfs,
    sem_tfr,
    sem_tfl,
):
    bq = q_ref.shape[0]
    tile = bq // 4
    heads = q_ref.shape[1] // HD
    nh = heads // 2
    both = 2 * bq
    scale = 1.0 / math.sqrt(HD)
    c2 = scale * math.log2(math.e)

    t = lax.axis_index("tm")
    h = lax.axis_index("height")
    c = lax.axis_index("heads")
    x = t // 2
    zl = t % 2
    zh = h // ny
    half = (zl + zh) % 2
    other = 1 - half
    rows_all = 2 * ny

    def at_height(hh):
        return (2 * x + (half + hh // ny) % 2, hh, c)

    partner = (2 * x + 1 - zl, h, c)
    left = (t - 2, h, c)
    right = (t + 2, h, c)
    up = at_height(h - 1)
    down = at_height(h + 1)
    has_left = x > 0
    has_right = x < nx - 1
    has_up = h > 0
    has_down = h < rows_all - 1

    y = h % ny
    words_n = tq_ref.shape[0]
    lanes = words_n // HD
    z_peer = (2 * x + (half + 1 - zh) % 2, (1 - zh) * ny + y, c)
    y_peers = [(t, zh * ny + (y + p) % ny, c) for p in range(1, ny)]
    x_peers = [(2 * ((x + p) % nx) + zl, h, c) for p in range(1, nx)]
    cross_up = h == ny
    cross_down = h == ny - 1

    barrier = pltpu.get_barrier_semaphore()
    for dev in [partner, z_peer] + y_peers + x_peers:
        pl.semaphore_signal(barrier, inc=1, device_id=dev, device_id_type=MESH)
    for cond, dev in ((cross_up, up), (cross_down, down)):
        @pl.when(cond)
        def _(dev=dev):
            pl.semaphore_signal(barrier, inc=1, device_id=dev, device_id_type=MESH)

    pl.semaphore_wait(
        barrier,
        nx + ny + cross_up.astype(jnp.int32) + cross_down.astype(jnp.int32),
    )

    def remote(src, dst, ssem, rsem, dev):
        return pltpu.make_async_remote_copy(
            src_ref=src, dst_ref=dst, send_sem=ssem, recv_sem=rsem,
            device_id=dev, device_id_type=MESH,
        )

    def head_cols(which, i):
        return pl.ds(pl.multiple_of((which * nh + i) * HD, HD), HD)

    ins = (q_ref, k_ref, v_ref, g_ref)
    outs = (out_ref, dq_ref, dk_ref, dv_ref)

    def landing(i, j):
        if j == 0:
            return qg.at[i, 0, pl.ds(pl.multiple_of(zl * bq, bq), bq)]
        if j == 3:
            return qg.at[i, 1, pl.ds(pl.multiple_of(zl * bq, bq), bq)]
        return kv.at[i, j - 1, 1, 1 + zl]

    def r1(i, j):
        return remote(
            ins[j].at[:, head_cols(other, i)], landing(i, j),
            sem_r1s.at[i, j], sem_r1r.at[i, j], partner,
        )

    def local_in(i, j):
        return pltpu.make_async_copy(
            ins[j].at[:, head_cols(half, i)], landing(i, j), sem_loc.at[i, j]
        )

    mask_cols = pl.ds(pl.multiple_of(zl * bq, bq), bq)
    mask_out = remote(mask_ref, mask.at[:, mask_cols], sem_mask.at[0], sem_mask.at[1], partner)
    mask_own = pltpu.make_async_copy(mask_ref, mask.at[:, mask_cols], sem_mask.at[2])

    def r2(i, d):
        return remote(
            kv.at[i, :, 1, pl.ds(1, 2)], kv.at[i, :, 2 - 2 * d, pl.ds(1, 2)],
            sem_r2s.at[i, d], sem_r2r.at[i, d], (up, down)[d],
        )

    def r3(i, r, d):
        return remote(
            kv.at[i, :, r, 1 + d], kv.at[i, :, r, 3 - 3 * d],
            sem_r3s.at[i, r, d], sem_r3r.at[i, r, d], (left, right)[d],
        )

    def g1(i, r, d):
        return remote(
            share.at[i, :, r, 3 * d], g1r.at[i, d, :, r],
            sem_g1s.at[i, r, d], sem_g1r.at[i, r, d], (left, right)[d],
        )

    def g2(i, d):
        return remote(
            share.at[i, :, 2 * d, pl.ds(1, 2)], g2r.at[i, d],
            sem_g2s.at[i, d], sem_g2r.at[i, d], (up, down)[d],
        )

    def g3(i, j):
        return remote(
            fin.at[i, j, pl.ds(pl.multiple_of((1 - zl) * bq, bq), bq)],
            outs[j].at[:, head_cols(half, i)],
            sem_g3s.at[i, j], sem_g3r.at[i, j], partner,
        )

    def local_out(i, j):
        return pltpu.make_async_copy(
            fin.at[i, j, pl.ds(pl.multiple_of(zl * bq, bq), bq)],
            outs[j].at[:, head_cols(half, i)], sem_out.at[i, j],
        )

    def row_on(r):
        return (h + r - 1 >= 0) & (h + r - 1 < rows_all)

    side_on = (has_left, has_right)
    vert_on = (has_up, has_down)

    def wait_r1(i):
        for j in range(4):
            local_in(i, j).wait()
            r1(i, j).wait_recv()

    def start_r2(i):
        for d in range(2):
            pl.when(vert_on[d])(lambda d=d: r2(i, d).start())

    def wait_r2(i):
        for d in range(2):
            pl.when(vert_on[1 - d])(lambda d=d: r2(i, d).wait_recv())

    def for_sides(i, rows, act, flip):
        for r in rows:
            for d in range(2):
                on = side_on[1 - d] if flip else side_on[d]
                if r != 1:
                    on = on & row_on(r)
                pl.when(on)(lambda r=r, d=d: act(i, r, d))

    def start_r3(i, rows):
        for_sides(i, rows, lambda i, r, d: r3(i, r, d).start(), False)

    def wait_r3(i):
        for_sides(i, (0, 1, 2), lambda i, r, d: r3(i, r, d).wait_recv(), True)

    first = (x == 0) & (h == 0)
    half_rows = part.shape[1] // 2
    quarter = half_rows // ny
    piece = quarter // nx
    z_at = zh * half_rows
    y_at = z_at + y * quarter
    x_at = y_at + x * piece
    round_y = [(j, y_peers[j], (y + j + 1) % ny) for j in range(ny - 1)]
    round_x = [(j, x_peers[j], (x + j + 1) % nx) for j in range(nx - 1)]
    n_y, n_x = ny - 1, nx - 1

    def rows8(at, n):
        return pl.ds(pl.multiple_of(at, 8), n)

    def ar(n, src, dst, k, dev):
        return remote(src, dst, sem_ars.at[n, k], sem_arr.at[n, k], dev)

    def ar_copies(n, step):
        if step == 0:
            return [ar(n, part.at[n, rows8((1 - zh) * half_rows, half_rows)], from_z.at[n], 0, z_peer)]
        if step == 1:
            return [
                ar(n, part.at[n, rows8(z_at + to * quarter, quarter)], from_y.at[n, j], 1 + j, dev)
                for j, dev, to in round_y
            ]
        if step == 2:
            return [
                ar(n, part.at[n, rows8(y_at + to * piece, piece)], from_x.at[n, j], 1 + n_y + j, dev)
                for j, dev, to in round_x
            ]
        if step == 3:
            mine = whole.at[n, rows8(x_at, piece)]
            return [ar(n, mine, mine, 1 + n_y + n_x + j, dev) for j, dev, _ in round_x]
        if step == 4:
            mine = whole.at[n, rows8(y_at, quarter)]
            return [ar(n, mine, mine, 1 + n_y + 2 * n_x + j, dev) for j, dev, _ in round_y]
        mine = whole.at[n, rows8(z_at, half_rows)]
        return [ar(n, mine, mine, 1 + 2 * n_y + 2 * n_x, z_peer)]

    def ar_step(n, step):
        if step > 0:
            for copy in ar_copies(n, step - 1):
                copy.wait_recv()
        if step == 1:
            part[n, rows8(z_at, half_rows)] += from_z[n]
        if step == 2:
            at = rows8(y_at, quarter)
            total = part[n, at]
            for j in range(n_y):
                total = total + from_y[n, j]
            part[n, at] = total
        if step == 3:
            at = rows8(x_at, piece)
            total = part[n, at]
            for j in range(n_x):
                total = total + from_x[n, j]
            whole[n, at] = total
        if step < 6:
            for copy in ar_copies(n, step):
                copy.start()

    def st_copies(step):
        if step == 0:
            peers, base = [z_peer], 0
        elif step == 1:
            peers, base = y_peers, 1
        else:
            peers, base = x_peers, 1 + n_y
        return [
            remote(st.at[step], st_in.at[base + j], sem_sts.at[base + j], sem_str.at[base + j], dev)
            for j, dev in enumerate(peers)
        ], base

    def st_start(step):
        for copy in st_copies(step)[0]:
            copy.start()

    def st_merge(step):
        copies, base = st_copies(step)
        for copy in copies:
            copy.wait_recv()
        own = st[step]
        peak = own[0:nh]
        for j in range(len(copies)):
            peak = jnp.maximum(peak, st_in[base + j][0:nh])
        total = own[nh : 2 * nh] * jnp.exp2(own[0:nh] - peak)
        for j in range(len(copies)):
            got = st_in[base + j]
            total = total + got[nh : 2 * nh] * jnp.exp2(got[0:nh] - peak)
        st[step + 1, 0:nh] = peak
        st[step + 1, nh : 2 * nh] = total

    def text_scores(i):
        keys = kv[i, 0, 1, 1:3].reshape(both, HD)
        return mm_nt(keys, tq_ref[:, head_cols(half, i)]) * c2

    def words_scores(i):
        cols = head_cols(half, i)
        s = mm_nt(tk_ref[:, cols], tq_ref[:, cols]) * c2
        return jnp.where(tm_ref[:, 0:1] > 0.5, s, NEG)

    def text_stats(i):
        s = text_scores(i)
        peak = jnp.max(s, 0, keepdims=True)
        st[0, pl.ds(i, 1)] = peak
        st[0, pl.ds(nh + i, 1)] = jnp.sum(jnp.exp2(s - peak), 0, keepdims=True)

        @pl.when(first)
        def _():
            s2 = words_scores(i)
            old = st[0, pl.ds(i, 1)]
            new = jnp.maximum(old, jnp.max(s2, 0, keepdims=True))
            st[0, pl.ds(i, 1)] = new
            st[0, pl.ds(nh + i, 1)] = st[0, pl.ds(nh + i, 1)] * jnp.exp2(old - new) + jnp.sum(
                jnp.exp2(s2 - new), 0, keepdims=True
            )

    def put_t(n, i, value):
        for a in range(lanes):
            part[n, rows8(i * words_n + a * HD, HD)] = value[:, a * HD : (a + 1) * HD]

    def add_t(n, i, value):
        for a in range(lanes):
            part[n, rows8(i * words_n + a * HD, HD)] += value[:, a * HD : (a + 1) * HD]

    def get_t(n, i):
        return jnp.concatenate(
            [whole[n, rows8(i * words_n + a * HD, HD)] for a in range(lanes)], axis=1
        )

    def text_forward(i):
        row = lse[pl.ds(i, 1)]
        w = jnp.exp2(text_scores(i) - row).astype(BF16)
        put_t(0, i, mm_tn(kv[i, 1, 1, 1:3].reshape(both, HD), w))

        @pl.when(first)
        def _():
            w2 = jnp.exp2(words_scores(i) - row).astype(BF16)
            add_t(0, i, mm_tn(tv_ref[:, head_cols(half, i)], w2))

    def td_at(i, a):
        at = 2 * i + a
        return (2 + at // nh, rows8((at % nh) * words_n, words_n))

    def text_backward(i):
        cols = head_cols(half, i)
        row = lse[pl.ds(i, 1)]
        q = tq_ref[:, cols]
        g = tg_ref[:, cols]
        o_round = get_t(0, i).astype(BF16).astype(F32)
        t_fin[0, i] = o_round.T.astype(BF16)
        delta = jnp.sum(o_round * g.astype(F32).T, 0, keepdims=True)

        def one(s, k, v):
            p = jnp.exp2(s - row)
            ds = (p * (mm_nt(v, g) - delta)).astype(BF16)
            return mm_tn(k, ds), mm_nn(ds, q) * scale, mm_nn(p.astype(BF16), g)

        a_q, a_k, a_v = one(
            text_scores(i), kv[i, 0, 1, 1:3].reshape(both, HD), kv[i, 1, 1, 1:3].reshape(both, HD)
        )
        put_t(1, i, a_q)
        t_kv[i, 0] = a_k
        t_kv[i, 1] = a_v

        @pl.when(first)
        def _():
            b_q, b_k, b_v = one(words_scores(i), tk_ref[:, cols], tv_ref[:, cols])
            add_t(1, i, b_q)
            n, at = td_at(i, 0)
            part[n, at] += b_k
            n, at = td_at(i, 1)
            part[n, at] += b_v

    t_outs = (tout_ref, tdq_ref, tdk_ref, tdv_ref)

    def t_out(j, i):
        return remote(
            t_fin.at[j, i], t_outs[j].at[:, head_cols(half, i)],
            sem_tfs.at[j, i], sem_tfr.at[j, i], partner,
        )

    def t_loc(j, i):
        return pltpu.make_async_copy(
            t_fin.at[j, i], t_outs[j].at[:, head_cols(half, i)], sem_tfl.at[j, i]
        )

    def send_text(j, i):
        t_out(j, i).start()
        t_loc(j, i).start()

    def finish_td(i, a):
        n, at = td_at(i, a)
        t_fin[2 + a, i] = whole[n, at].astype(BF16)
        send_text(2 + a, i)

    @pl.loop(0, nh)
    def _(i):
        for j in range(4):
            r1(i, j).start()
            local_in(i, j).start()

    mask_out.start()
    mask_own.start()

    @pl.loop(0, nh)
    def _(i):
        @pl.when(jnp.logical_not(has_right))
        def _():
            g1r[i, 0] = jnp.zeros(g1r.shape[2:], BF16)

        @pl.when(jnp.logical_not(has_left))
        def _():
            g1r[i, 1] = jnp.zeros(g1r.shape[2:], BF16)

        @pl.when(jnp.logical_not(has_down))
        def _():
            g2r[i, 0] = jnp.zeros(g2r.shape[2:], BF16)

        @pl.when(jnp.logical_not(has_up))
        def _():
            g2r[i, 1] = jnp.zeros(g2r.shape[2:], BF16)

    mask_own.wait()
    mask_out.wait_recv()
    part[2] = jnp.zeros(part.shape[1:], F32)
    part[3] = jnp.zeros(part.shape[1:], F32)
    st[0] = jnp.zeros(st.shape[1:], F32)
    wait_r1(0)
    start_r2(0)
    start_r3(0, (1,))
    text_stats(0)

    def online(s, v, save, qs, keep):
        m_old = m_run[0:1, qs]
        m_new = jnp.maximum(m_old, jnp.max(s, 0, keepdims=True))
        alpha = jnp.exp2(m_old - m_new)
        e = jnp.exp2(s - m_new)
        l_run[0:1, qs] = l_run[0:1, qs] * alpha + jnp.sum(e, 0, keepdims=True)
        m_run[0:1, qs] = m_new
        m_saved[pl.ds(save, 1), qs] = m_new
        w = e.astype(BF16)
        keep(w)
        o_t[:, qs] = o_t[:, qs] * alpha + mm_tn(v, w)

    def fwd(i, row, col, qs, keep):
        s = mm_nt(kv[i, 0, row, col], qg[i, 0, qs]) * c2
        at = (col * 3 + row) * 2
        first = mask[pl.ds(at, 1), qs]
        last = mask[pl.ds(at + 1, 1), qs]
        s = jnp.concatenate(
            [
                jnp.where(first > 0.5, s[:tile], NEG),
                s[tile : 3 * tile],
                jnp.where(last > 0.5, s[3 * tile :], NEG),
            ],
            axis=0,
        )
        online(s, kv[i, 1, row, col], col * 3 + row, qs, keep)

    def fwd_mid(i, row, col):
        def keep(w):
            p_mid[row, col - 1] = w

        fwd(i, row, col, pl.ds(0, both), keep)

    def fwd_side(i, row, d):
        def keep(w):
            p_side[row, d] = w

        fwd(i, row, 3 * d, pl.ds(d * bq, bq), keep)

    def back(w0, k, v, q, g, save, qs):
        f = jnp.exp2(m_saved[pl.ds(save, 1), qs] - m_run[0:1, qs]) * l_run[0:1, qs]
        dp = mm_nt(v, g)
        w = w0.astype(F32) * f
        ds = (w * (dp - d_row[0:1, qs])).astype(BF16)
        d_k = mm_nn(ds, q) * scale
        d_v = mm_nn(w.astype(BF16), g)
        dq_t[:, qs] += mm_tn(k, ds)
        return d_k, d_v

    def bwd(i, row, col, qs, w0):
        d_k, d_v = back(
            w0, kv[i, 0, row, col], kv[i, 1, row, col], qg[i, 0, qs], qg[i, 1, qs],
            col * 3 + row, qs,
        )
        share[i, 0, row, col] = d_k.astype(BF16)
        share[i, 1, row, col] = d_v.astype(BF16)

    def add_g1(i):
        for_sides(i, (0, 1, 2), lambda i, r, d: g1(i, r, d).wait_recv(), True)
        for r in (0, 2):
            @pl.when(row_on(r))
            def _(r=r):
                for a in range(2):
                    for d in range(2):
                        col = 2 - d
                        share[i, a, r, col] = (
                            share[i, a, r, col].astype(F32) + g1r[i, d, a, r].astype(F32)
                        ).astype(BF16)
        for d in range(2):
            pl.when(vert_on[d])(lambda d=d: g2(i, d).start())

    def add_g2(i):
        for d in range(2):
            pl.when(vert_on[1 - d])(lambda d=d: g2(i, d).wait_recv())
        for a in range(2):
            for s in range(2):
                total = (
                    share[i, a, 1, 1 + s].astype(F32)
                    + g1r[i, 1 - s, a, 1].astype(F32)
                    + g2r[i, 0, a, s].astype(F32)
                    + g2r[i, 1, a, s].astype(F32)
                    + t_kv[i, a, s * bq : (s + 1) * bq]
                )
                fin[i, 2 + a, s * bq : (s + 1) * bq] = total.astype(BF16)
        for j in (2, 3):
            g3(i, j).start()
            local_out(i, j).start()

    @pl.loop(0, nh)
    def _(i):
        m_run[0:1, :] = jnp.full((1, both), NEG, F32)
        l_run[0:1, :] = jnp.zeros((1, both), F32)
        o_t[...] = jnp.zeros(o_t.shape, F32)
        dq_t[...] = jnp.zeros(dq_t.shape, F32)

        @pl.when(i == 1)
        def _():
            @pl.loop(0, nh)
            def _(j):
                text_backward(j)
                send_text(0, j)

            ar_step(1, 0)

        @pl.loop(1, 3)
        def _(col):
            fwd_mid(i, 1, col)

        @pl.when(i == 1)
        def _():
            ar_step(1, 1)

        @pl.when(i == 0)
        def _():
            wait_r1(1)
            start_r2(1)
            start_r3(1, (1,))
            text_stats(1)
            wait_r2(0)
            start_r3(0, (0, 2))

        @pl.loop(0, 4)
        def _(n):
            row = (n // 2) * 2

            @pl.when(row_on(row))
            def _():
                fwd_mid(i, row, 1 + n % 2)

        @pl.when(i == 0)
        def _():
            wait_r1(2)
            start_r2(2)
            start_r3(2, (1,))
            text_stats(2)
            st_start(0)

        @pl.when(i == 1)
        def _():
            ar_step(1, 2)

        @pl.when(i < nh - 1)
        def _():
            wait_r2(i + 1)
            start_r3(i + 1, (0, 2))

        words = head_cols(half, i)
        s_text = jnp.where(
            tm_ref[:, 0:1] > 0.5, mm_nt(tk_ref[:, words], qg[i, 0]) * c2, NEG
        )

        def keep_text(w):
            p_text[...] = w

        online(s_text, tv_ref[:, words], 12, pl.ds(0, both), keep_text)

        @pl.when(i > 0)
        def _():
            add_g1(i - 1)

        @pl.when(i == 0)
        def _():
            st_merge(0)
            st_start(1)

        @pl.when(i == 1)
        def _():
            ar_step(1, 3)

        wait_r3(i)
        for d in range(2):
            @pl.when(side_on[d])
            def _(d=d):
                @pl.loop(0, 3)
                def _(row):
                    @pl.when(row_on(row))
                    def _():
                        fwd_side(i, row, d)

            @pl.when(i == 0)
            def _(d=d):
                st_merge(d + 1)
                if d == 0:
                    st_start(2)

            @pl.when(i == 1)
            def _(d=d):
                ar_step(1, 4 + d)

        @pl.when(i == 0)
        def _():
            lse[0:nh] = st[3, 0:nh] + jnp.log2(st[3, nh : 2 * nh])

            @pl.loop(0, nh)
            def _(j):
                text_forward(j)

        @pl.when(i == 1)
        def _():
            ar_step(1, 6)

            @pl.loop(0, nh)
            def _(j):
                t_fin[1, j] = (get_t(1, j) * scale).T.astype(BF16)
                send_text(1, j)

        inv = 1.0 / l_run[0:1, :]
        l_run[0:1, :] = inv
        o_round = (o_t[...] * inv).astype(BF16).astype(F32)
        fin[i, 0] = o_round.T.astype(BF16)
        g_t = qg[i, 1].astype(F32).T
        d_row[0:1, :] = jnp.sum(o_round * g_t, 0, keepdims=True)
        g3(i, 0).start()
        local_out(i, 0).start()

        d_k, d_v = back(
            p_text[...], tk_ref[:, words], tv_ref[:, words], qg[i, 0], qg[i, 1],
            12, pl.ds(0, both),
        )
        n, at = td_at(i, 0)
        part[n, at] += d_k
        n, at = td_at(i, 1)
        part[n, at] += d_v
        turn = jnp.where(i == 0, 0, i + 1)
        ar_step(turn, 0)

        for d in range(2):
            @pl.when(side_on[d])
            def _(d=d):
                @pl.loop(0, 3)
                def _(row):
                    @pl.when(row_on(row))
                    def _():
                        bwd(i, row, 3 * d, pl.ds(d * bq, bq), p_side[row, d])
                        g1(i, row, d).start()

            ar_step(turn, 1 + d)

        @pl.when(i > 0)
        def _():
            add_g2(i - 1)

        for stage, row in enumerate((0, 2, 1)):
            @pl.when(row_on(row))
            def _(row=row):
                @pl.loop(1, 3)
                def _(col):
                    bwd(i, row, col, pl.ds(0, both), p_mid[row, col - 1])

            ar_step(turn, 3 + stage)

        fin[i, 1] = (dq_t[...] * scale).T.astype(BF16)
        g3(i, 1).start()
        local_out(i, 1).start()

        @pl.when(i < nh - 1)
        def _():
            ar_step(turn, 6)

    add_g1(nh - 1)
    for at in range(nh):
        finish_td(at // 2, at % 2)
    ar_step(3, 6)
    for at in range(nh, 2 * nh):
        finish_td(at // 2, at % 2)
    add_g2(nh - 1)

    for step in range(3):
        for copy in st_copies(step)[0]:
            copy.wait_send()

    @pl.loop(0, 4)
    def _(n):
        for step in range(6):
            for copy in ar_copies(n, step):
                copy.wait_send()

    for n in range(4):
        for j in range(nh):
            t_out(n, j).wait_send()
            t_out(n, j).wait_recv()
            t_loc(n, j).wait()

    mask_out.wait_send()

    @pl.loop(0, nh)
    def _(i):
        for j in range(4):
            r1(i, j).wait_send()
            g3(i, j).wait_send()
            g3(i, j).wait_recv()
            local_out(i, j).wait()
        for d in range(2):
            @pl.when(vert_on[d])
            def _(d=d):
                r2(i, d).wait_send()
                g2(i, d).wait_send()
        for_sides(i, (0, 1, 2), lambda i, r, d: r3(i, r, d).wait_send(), False)
        for_sides(i, (0, 1, 2), lambda i, r, d: g1(i, r, d).wait_send(), False)


def window_pass(
    query, key, value, grad, mask, text_query, text_key, text_value, text_grad, text_mask
):
    nx = lax.axis_size("tm") // 2
    ny = lax.axis_size("height") // 2
    bq, channels = query.shape
    nh = channels // HD // 2
    words = text_key.shape[0]
    both = 2 * bq
    rows = nh * words
    sds = jax.ShapeDtypeStruct
    hbm = pl.BlockSpec(memory_space=pl.ANY)
    vmem = pl.BlockSpec(memory_space=pltpu.VMEM)
    dma = pltpu.SemaphoreType.DMA
    return pl.pallas_call(
        functools.partial(window_kernel, nx, ny),
        out_shape=[sds((bq, channels), BF16)] * 4 + [sds((words, channels), BF16)] * 4,
        in_specs=[hbm] * 4 + [vmem] * 6,
        out_specs=[hbm] * 8,
        scratch_shapes=[
            pltpu.VMEM((nh, 2, 3, 4, bq, HD), BF16),
            pltpu.VMEM((nh, 2, both, HD), BF16),
            pltpu.VMEM((24, both), F32),
            pltpu.VMEM((3, 2, bq, both), BF16),
            pltpu.VMEM((3, 2, bq, bq), BF16),
            pltpu.VMEM((words, both), BF16),
            pltpu.VMEM((16, both), F32),
            pltpu.VMEM((8, both), F32),
            pltpu.VMEM((8, both), F32),
            pltpu.VMEM((8, both), F32),
            pltpu.VMEM((HD, both), F32),
            pltpu.VMEM((HD, both), F32),
            pltpu.VMEM((nh, 2, 3, 4, bq, HD), BF16),
            pltpu.VMEM((nh, 2, 2, 3, bq, HD), BF16),
            pltpu.VMEM((nh, 2, 2, 2, bq, HD), BF16),
            pltpu.VMEM((nh, 4, both, HD), BF16),
            pltpu.VMEM((4, 8, words), F32),
            pltpu.VMEM((nx + ny - 1, 8, words), F32),
            pltpu.VMEM((8, words), F32),
            pltpu.VMEM((4, rows, HD), F32),
            pltpu.VMEM((4, rows // 2, HD), F32),
            pltpu.VMEM((4, ny - 1, rows // 2 // ny, HD), F32),
            pltpu.VMEM((4, nx - 1, rows // 2 // ny // nx, HD), F32),
            pltpu.VMEM((4, rows, HD), F32),
            pltpu.VMEM((nh, 2, both, HD), F32),
            pltpu.VMEM((4, nh, words, HD), BF16),
            dma((nh, 4)),
            dma((nh, 4)),
            dma((nh, 4)),
            dma((3,)),
            dma((nh, 2)),
            dma((nh, 2)),
            dma((nh, 3, 2)),
            dma((nh, 3, 2)),
            dma((nh, 3, 2)),
            dma((nh, 3, 2)),
            dma((nh, 2)),
            dma((nh, 2)),
            dma((nh, 4)),
            dma((nh, 4)),
            dma((nh, 4)),
            dma((nx + ny - 1,)),
            dma((nx + ny - 1,)),
            dma((4, 2 * (nx + ny - 1))),
            dma((4, 2 * (nx + ny - 1))),
            dma((4, nh)),
            dma((4, nh)),
            dma((4, nh)),
        ],
        compiler_params=pltpu.CompilerParams(
            collective_id=0, has_side_effects=True, vmem_limit_bytes=62 * 2**20
        ),
        name="window",
    )(query, key, value, grad, mask, text_query, text_key, text_value, text_grad, text_mask)


def edge_mask(tile_lists, tile, slot):
    lists = tile_lists.reshape(4, 3, 3, 3)
    rows = []
    for col in (0, 3):
        on = jnp.any((lists >= 0) & (lists % 4 == col), axis=-1)
        rows.append(on)
    on = jnp.stack(rows, -1)
    on = jnp.transpose(on, (1, 2, 3, 0)).reshape(18, 4).astype(F32)
    on = jnp.repeat(on, tile, axis=1)
    pad = jnp.zeros((6, on.shape[1]), F32)
    return jnp.where(
        slot == 0, jnp.concatenate([on, pad]), jnp.concatenate([pad, on])
    )


def body(
    query_latent,
    key_latent,
    value_latent,
    grad_latent,
    tile_lists,
    text_query,
    text_key,
    text_value,
    grad_text,
    text_mask,
):
    frames, rows, width_tiles, tile, channels = query_latent.shape
    flat = [
        a.reshape(width_tiles * tile, channels)
        for a in (query_latent, key_latent, value_latent, grad_latent)
    ]
    mask = edge_mask(tile_lists, tile, lax.axis_index("tm") % 2)
    text_on = jnp.broadcast_to(
        (text_mask > 0).astype(F32)[:, None], (text_mask.shape[0], HD)
    )
    outs = window_pass(*flat, mask, text_query, text_key, text_value, grad_text, text_on)
    return tuple(a.reshape(query_latent.shape) for a in outs[:4]) + tuple(outs[4:])


def solution(mesh):
    latent = P("tm", "height", None, None, "heads")
    text = P(None, "heads")
    in_specs = (latent,) * 4 + (P("tm", "height", None, None),) + (text,) * 4 + (P(),)
    out_specs = (latent,) * 4 + (text,) * 4
    return jax.shard_map(body, mesh=mesh, in_specs=in_specs, out_specs=out_specs, check_vma=False)
```

```python
import functools
import math

import jax
import jax.numpy as jnp
from jax import lax
from jax.experimental import pallas as pl
from jax.experimental.pallas import tpu as pltpu
from jax.sharding import PartitionSpec as P

HD = 128
NEG = -1e30
F32 = jnp.float32
BF16 = jnp.bfloat16
MESH = pl.DeviceIdType.MESH


def mm_nt(a, b):
    return lax.dot_general(a, b, (((1,), (1,)), ((), ())), preferred_element_type=F32)


def mm_tn(a, b):
    return lax.dot_general(a, b, (((0,), (0,)), ((), ())), preferred_element_type=F32)


def mm_nn(a, b):
    return jnp.dot(a, b, preferred_element_type=F32)


def window_kernel(
    nx,
    ny,
    q_ref,
    k_ref,
    v_ref,
    g_ref,
    mask_ref,
    tq_ref,
    tk_ref,
    tv_ref,
    tg_ref,
    tm_ref,
    out_ref,
    dq_ref,
    dk_ref,
    dv_ref,
    tout_ref,
    tdq_ref,
    tdk_ref,
    tdv_ref,
    kv,
    qg,
    mask,
    p_mid,
    p_side,
    p_text,
    m_saved,
    m_run,
    l_run,
    d_row,
    o_t,
    dq_t,
    share,
    g1r,
    g2r,
    fin,
    st,
    lse,
    part0,
    gh0,
    gx0,
    whole0,
    part,
    gh,
    gx,
    gx2,
    gh2,
    whole,
    t_kv,
    t_fin,
    sem_loc,
    sem_r1s,
    sem_r1r,
    sem_mask,
    sem_r2s,
    sem_r2r,
    sem_r3s,
    sem_r3r,
    sem_g1s,
    sem_g1r,
    sem_g2s,
    sem_g2r,
    sem_g3s,
    sem_g3r,
    sem_out,
    sem_txs,
    sem_txr,
    sem_tfs,
    sem_tfr,
    sem_tfl,
):
    bq = q_ref.shape[0]
    tile = bq // 4
    heads = q_ref.shape[1] // HD
    nh = heads // 2
    both = 2 * bq
    scale = 1.0 / math.sqrt(HD)
    c2 = scale * math.log2(math.e)

    t = lax.axis_index("tm")
    h = lax.axis_index("height")
    c = lax.axis_index("heads")
    x = t // 2
    zl = t % 2
    zh = h // ny
    half = (zl + zh) % 2
    other = 1 - half
    rows_all = 2 * ny

    def at_grid(xx, hh):
        return (2 * xx + (half + hh // ny) % 2, hh, c)

    partner = (2 * x + 1 - zl, h, c)
    left = (t - 2, h, c)
    right = (t + 2, h, c)
    up = at_grid(x, h - 1)
    down = at_grid(x, h + 1)
    has_left = x > 0
    has_right = x < nx - 1
    has_up = h > 0
    has_down = h < rows_all - 1

    words_n = tq_ref.shape[0]
    h_peers = [(j, (h + j + 1) % rows_all) for j in range(rows_all - 1)]
    x_peers = [(j, (x + j + 1) % nx) for j in range(nx - 1)]

    barrier = pltpu.get_barrier_semaphore()
    pl.semaphore_signal(barrier, inc=1, device_id=partner, device_id_type=MESH)
    for _, to in h_peers:
        pl.semaphore_signal(barrier, inc=1, device_id=at_grid(x, to), device_id_type=MESH)
    for _, to in x_peers:
        pl.semaphore_signal(barrier, inc=1, device_id=at_grid(to, h), device_id_type=MESH)
    pl.semaphore_wait(barrier, nx + rows_all - 1)

    def remote(src, dst, ssem, rsem, dev):
        return pltpu.make_async_remote_copy(
            src_ref=src, dst_ref=dst, send_sem=ssem, recv_sem=rsem,
            device_id=dev, device_id_type=MESH,
        )

    def head_cols(which, i):
        return pl.ds(pl.multiple_of((which * nh + i) * HD, HD), HD)

    ins = (q_ref, k_ref, v_ref, g_ref)
    outs = (out_ref, dq_ref, dk_ref, dv_ref)

    def landing(i, j):
        if j == 0:
            return qg.at[i, 0, pl.ds(pl.multiple_of(zl * bq, bq), bq)]
        if j == 3:
            return qg.at[i, 1, pl.ds(pl.multiple_of(zl * bq, bq), bq)]
        return kv.at[i, j - 1, 1, 1 + zl]

    def r1(i, j):
        return remote(
            ins[j].at[:, head_cols(other, i)], landing(i, j),
            sem_r1s.at[i, j], sem_r1r.at[i, j], partner,
        )

    def local_in(i, j):
        return pltpu.make_async_copy(
            ins[j].at[:, head_cols(half, i)], landing(i, j), sem_loc.at[i, j]
        )

    mask_cols = pl.ds(pl.multiple_of(zl * bq, bq), bq)
    mask_out = remote(mask_ref, mask.at[:, mask_cols], sem_mask.at[0], sem_mask.at[1], partner)
    mask_own = pltpu.make_async_copy(mask_ref, mask.at[:, mask_cols], sem_mask.at[2])

    def r2(i, d, s):
        return remote(
            kv.at[i, :, 1, 1 + s], kv.at[i, :, 2 - 2 * d, 1 + s],
            sem_r2s.at[i, d, s], sem_r2r.at[i, d, s], (up, down)[d],
        )

    def r3(i, r, d):
        return remote(
            kv.at[i, :, r, 1 + d], kv.at[i, :, r, 3 - 3 * d],
            sem_r3s.at[i, r, d], sem_r3r.at[i, r, d], (left, right)[d],
        )

    def g1(i, r, d):
        return remote(
            share.at[i, :, r, 3 * d], g1r.at[i, d, :, r],
            sem_g1s.at[i, r, d], sem_g1r.at[i, r, d], (left, right)[d],
        )

    def g2(i, d):
        return remote(
            share.at[i, :, 2 * d, pl.ds(1, 2)], g2r.at[i, d],
            sem_g2s.at[i, d], sem_g2r.at[i, d], (up, down)[d],
        )

    def g3(i, j):
        return remote(
            fin.at[i, j, pl.ds(pl.multiple_of((1 - zl) * bq, bq), bq)],
            outs[j].at[:, head_cols(half, i)],
            sem_g3s.at[i, j], sem_g3r.at[i, j], partner,
        )

    def local_out(i, j):
        return pltpu.make_async_copy(
            fin.at[i, j, pl.ds(pl.multiple_of(zl * bq, bq), bq)],
            outs[j].at[:, head_cols(half, i)], sem_out.at[i, j],
        )

    def row_on(r):
        return (h + r - 1 >= 0) & (h + r - 1 < rows_all)

    side_on = (has_left, has_right)
    vert_on = (has_up, has_down)

    def wait_in(i, which):
        for j in which:
            r1(i, j).wait_recv()

    def wait_local(i, which):
        for j in which:
            local_in(i, j).wait()

    def start_r2(i, s):
        for d in range(2):
            pl.when(vert_on[d])(lambda d=d: r2(i, d, s).start())

    def wait_r2(i):
        for d in range(2):
            @pl.when(vert_on[1 - d])
            def _(d=d):
                r2(i, d, 0).wait_recv()
                r2(i, d, 1).wait_recv()

    def start_own(i):
        wait_local(i, (1, 2))
        start_r2(i, zl)
        for d in range(2):
            pl.when((zl == d) & side_on[d])(lambda d=d: r3(i, 1, d).start())

    def start_traded(i):
        wait_in(i, (1, 2))
        start_r2(i, 1 - zl)
        for d in range(2):
            pl.when((zl != d) & side_on[d])(lambda d=d: r3(i, 1, d).start())

    def for_sides(i, rows, act, flip):
        for r in rows:
            for d in range(2):
                on = side_on[1 - d] if flip else side_on[d]
                if r != 1:
                    on = on & row_on(r)
                pl.when(on)(lambda r=r, d=d: act(i, r, d))

    def start_r3(i, rows):
        for_sides(i, rows, lambda i, r, d: r3(i, r, d).start(), False)

    def wait_r3(i):
        for_sides(i, (0, 1, 2), lambda i, r, d: r3(i, r, d).wait_recv(), True)

    first = (x == 0) & (h == 0)

    per = words_n // rows_all // nx

    class Round:
        def __init__(self, n, src, got_outer, got_inner, dst, lo, hi, h_outer):
            self.n, self.src, self.dst = n, src, dst
            self.got_outer, self.got_inner = got_outer, got_inner
            self.lo, self.hi, self.tiles = lo, hi, pl.ds(lo, hi - lo)
            self.h_outer = h_outer
            self.band = words_n // (rows_all if h_outer else nx)
            self.me = (h, x) if h_outer else (x, h)
            self.outer_peers = h_peers if h_outer else x_peers
            self.inner_peers = x_peers if h_outer else h_peers

        def device(self, o, i):
            return at_grid(i, o) if self.h_outer else at_grid(o, i)

        def rows(self, o):
            return pl.ds(pl.multiple_of(o * self.band, 8), self.band)

        def piece(self, o, i):
            return pl.ds(pl.multiple_of(o * self.band + i * per, 8), per)

        def own_rows(self):
            return self.rows(self.me[0])

        def own_piece(self):
            return self.piece(*self.me)

        def copies(self, stage):
            o, i = self.me
            if stage == 0:
                pairs = [
                    (self.src.at[self.tiles, self.rows(to)], self.got_outer.at[j], (to, i))
                    for j, to in self.outer_peers
                ]
            elif stage == 1:
                pairs = [
                    (self.src.at[self.tiles, self.piece(o, to)], self.got_inner.at[j], (o, to))
                    for j, to in self.inner_peers
                ]
            elif stage == 2:
                own = self.dst.at[self.tiles, self.own_piece()]
                pairs = [(own, own, (o, to)) for j, to in self.inner_peers]
            else:
                own = self.dst.at[self.tiles, self.own_rows()]
                pairs = [(own, own, (to, i)) for j, to in self.outer_peers]
            return [
                remote(
                    a, b, sem_txs.at[self.n, stage, j], sem_txr.at[self.n, stage, j],
                    self.device(*to),
                )
                for j, (a, b, to) in enumerate(pairs)
            ]

        def send(self, stage):
            for copy in self.copies(stage):
                copy.start()

        def got(self, stage):
            for copy in self.copies(stage):
                copy.wait_recv()

        def sent(self):
            for stage in range(4):
                for copy in self.copies(stage):
                    copy.wait_send()

    round0 = Round(0, part0, gh0, gx0, whole0, 0, nh + 2, True)
    round1 = Round(1, part, gh, gx, whole, 0, 3 * nh - 2, True)
    round2 = Round(2, part, gx2, gh2, whole, 3 * nh - 2, 3 * nh, False)

    def merged(own, parts):
        peak = own(nh)
        for p in parts:
            peak = jnp.maximum(peak, p[nh])
        f = jnp.exp2(own(nh) - peak)
        total = own(nh + 1) * f
        values = [own(i) * f[:, i : i + 1] for i in range(nh)]
        for p in parts:
            f = jnp.exp2(p[nh] - peak)
            total = total + p[nh + 1] * f
            values = [v + p[i] * f[:, i : i + 1] for i, v in enumerate(values)]
        return values, peak, total

    def merge0_outer():
        round0.got(0)
        at = round0.own_rows()
        values, peak, total = merged(
            lambda a: part0[a, at], [gh0.at[j] for j, _ in h_peers]
        )
        for i in range(nh):
            part0[i, at] = values[i]
        part0[nh, at] = peak
        part0[nh + 1, at] = total
        round0.send(1)

    def merge0_inner():
        round0.got(1)
        at = round0.own_piece()
        values, peak, total = merged(
            lambda a: part0[a, at], [gx0.at[j] for j, _ in x_peers]
        )
        for i in range(nh):
            value = values[i] / total[:, i : i + 1]
            whole0[i, at] = value.astype(BF16).astype(F32)
        whole0[nh, at] = peak + jnp.log2(total)
        whole0[nh + 1, at] = total
        round0.send(2)

    def merge_outer(rnd):
        rnd.got(0)
        at = rnd.own_rows()
        for a in range(rnd.lo, rnd.hi):
            total = part[a, at]
            for j, _ in rnd.outer_peers:
                total = total + rnd.got_outer[j, a - rnd.lo]
            part[a, at] = total
        rnd.send(1)

    def merge_inner(rnd):
        rnd.got(1)
        at = rnd.own_piece()
        for a in range(rnd.lo, rnd.hi):
            total = part[a, at]
            for j, _ in rnd.inner_peers:
                total = total + rnd.got_inner[j, a - rnd.lo]
            whole[a, at] = total
        rnd.send(2)

    def spread(rnd):
        rnd.got(2)
        rnd.send(3)

    def text_scores(i):
        keys = kv[i, 0, 1, 1:3].reshape(both, HD)
        return mm_nt(keys, tq_ref[:, head_cols(half, i)]) * c2

    def words_scores(i):
        cols = head_cols(half, i)
        s = mm_nt(tk_ref[:, cols], tq_ref[:, cols]) * c2
        return jnp.where(tm_ref[:, 0:1] > 0.5, s, NEG)

    def text_partial(i):
        def one(s, v, old):
            peak = jnp.max(s, 0, keepdims=True)
            if old is not None:
                peak = jnp.maximum(peak, old[0])
            e = jnp.exp2(s - peak)
            total = jnp.sum(e, 0, keepdims=True)
            value = mm_tn(v, e.astype(BF16))
            if old is not None:
                f = jnp.exp2(old[0] - peak)
                total = total + old[1] * f
                value = value + old[2].T * f
            st[0, pl.ds(i, 1)] = peak
            st[1, pl.ds(i, 1)] = total
            part0[i] = value.T

        one(text_scores(i), kv[i, 1, 1, 1:3].reshape(both, HD), None)

        @pl.when(first)
        def _():
            old = (st[0, pl.ds(i, 1)], st[1, pl.ds(i, 1)], part0[i])
            one(words_scores(i), tv_ref[:, head_cols(half, i)], old)

    def text_start():
        part0[nh] = st[0].T
        part0[nh + 1] = st[1].T
        round0.send(0)

    def text_backward(i):
        cols = head_cols(half, i)
        row = lse[pl.ds(i, 1)]
        q = tq_ref[:, cols]
        g = tg_ref[:, cols]
        o_round = whole0[i]
        t_fin[0, i] = o_round.astype(BF16)
        delta = jnp.sum((o_round * g.astype(F32)).T, 0, keepdims=True)

        def one(s, k, v):
            p = jnp.exp2(s - row)
            ds = (p * (mm_nt(v, g) - delta)).astype(BF16)
            return (
                (mm_tn(k, ds) * scale).T,
                mm_nn(ds, q) * scale,
                mm_nn(p.astype(BF16), g),
            )

        a_q, a_k, a_v = one(
            text_scores(i), kv[i, 0, 1, 1:3].reshape(both, HD), kv[i, 1, 1, 1:3].reshape(both, HD)
        )
        part[i] = a_q
        t_kv[i, 0] = a_k
        t_kv[i, 1] = a_v

        @pl.when(first)
        def _():
            b_q, b_k, b_v = one(words_scores(i), tk_ref[:, cols], tv_ref[:, cols])
            part[i] += b_q
            part[nh + 2 * i] += b_k
            part[nh + 2 * i + 1] += b_v

    t_outs = (tout_ref, tdq_ref, tdk_ref, tdv_ref)

    def t_out(j, i):
        return remote(
            t_fin.at[j, i], t_outs[j].at[:, head_cols(half, i)],
            sem_tfs.at[j, i], sem_tfr.at[j, i], partner,
        )

    def t_loc(j, i):
        return pltpu.make_async_copy(
            t_fin.at[j, i], t_outs[j].at[:, head_cols(half, i)], sem_tfl.at[j, i]
        )

    def send_text(j, i):
        t_out(j, i).start()
        t_loc(j, i).start()

    def finish_td(i):
        for a in range(2):
            t_fin[2 + a, i] = whole[nh + 2 * i + a].astype(BF16)
            send_text(2 + a, i)

    for i in range(nh):
        for j in (1, 2):
            local_in(i, j).start()
    for i, js in ((0, (1, 2)), (0, (0, 3)), (1, (1, 2)), (2, (1, 2)), (1, (0, 3)), (2, (0, 3))):
        for j in js:
            r1(i, j).start()
    for i in range(nh):
        for j in (0, 3):
            local_in(i, j).start()
    start_own(0)

    mask_out.start()
    mask_own.start()

    @pl.loop(0, nh)
    def _(i):
        @pl.when(jnp.logical_not(has_right))
        def _():
            g1r[i, 0] = jnp.zeros(g1r.shape[2:], BF16)

        @pl.when(jnp.logical_not(has_left))
        def _():
            g1r[i, 1] = jnp.zeros(g1r.shape[2:], BF16)

        @pl.when(jnp.logical_not(has_down))
        def _():
            g2r[i, 0] = jnp.zeros(g2r.shape[2:], BF16)

        @pl.when(jnp.logical_not(has_up))
        def _():
            g2r[i, 1] = jnp.zeros(g2r.shape[2:], BF16)

    @pl.loop(nh, 3 * nh)
    def _(a):
        part[a] = jnp.zeros(part.shape[1:], F32)

    st[...] = jnp.zeros(st.shape, F32)
    start_traded(0)
    text_partial(0)
    mask_own.wait()
    mask_out.wait_recv()

    def online(s, v, save, qs, keep):
        m_old = m_run[0:1, qs]
        m_new = jnp.maximum(m_old, jnp.max(s, 0, keepdims=True))
        alpha = jnp.exp2(m_old - m_new)
        e = jnp.exp2(s - m_new)
        l_run[0:1, qs] = l_run[0:1, qs] * alpha + jnp.sum(e, 0, keepdims=True)
        m_run[0:1, qs] = m_new
        m_saved[pl.ds(save, 1), qs] = m_new
        w = e.astype(BF16)
        keep(w)
        o_t[:, qs] = o_t[:, qs] * alpha + mm_tn(v, w)

    def fwd(i, row, col, qs, keep):
        s = mm_nt(kv[i, 0, row, col], qg[i, 0, qs]) * c2
        at = (col * 3 + row) * 2
        first = mask[pl.ds(at, 1), qs]
        last = mask[pl.ds(at + 1, 1), qs]
        s = jnp.concatenate(
            [
                jnp.where(first > 0.5, s[:tile], NEG),
                s[tile : 3 * tile],
                jnp.where(last > 0.5, s[3 * tile :], NEG),
            ],
            axis=0,
        )
        online(s, kv[i, 1, row, col], col * 3 + row, qs, keep)

    def fwd_mid(i, row, col):
        def keep(w):
            p_mid[row, col - 1] = w

        fwd(i, row, col, pl.ds(0, both), keep)

    def fwd_side(i, row, d):
        def keep(w):
            p_side[row, d] = w

        fwd(i, row, 3 * d, pl.ds(d * bq, bq), keep)

    def back(w0, k, v, q, g, save, qs):
        f = jnp.exp2(m_saved[pl.ds(save, 1), qs] - m_run[0:1, qs]) * l_run[0:1, qs]
        dp = mm_nt(v, g)
        w = w0.astype(F32) * f
        ds = (w * (dp - d_row[0:1, qs])).astype(BF16)
        d_k = mm_nn(ds, q) * scale
        d_v = mm_nn(w.astype(BF16), g)
        dq_t[:, qs] += mm_tn(k, ds)
        return d_k, d_v

    def bwd(i, row, col, qs, w0):
        d_k, d_v = back(
            w0, kv[i, 0, row, col], kv[i, 1, row, col], qg[i, 0, qs], qg[i, 1, qs],
            col * 3 + row, qs,
        )
        share[i, 0, row, col] = d_k.astype(BF16)
        share[i, 1, row, col] = d_v.astype(BF16)

    def add_g1(i):
        for_sides(i, (0, 2), lambda i, r, d: g1(i, r, d).wait_recv(), True)
        for r in (0, 2):
            @pl.when(row_on(r))
            def _(r=r):
                for a in range(2):
                    for d in range(2):
                        col = 2 - d
                        share[i, a, r, col] = (
                            share[i, a, r, col].astype(F32) + g1r[i, d, a, r].astype(F32)
                        ).astype(BF16)
        for d in range(2):
            pl.when(vert_on[d])(lambda d=d: g2(i, d).start())

    def add_g2(i):
        for_sides(i, (1,), lambda i, r, d: g1(i, r, d).wait_recv(), True)
        for d in range(2):
            pl.when(vert_on[1 - d])(lambda d=d: g2(i, d).wait_recv())
        for a in range(2):
            for s in range(2):
                total = (
                    share[i, a, 1, 1 + s].astype(F32)
                    + g1r[i, 1 - s, a, 1].astype(F32)
                    + g2r[i, 0, a, s].astype(F32)
                    + g2r[i, 1, a, s].astype(F32)
                    + t_kv[i, a, s * bq : (s + 1) * bq]
                )
                fin[i, 2 + a, s * bq : (s + 1) * bq] = total.astype(BF16)
        for j in (2, 3):
            g3(i, j).start()
            local_out(i, j).start()

    @pl.loop(0, nh)
    def _(i):
        m_run[0:1, :] = jnp.full((1, both), NEG, F32)
        l_run[0:1, :] = jnp.zeros((1, both), F32)
        o_t[...] = jnp.zeros(o_t.shape, F32)
        dq_t[...] = jnp.zeros(dq_t.shape, F32)

        wait_local(i, (0, 3))
        wait_in(i, (0, 3))

        @pl.loop(1, 3)
        def _(col):
            fwd_mid(i, 1, col)

        @pl.when(i == 0)
        def _():
            wait_r2(0)
            start_r3(0, (0, 2))
            start_own(1)
            start_traded(1)
            text_partial(1)

        @pl.when(i == 1)
        def _():
            merge0_inner()

        @pl.loop(0, 4)
        def _(n):
            row = (n // 2) * 2

            @pl.when(row_on(row))
            def _():
                fwd_mid(i, row, 1 + n % 2)

        @pl.when(i == 0)
        def _():
            start_own(2)
            start_traded(2)
            text_partial(2)
            text_start()
            wait_r2(1)
            start_r3(1, (0, 2))

        @pl.when(i == 2)
        def _():
            merge_inner(round1)

        words = head_cols(half, i)
        s_text = jnp.where(
            tm_ref[:, 0:1] > 0.5, mm_nt(tk_ref[:, words], qg[i, 0]) * c2, NEG
        )

        def keep_text(w):
            p_text[...] = w

        online(s_text, tv_ref[:, words], 12, pl.ds(0, both), keep_text)

        wait_r3(i)
        for d in range(2):
            @pl.when(side_on[d])
            def _(d=d):
                @pl.loop(0, 3)
                def _(row):
                    @pl.when(row_on(row))
                    def _():
                        fwd_side(i, row, d)

        @pl.when(i == 0)
        def _():
            wait_r2(2)
            start_r3(2, (0, 2))
            merge0_outer()

        @pl.when(i == 1)
        def _():
            spread(round0)

        @pl.when(i == 2)
        def _():
            spread(round1)

        inv = 1.0 / l_run[0:1, :]
        l_run[0:1, :] = inv
        o_round = (o_t[...] * inv).astype(BF16).astype(F32)
        fin[i, 0] = o_round.T.astype(BF16)
        g_t = qg[i, 1].astype(F32).T
        d_row[0:1, :] = jnp.sum(o_round * g_t, 0, keepdims=True)
        g3(i, 0).start()
        local_out(i, 0).start()

        d_k, d_v = back(
            p_text[...], tk_ref[:, words], tv_ref[:, words], qg[i, 0], qg[i, 1],
            12, pl.ds(0, both),
        )
        part[nh + 2 * i] += d_k
        part[nh + 2 * i + 1] += d_v

        @pl.when(i == 2)
        def _():
            round2.send(0)

        for d in range(2):
            @pl.when(side_on[d])
            def _(d=d):
                @pl.loop(0, 3)
                def _(n):
                    row = (2 * n) % 3

                    @pl.when(row_on(row))
                    def _():
                        bwd(i, row, 3 * d, pl.ds(d * bq, bq), p_side[row, d])
                        g1(i, row, d).start()

            @pl.when(i == 2)
            def _(d=d):
                (merge_outer, merge_inner)[d](round2)

        @pl.when(i == 1)
        def _():
            round0.got(3)
            lse[...] = whole0[nh].T[0:8]

            @pl.loop(0, nh)
            def _(j):
                text_backward(j)
                send_text(0, j)

            round1.send(0)

        @pl.when(i > 0)
        def _():
            add_g1(i - 1)

        @pl.when(i == 2)
        def _():
            spread(round2)

        for stage, row in enumerate((0, 2, 1)):
            @pl.when(row_on(row))
            def _(row=row):
                @pl.loop(1, 3)
                def _(col):
                    bwd(i, row, col, pl.ds(0, both), p_mid[row, col - 1])

        @pl.when(i == 1)
        def _():
            merge_outer(round1)

        @pl.when(i == 2)
        def _():
            round1.got(3)
            for j in range(nh):
                t_fin[1, j] = whole[j].astype(BF16)
                send_text(1, j)
            for j in range(nh - 1):
                finish_td(j)

        @pl.when(i > 0)
        def _():
            add_g2(i - 1)

        fin[i, 1] = (dq_t[...] * scale).T.astype(BF16)
        g3(i, 1).start()
        local_out(i, 1).start()

    add_g1(nh - 1)
    round2.got(3)
    finish_td(nh - 1)
    add_g2(nh - 1)

    for rnd in (round0, round1, round2):
        rnd.sent()

    for n in range(4):
        for j in range(nh):
            t_out(n, j).wait_send()
            t_out(n, j).wait_recv()
            t_loc(n, j).wait()

    mask_out.wait_send()

    @pl.loop(0, nh)
    def _(i):
        for j in range(4):
            r1(i, j).wait_send()
            g3(i, j).wait_send()
            g3(i, j).wait_recv()
            local_out(i, j).wait()
        for d in range(2):
            @pl.when(vert_on[d])
            def _(d=d):
                r2(i, d, 0).wait_send()
                r2(i, d, 1).wait_send()
                g2(i, d).wait_send()
        for_sides(i, (0, 1, 2), lambda i, r, d: r3(i, r, d).wait_send(), False)
        for_sides(i, (0, 1, 2), lambda i, r, d: g1(i, r, d).wait_send(), False)


def window_pass(
    query, key, value, grad, mask, text_query, text_key, text_value, text_grad, text_mask
):
    nx = lax.axis_size("tm") // 2
    ny = lax.axis_size("height") // 2
    bq, channels = query.shape
    nh = channels // HD // 2
    words = text_key.shape[0]
    both = 2 * bq
    sds = jax.ShapeDtypeStruct
    hbm = pl.BlockSpec(memory_space=pl.ANY)
    vmem = pl.BlockSpec(memory_space=pltpu.VMEM)
    dma = pltpu.SemaphoreType.DMA
    return pl.pallas_call(
        functools.partial(window_kernel, nx, ny),
        out_shape=[sds((bq, channels), BF16)] * 4 + [sds((words, channels), BF16)] * 4,
        in_specs=[hbm] * 4 + [vmem] * 6,
        out_specs=[hbm] * 8,
        scratch_shapes=[
            pltpu.VMEM((nh, 2, 3, 4, bq, HD), BF16),
            pltpu.VMEM((nh, 2, both, HD), BF16),
            pltpu.VMEM((24, both), F32),
            pltpu.VMEM((3, 2, bq, both), BF16),
            pltpu.VMEM((3, 2, bq, bq), BF16),
            pltpu.VMEM((words, both), BF16),
            pltpu.VMEM((16, both), F32),
            pltpu.VMEM((8, both), F32),
            pltpu.VMEM((8, both), F32),
            pltpu.VMEM((8, both), F32),
            pltpu.VMEM((HD, both), F32),
            pltpu.VMEM((HD, both), F32),
            pltpu.VMEM((nh, 2, 3, 4, bq, HD), BF16),
            pltpu.VMEM((nh, 2, 2, 3, bq, HD), BF16),
            pltpu.VMEM((nh, 2, 2, 2, bq, HD), BF16),
            pltpu.VMEM((nh, 4, both, HD), BF16),
            pltpu.VMEM((2, HD, words), F32),
            pltpu.VMEM((8, words), F32),
            pltpu.VMEM((nh + 2, words, HD), F32),
            pltpu.VMEM((2 * ny - 1, nh + 2, words // (2 * ny), HD), F32),
            pltpu.VMEM((nx - 1, nh + 2, words // (2 * ny * nx), HD), F32),
            pltpu.VMEM((nh + 2, words, HD), F32),
            pltpu.VMEM((3 * nh, words, HD), F32),
            pltpu.VMEM((2 * ny - 1, 3 * nh - 2, words // (2 * ny), HD), F32),
            pltpu.VMEM((nx - 1, 3 * nh - 2, words // (2 * ny * nx), HD), F32),
            pltpu.VMEM((nx - 1, 2, words // nx, HD), F32),
            pltpu.VMEM((2 * ny - 1, 2, words // (2 * ny * nx), HD), F32),
            pltpu.VMEM((3 * nh, words, HD), F32),
            pltpu.VMEM((nh, 2, both, HD), F32),
            pltpu.VMEM((4, nh, words, HD), BF16),
            dma((nh, 4)),
            dma((nh, 4)),
            dma((nh, 4)),
            dma((3,)),
            dma((nh, 2, 2)),
            dma((nh, 2, 2)),
            dma((nh, 3, 2)),
            dma((nh, 3, 2)),
            dma((nh, 3, 2)),
            dma((nh, 3, 2)),
            dma((nh, 2)),
            dma((nh, 2)),
            dma((nh, 4)),
            dma((nh, 4)),
            dma((nh, 4)),
            dma((3, 4, 2 * ny - 1)),
            dma((3, 4, 2 * ny - 1)),
            dma((4, nh)),
            dma((4, nh)),
            dma((4, nh)),
        ],
        compiler_params=pltpu.CompilerParams(
            collective_id=0, has_side_effects=True, vmem_limit_bytes=62 * 2**20
        ),
        name="window",
    )(query, key, value, grad, mask, text_query, text_key, text_value, text_grad, text_mask)


def settle_kernel(*refs):
    n = (len(refs) - 2) // 3
    sems_in, sems_out = refs[-2:]
    ins = [pltpu.make_async_copy(refs[j], refs[2 * n + j], sems_in.at[j]) for j in range(n)]
    outs = [pltpu.make_async_copy(refs[2 * n + j], refs[n + j], sems_out.at[j]) for j in range(n)]
    for copy in ins:
        copy.start()
    for j in range(n):
        ins[j].wait()
        outs[j].start()
    for copy in outs:
        copy.wait()


def settle(arrays):
    hbm = pl.BlockSpec(memory_space=pl.ANY)
    n = len(arrays)
    return pl.pallas_call(
        settle_kernel,
        out_shape=[jax.ShapeDtypeStruct(a.shape, a.dtype) for a in arrays],
        in_specs=[hbm] * n,
        out_specs=[hbm] * n,
        scratch_shapes=[pltpu.VMEM(a.shape, a.dtype) for a in arrays]
        + [pltpu.SemaphoreType.DMA((n,)), pltpu.SemaphoreType.DMA((n,))],
        compiler_params=pltpu.CompilerParams(vmem_limit_bytes=62 * 2**20),
        name="settle",
    )(*arrays)


def edge_mask(tile_lists, tile, slot):
    lists = tile_lists.reshape(4, 3, 3, 3)
    rows = []
    for col in (0, 3):
        on = jnp.any((lists >= 0) & (lists % 4 == col), axis=-1)
        rows.append(on)
    on = jnp.stack(rows, -1)
    on = jnp.transpose(on, (1, 2, 3, 0)).reshape(18, 4).astype(F32)
    on = jnp.repeat(on, tile, axis=1)
    pad = jnp.zeros((6, on.shape[1]), F32)
    return jnp.where(
        slot == 0, jnp.concatenate([on, pad]), jnp.concatenate([pad, on])
    )


def body(
    query_latent,
    key_latent,
    value_latent,
    grad_latent,
    tile_lists,
    text_query,
    text_key,
    text_value,
    grad_text,
    text_mask,
):
    frames, rows, width_tiles, tile, channels = query_latent.shape
    flat = [
        a.reshape(width_tiles * tile, channels)
        for a in (query_latent, key_latent, value_latent, grad_latent)
    ]
    mask = edge_mask(tile_lists, tile, lax.axis_index("tm") % 2)
    text_on = jnp.broadcast_to(
        (text_mask > 0).astype(F32)[:, None], (text_mask.shape[0], HD)
    )
    outs = window_pass(*flat, mask, text_query, text_key, text_value, grad_text, text_on)
    outs = settle(outs)
    return tuple(a.reshape(query_latent.shape) for a in outs[:4]) + tuple(outs[4:])


def solution(mesh):
    latent = P("tm", "height", None, None, "heads")
    text = P(None, "heads")
    in_specs = (latent,) * 4 + (P("tm", "height", None, None),) + (text,) * 4 + (P(),)
    out_specs = (latent,) * 4 + (text,) * 4
    return jax.shard_map(body, mesh=mesh, in_specs=in_specs, out_specs=out_specs, check_vma=False)
```

```python
import functools
import math

import jax
import jax.numpy as jnp
from jax import lax
from jax.experimental import pallas as pl
from jax.experimental.pallas import tpu as pltpu
from jax.sharding import PartitionSpec as P

HD = 128
NEG = -1e30
F32 = jnp.float32
BF16 = jnp.bfloat16
MESH = pl.DeviceIdType.MESH


def mm_nt(a, b):
    return lax.dot_general(a, b, (((1,), (1,)), ((), ())), preferred_element_type=F32)


def mm_tn(a, b):
    return lax.dot_general(a, b, (((0,), (0,)), ((), ())), preferred_element_type=F32)


def mm_nn(a, b):
    return jnp.dot(a, b, preferred_element_type=F32)


def window_kernel(
    nx,
    ny,
    q_ref,
    k_ref,
    v_ref,
    g_ref,
    mask_ref,
    tq_ref,
    tk_ref,
    tv_ref,
    tg_ref,
    tm_ref,
    out_ref,
    dq_ref,
    dk_ref,
    dv_ref,
    tout_ref,
    tdq_ref,
    tdk_ref,
    tdv_ref,
    kv,
    qg,
    mask,
    p_mid,
    p_side,
    p_text,
    m_saved,
    m_run,
    l_run,
    d_row,
    o_t,
    dq_t,
    share,
    g1r,
    g2r,
    fin,
    st,
    lse,
    part0,
    gh0,
    gx0,
    whole0,
    part,
    part_b,
    gh,
    gx,
    whole,
    t_kv,
    t_fin,
    sem_loc,
    sem_r1s,
    sem_r1r,
    sem_mask,
    sem_r2s,
    sem_r2r,
    sem_r3s,
    sem_r3r,
    sem_g1s,
    sem_g1r,
    sem_g2s,
    sem_g2r,
    sem_g3s,
    sem_g3r,
    sem_out,
    sem_txs,
    sem_txr,
    sem_tfs,
    sem_tfr,
    sem_tfl,
):
    bq = q_ref.shape[0]
    tile = bq // 4
    heads = q_ref.shape[1] // HD
    nh = heads // 2
    both = 2 * bq
    scale = 1.0 / math.sqrt(HD)
    c2 = scale * math.log2(math.e)

    t = lax.axis_index("tm")
    h = lax.axis_index("height")
    c = lax.axis_index("heads")
    x = t // 2
    zl = t % 2
    zh = h // ny
    half = (zl + zh) % 2
    other = 1 - half
    rows_all = 2 * ny

    def at_grid(xx, hh):
        return (2 * xx + (half + hh // ny) % 2, hh, c)

    partner = (2 * x + 1 - zl, h, c)
    left = (t - 2, h, c)
    right = (t + 2, h, c)
    up = at_grid(x, h - 1)
    down = at_grid(x, h + 1)
    has_left = x > 0
    has_right = x < nx - 1
    has_up = h > 0
    has_down = h < rows_all - 1

    words_n = tq_ref.shape[0]
    h_peers = [(j, (h + j + 1) % rows_all) for j in range(rows_all - 1)]
    x_peers = [(j, (x + j + 1) % nx) for j in range(nx - 1)]

    barrier = pltpu.get_barrier_semaphore()
    pl.semaphore_signal(barrier, inc=1, device_id=partner, device_id_type=MESH)
    for _, to in h_peers:
        pl.semaphore_signal(barrier, inc=1, device_id=at_grid(x, to), device_id_type=MESH)
    for _, to in x_peers:
        pl.semaphore_signal(barrier, inc=1, device_id=at_grid(to, h), device_id_type=MESH)
    pl.semaphore_wait(barrier, nx + rows_all - 1)

    def remote(src, dst, ssem, rsem, dev):
        return pltpu.make_async_remote_copy(
            src_ref=src, dst_ref=dst, send_sem=ssem, recv_sem=rsem,
            device_id=dev, device_id_type=MESH,
        )

    def head_cols(which, i):
        return pl.ds(pl.multiple_of((which * nh + i) * HD, HD), HD)

    ins = (q_ref, k_ref, v_ref, g_ref)
    outs = (out_ref, dq_ref, dk_ref, dv_ref)

    def landing(i, j):
        if j == 0:
            return qg.at[i, 0, pl.ds(pl.multiple_of(zl * bq, bq), bq)]
        if j == 3:
            return qg.at[i, 1, pl.ds(pl.multiple_of(zl * bq, bq), bq)]
        return kv.at[i, j - 1, 1, 1 + zl]

    def r1(i, j):
        return remote(
            ins[j].at[:, head_cols(other, i)], landing(i, j),
            sem_r1s.at[i, j], sem_r1r.at[i, j], partner,
        )

    def local_in(i, j):
        return pltpu.make_async_copy(
            ins[j].at[:, head_cols(half, i)], landing(i, j), sem_loc.at[i, j]
        )

    mask_cols = pl.ds(pl.multiple_of(zl * bq, bq), bq)
    mask_out = remote(mask_ref, mask.at[:, mask_cols], sem_mask.at[0], sem_mask.at[1], partner)
    mask_own = pltpu.make_async_copy(mask_ref, mask.at[:, mask_cols], sem_mask.at[2])

    def r2(i, d, s):
        return remote(
            kv.at[i, :, 1, 1 + s], kv.at[i, :, 2 - 2 * d, 1 + s],
            sem_r2s.at[i, d, s], sem_r2r.at[i, d, s], (up, down)[d],
        )

    def r3(i, r, d):
        return remote(
            kv.at[i, :, r, 1 + d], kv.at[i, :, r, 3 - 3 * d],
            sem_r3s.at[i, r, d], sem_r3r.at[i, r, d], (left, right)[d],
        )

    def g1(i, r, d):
        return remote(
            share.at[i, :, r, 3 * d], g1r.at[i, d, :, r],
            sem_g1s.at[i, r, d], sem_g1r.at[i, r, d], (left, right)[d],
        )

    def g2(i, d):
        return remote(
            share.at[i, :, 2 * d, pl.ds(1, 2)], g2r.at[i, d],
            sem_g2s.at[i, d], sem_g2r.at[i, d], (up, down)[d],
        )

    def g3(i, j):
        return remote(
            fin.at[i, j, pl.ds(pl.multiple_of((1 - zl) * bq, bq), bq)],
            outs[j].at[:, head_cols(half, i)],
            sem_g3s.at[i, j], sem_g3r.at[i, j], partner,
        )

    def local_out(i, j):
        return pltpu.make_async_copy(
            fin.at[i, j, pl.ds(pl.multiple_of(zl * bq, bq), bq)],
            outs[j].at[:, head_cols(half, i)], sem_out.at[i, j],
        )

    def row_on(r):
        return (h + r - 1 >= 0) & (h + r - 1 < rows_all)

    side_on = (has_left, has_right)
    vert_on = (has_up, has_down)

    def wait_in(i, which):
        for j in which:
            r1(i, j).wait_recv()

    def wait_local(i, which):
        for j in which:
            local_in(i, j).wait()

    def start_r2(i, s):
        for d in range(2):
            pl.when(vert_on[d])(lambda d=d: r2(i, d, s).start())

    def wait_r2(i):
        for d in range(2):
            @pl.when(vert_on[1 - d])
            def _(d=d):
                r2(i, d, 0).wait_recv()
                r2(i, d, 1).wait_recv()

    def start_own(i):
        wait_local(i, (1, 2))
        start_r2(i, zl)
        for d in range(2):
            pl.when((zl == d) & side_on[d])(lambda d=d: r3(i, 1, d).start())

    def start_traded(i):
        wait_in(i, (1, 2))
        start_r2(i, 1 - zl)
        for d in range(2):
            pl.when((zl != d) & side_on[d])(lambda d=d: r3(i, 1, d).start())

    def for_sides(i, rows, act, flip):
        for r in rows:
            for d in range(2):
                on = side_on[1 - d] if flip else side_on[d]
                if r != 1:
                    on = on & row_on(r)
                pl.when(on)(lambda r=r, d=d: act(i, r, d))

    def start_r3(i, rows):
        for_sides(i, rows, lambda i, r, d: r3(i, r, d).start(), False)

    def wait_r3(i):
        for_sides(i, (0, 1, 2), lambda i, r, d: r3(i, r, d).wait_recv(), True)

    first = (x == 0) & (h == 0)

    band = words_n // rows_all

    def band_of(hh):
        return pl.ds(pl.multiple_of(hh * band, 8), band)

    own_band = band_of(h)

    class Round:
        def __init__(self, n, first_src, src, got_h, got_x, dst, lo, hi):
            self.n, self.first_src, self.src, self.dst = n, first_src, src, dst
            self.got_h, self.got_x = got_h, got_x
            self.lo, self.hi, self.tiles = lo, hi, pl.ds(lo, hi - lo)

        def copies(self, stage):
            if stage == 0:
                trips = [
                    (self.first_src.at[self.tiles, band_of(to)], self.got_h.at[j, self.tiles], (x, to))
                    for j, to in h_peers
                ]
            elif stage == 1:
                own = self.src.at[self.tiles, own_band]
                trips = [(own, self.got_x.at[j, self.tiles], (to, h)) for j, to in x_peers]
            else:
                own = self.dst.at[self.tiles, own_band]
                trips = [(own, own, (x, to)) for j, to in h_peers]
            return [
                remote(
                    a, b, sem_txs.at[self.n, stage, j], sem_txr.at[self.n, stage, j], at_grid(*to)
                )
                for j, (a, b, to) in enumerate(trips)
            ]

        def send(self, stage):
            for copy in self.copies(stage):
                copy.start()

        def got(self, stage):
            for copy in self.copies(stage):
                copy.wait_recv()

        def sent(self):
            for stage in range(3):
                for copy in self.copies(stage):
                    copy.wait_send()

    round0 = Round(0, part0, part0, gh0, gx0, whole0, 0, nh + 2)
    round1 = Round(1, part_b, part, gh, gx, whole, 0, 3 * nh - 2)
    round2 = Round(2, part_b, part, gh, gx, whole, 3 * nh - 2, 3 * nh)

    def merged(own, parts):
        peak = own(nh)
        for p in parts:
            peak = jnp.maximum(peak, p[nh])
        f = jnp.exp2(own(nh) - peak)
        total = own(nh + 1) * f
        values = [own(i) * f[:, i : i + 1] for i in range(nh)]
        for p in parts:
            f = jnp.exp2(p[nh] - peak)
            total = total + p[nh + 1] * f
            values = [v + p[i] * f[:, i : i + 1] for i, v in enumerate(values)]
        return values, peak, total

    def merge0_h():
        round0.got(0)
        values, peak, total = merged(
            lambda a: part0[a, own_band], [gh0.at[j] for j, _ in h_peers]
        )
        for i in range(nh):
            part0[i, own_band] = values[i]
        part0[nh, own_band] = peak
        part0[nh + 1, own_band] = total
        round0.send(1)

    def merge0_x():
        round0.got(1)
        values, peak, total = merged(
            lambda a: part0[a, own_band], [gx0.at[j] for j, _ in x_peers]
        )
        for i in range(nh):
            value = values[i] / total[:, i : i + 1]
            whole0[i, own_band] = value.astype(BF16).astype(F32)
        whole0[nh, own_band] = peak + jnp.log2(total)
        whole0[nh + 1, own_band] = total
        round0.send(2)

    def launch(rnd):
        for a in range(rnd.lo, rnd.hi):
            part_b[a] = part[a].astype(BF16)
        rnd.send(0)

    def merge_h(rnd):
        rnd.got(0)
        for a in range(rnd.lo, rnd.hi):
            total = part[a, own_band]
            for j, _ in h_peers:
                total = total + gh[j, a].astype(F32)
            part[a, own_band] = total
        rnd.send(1)

    def merge_x(rnd):
        rnd.got(1)
        for a in range(rnd.lo, rnd.hi):
            total = part[a, own_band]
            for j, _ in x_peers:
                total = total + gx[j, a]
            whole[a, own_band] = total.astype(BF16)
        rnd.send(2)

    def text_scores(i):
        keys = kv[i, 0, 1, 1:3].reshape(both, HD)
        return mm_nt(keys, tq_ref[:, head_cols(half, i)]) * c2

    def words_scores(i):
        cols = head_cols(half, i)
        s = mm_nt(tk_ref[:, cols], tq_ref[:, cols]) * c2
        return jnp.where(tm_ref[:, 0:1] > 0.5, s, NEG)

    def text_partial(i):
        def one(s, v, old):
            peak = jnp.max(s, 0, keepdims=True)
            if old is not None:
                peak = jnp.maximum(peak, old[0])
            e = jnp.exp2(s - peak)
            total = jnp.sum(e, 0, keepdims=True)
            value = mm_tn(v, e.astype(BF16))
            if old is not None:
                f = jnp.exp2(old[0] - peak)
                total = total + old[1] * f
                value = value + old[2].T * f
            st[0, pl.ds(i, 1)] = peak
            st[1, pl.ds(i, 1)] = total
            part0[i] = value.T

        one(text_scores(i), kv[i, 1, 1, 1:3].reshape(both, HD), None)

        @pl.when(first)
        def _():
            old = (st[0, pl.ds(i, 1)], st[1, pl.ds(i, 1)], part0[i])
            one(words_scores(i), tv_ref[:, head_cols(half, i)], old)

    def text_start():
        part0[nh] = st[0].T
        part0[nh + 1] = st[1].T
        round0.send(0)

    def text_backward(i):
        cols = head_cols(half, i)
        row = lse[pl.ds(i, 1)]
        q = tq_ref[:, cols]
        g = tg_ref[:, cols]
        o_round = whole0[i]
        t_fin[0, i] = o_round.astype(BF16)
        delta = jnp.sum((o_round * g.astype(F32)).T, 0, keepdims=True)

        def one(s, k, v):
            p = jnp.exp2(s - row)
            ds = (p * (mm_nt(v, g) - delta)).astype(BF16)
            return (
                (mm_tn(k, ds) * scale).T,
                mm_nn(ds, q) * scale,
                mm_nn(p.astype(BF16), g),
            )

        a_q, a_k, a_v = one(
            text_scores(i), kv[i, 0, 1, 1:3].reshape(both, HD), kv[i, 1, 1, 1:3].reshape(both, HD)
        )
        part[i] = a_q
        t_kv[i, 0] = a_k
        t_kv[i, 1] = a_v

        @pl.when(first)
        def _():
            b_q, b_k, b_v = one(words_scores(i), tk_ref[:, cols], tv_ref[:, cols])
            part[i] += b_q
            part[nh + 2 * i] += b_k
            part[nh + 2 * i + 1] += b_v

    t_outs = (tout_ref, tdq_ref, tdk_ref, tdv_ref)

    def t_out(j, i):
        return remote(
            t_fin.at[j, i], t_outs[j].at[:, head_cols(half, i)],
            sem_tfs.at[j, i], sem_tfr.at[j, i], partner,
        )

    def t_loc(j, i):
        return pltpu.make_async_copy(
            t_fin.at[j, i], t_outs[j].at[:, head_cols(half, i)], sem_tfl.at[j, i]
        )

    def send_text(j, i):
        t_out(j, i).start()
        t_loc(j, i).start()

    def finish_td(i):
        for a in range(2):
            t_fin[2 + a, i] = whole[nh + 2 * i + a]
            send_text(2 + a, i)

    for i in range(nh):
        for j in (1, 2):
            local_in(i, j).start()
    for i, js in ((0, (1, 2)), (0, (0, 3)), (1, (1, 2)), (2, (1, 2)), (1, (0, 3)), (2, (0, 3))):
        for j in js:
            r1(i, j).start()
    for i in range(nh):
        for j in (0, 3):
            local_in(i, j).start()
    start_own(0)

    mask_out.start()
    mask_own.start()

    @pl.loop(0, nh)
    def _(i):
        @pl.when(jnp.logical_not(has_right))
        def _():
            g1r[i, 0] = jnp.zeros(g1r.shape[2:], BF16)

        @pl.when(jnp.logical_not(has_left))
        def _():
            g1r[i, 1] = jnp.zeros(g1r.shape[2:], BF16)

        @pl.when(jnp.logical_not(has_down))
        def _():
            g2r[i, 0] = jnp.zeros(g2r.shape[2:], BF16)

        @pl.when(jnp.logical_not(has_up))
        def _():
            g2r[i, 1] = jnp.zeros(g2r.shape[2:], BF16)

    @pl.loop(nh, 3 * nh)
    def _(a):
        part[a] = jnp.zeros(part.shape[1:], F32)

    st[...] = jnp.zeros(st.shape, F32)
    start_traded(0)
    text_partial(0)
    mask_own.wait()
    mask_out.wait_recv()

    def online(s, v, save, qs, keep):
        m_old = m_run[0:1, qs]
        m_new = jnp.maximum(m_old, jnp.max(s, 0, keepdims=True))
        alpha = jnp.exp2(m_old - m_new)
        e = jnp.exp2(s - m_new)
        l_run[0:1, qs] = l_run[0:1, qs] * alpha + jnp.sum(e, 0, keepdims=True)
        m_run[0:1, qs] = m_new
        m_saved[pl.ds(save, 1), qs] = m_new
        w = e.astype(BF16)
        keep(w)
        o_t[:, qs] = o_t[:, qs] * alpha + mm_tn(v, w)

    def fwd(i, row, col, qs, keep):
        s = mm_nt(kv[i, 0, row, col], qg[i, 0, qs]) * c2
        at = (col * 3 + row) * 2
        first = mask[pl.ds(at, 1), qs]
        last = mask[pl.ds(at + 1, 1), qs]
        s = jnp.concatenate(
            [
                jnp.where(first > 0.5, s[:tile], NEG),
                s[tile : 3 * tile],
                jnp.where(last > 0.5, s[3 * tile :], NEG),
            ],
            axis=0,
        )
        online(s, kv[i, 1, row, col], col * 3 + row, qs, keep)

    def fwd_mid(i, row, col):
        def keep(w):
            p_mid[row, col - 1] = w

        fwd(i, row, col, pl.ds(0, both), keep)

    def fwd_side(i, row, d):
        def keep(w):
            p_side[row, d] = w

        fwd(i, row, 3 * d, pl.ds(d * bq, bq), keep)

    def back(w0, k, v, q, g, save, qs):
        f = jnp.exp2(m_saved[pl.ds(save, 1), qs] - m_run[0:1, qs]) * l_run[0:1, qs]
        dp = mm_nt(v, g)
        w = w0.astype(F32) * f
        ds = (w * (dp - d_row[0:1, qs])).astype(BF16)
        d_k = mm_nn(ds, q) * scale
        d_v = mm_nn(w.astype(BF16), g)
        dq_t[:, qs] += mm_tn(k, ds)
        return d_k, d_v

    def bwd(i, row, col, qs, w0):
        d_k, d_v = back(
            w0, kv[i, 0, row, col], kv[i, 1, row, col], qg[i, 0, qs], qg[i, 1, qs],
            col * 3 + row, qs,
        )
        share[i, 0, row, col] = d_k.astype(BF16)
        share[i, 1, row, col] = d_v.astype(BF16)

    def add_g1(i):
        for_sides(i, (0, 2), lambda i, r, d: g1(i, r, d).wait_recv(), True)
        for r in (0, 2):
            @pl.when(row_on(r))
            def _(r=r):
                for a in range(2):
                    for d in range(2):
                        col = 2 - d
                        share[i, a, r, col] = (
                            share[i, a, r, col].astype(F32) + g1r[i, d, a, r].astype(F32)
                        ).astype(BF16)
        for d in range(2):
            pl.when(vert_on[d])(lambda d=d: g2(i, d).start())

    def add_g2(i):
        for_sides(i, (1,), lambda i, r, d: g1(i, r, d).wait_recv(), True)
        for d in range(2):
            pl.when(vert_on[1 - d])(lambda d=d: g2(i, d).wait_recv())
        for a in range(2):
            for s in range(2):
                total = (
                    share[i, a, 1, 1 + s].astype(F32)
                    + g1r[i, 1 - s, a, 1].astype(F32)
                    + g2r[i, 0, a, s].astype(F32)
                    + g2r[i, 1, a, s].astype(F32)
                    + t_kv[i, a, s * bq : (s + 1) * bq]
                )
                fin[i, 2 + a, s * bq : (s + 1) * bq] = total.astype(BF16)
        for j in (2, 3):
            g3(i, j).start()
            local_out(i, j).start()

    @pl.loop(0, nh)
    def _(i):
        m_run[0:1, :] = jnp.full((1, both), NEG, F32)
        l_run[0:1, :] = jnp.zeros((1, both), F32)
        o_t[...] = jnp.zeros(o_t.shape, F32)
        dq_t[...] = jnp.zeros(dq_t.shape, F32)

        wait_local(i, (0, 3))
        wait_in(i, (0, 3))

        @pl.loop(1, 3)
        def _(col):
            fwd_mid(i, 1, col)

        @pl.when(i == 0)
        def _():
            wait_r2(0)
            start_r3(0, (0, 2))
            start_own(1)
            start_traded(1)
            text_partial(1)

        @pl.when(i == 1)
        def _():
            merge0_x()

        @pl.loop(0, 4)
        def _(n):
            row = (n // 2) * 2

            @pl.when(row_on(row))
            def _():
                fwd_mid(i, row, 1 + n % 2)

        @pl.when(i == 0)
        def _():
            start_own(2)
            start_traded(2)
            text_partial(2)
            text_start()
            wait_r2(1)
            start_r3(1, (0, 2))

        @pl.when(i == 2)
        def _():
            merge_x(round1)

        words = head_cols(half, i)
        s_text = jnp.where(
            tm_ref[:, 0:1] > 0.5, mm_nt(tk_ref[:, words], qg[i, 0]) * c2, NEG
        )

        def keep_text(w):
            p_text[...] = w

        online(s_text, tv_ref[:, words], 12, pl.ds(0, both), keep_text)

        wait_r3(i)
        for d in range(2):
            @pl.when(side_on[d])
            def _(d=d):
                @pl.loop(0, 3)
                def _(row):
                    @pl.when(row_on(row))
                    def _():
                        fwd_side(i, row, d)

        @pl.when(i == 0)
        def _():
            wait_r2(2)
            start_r3(2, (0, 2))
            merge0_h()

        inv = 1.0 / l_run[0:1, :]
        l_run[0:1, :] = inv
        o_round = (o_t[...] * inv).astype(BF16).astype(F32)
        fin[i, 0] = o_round.T.astype(BF16)
        g_t = qg[i, 1].astype(F32).T
        d_row[0:1, :] = jnp.sum(o_round * g_t, 0, keepdims=True)
        g3(i, 0).start()
        local_out(i, 0).start()

        d_k, d_v = back(
            p_text[...], tk_ref[:, words], tv_ref[:, words], qg[i, 0], qg[i, 1],
            12, pl.ds(0, both),
        )
        part[nh + 2 * i] += d_k
        part[nh + 2 * i + 1] += d_v

        @pl.when(i == 2)
        def _():
            launch(round2)

        for d in range(2):
            @pl.when(side_on[d])
            def _(d=d):
                @pl.loop(0, 3)
                def _(n):
                    row = (2 * n) % 3

                    @pl.when(row_on(row))
                    def _():
                        bwd(i, row, 3 * d, pl.ds(d * bq, bq), p_side[row, d])

            if d == 0:
                @pl.when(i == 2)
                def _():
                    merge_h(round2)

            for row in (0, 2, 1):
                pl.when(side_on[d] & row_on(row))(lambda row=row, d=d: g1(i, row, d).start())

        @pl.when(i == 1)
        def _():
            round0.got(2)
            lse[...] = whole0[nh].T[0:8]

            @pl.loop(0, nh)
            def _(j):
                text_backward(j)
                send_text(0, j)

            launch(round1)

        @pl.when(i > 0)
        def _():
            add_g1(i - 1)

        for row in (0, 2, 1):
            @pl.when(row_on(row))
            def _(row=row):
                @pl.loop(1, 3)
                def _(col):
                    bwd(i, row, col, pl.ds(0, both), p_mid[row, col - 1])

            if row == 2:
                @pl.when(i == 2)
                def _():
                    merge_x(round2)

        @pl.when(i == 1)
        def _():
            merge_h(round1)

        @pl.when(i == 2)
        def _():
            round1.got(2)
            for j in range(nh):
                t_fin[1, j] = whole[j]
                send_text(1, j)
            for j in range(nh - 1):
                finish_td(j)

        @pl.when(i > 0)
        def _():
            add_g2(i - 1)

        fin[i, 1] = (dq_t[...] * scale).T.astype(BF16)
        g3(i, 1).start()
        local_out(i, 1).start()

    add_g1(nh - 1)
    round2.got(2)
    finish_td(nh - 1)
    add_g2(nh - 1)

    for rnd in (round0, round1, round2):
        rnd.sent()

    for n in range(4):
        for j in range(nh):
            t_out(n, j).wait_send()
            t_out(n, j).wait_recv()
            t_loc(n, j).wait()

    mask_out.wait_send()

    @pl.loop(0, nh)
    def _(i):
        for j in range(4):
            r1(i, j).wait_send()
            g3(i, j).wait_send()
            g3(i, j).wait_recv()
            local_out(i, j).wait()
        for d in range(2):
            @pl.when(vert_on[d])
            def _(d=d):
                r2(i, d, 0).wait_send()
                r2(i, d, 1).wait_send()
                g2(i, d).wait_send()
        for_sides(i, (0, 1, 2), lambda i, r, d: r3(i, r, d).wait_send(), False)
        for_sides(i, (0, 1, 2), lambda i, r, d: g1(i, r, d).wait_send(), False)


def window_pass(
    query, key, value, grad, mask, text_query, text_key, text_value, text_grad, text_mask
):
    nx = lax.axis_size("tm") // 2
    ny = lax.axis_size("height") // 2
    bq, channels = query.shape
    nh = channels // HD // 2
    words = text_key.shape[0]
    both = 2 * bq
    sds = jax.ShapeDtypeStruct
    hbm = pl.BlockSpec(memory_space=pl.ANY)
    vmem = pl.BlockSpec(memory_space=pltpu.VMEM)
    dma = pltpu.SemaphoreType.DMA
    return pl.pallas_call(
        functools.partial(window_kernel, nx, ny),
        out_shape=[sds((bq, channels), BF16)] * 4 + [sds((words, channels), BF16)] * 4,
        in_specs=[hbm] * 4 + [vmem] * 6,
        out_specs=[hbm] * 8,
        scratch_shapes=[
            pltpu.VMEM((nh, 2, 3, 4, bq, HD), BF16),
            pltpu.VMEM((nh, 2, both, HD), BF16),
            pltpu.VMEM((24, both), F32),
            pltpu.VMEM((3, 2, bq, both), BF16),
            pltpu.VMEM((3, 2, bq, bq), BF16),
            pltpu.VMEM((words, both), BF16),
            pltpu.VMEM((16, both), F32),
            pltpu.VMEM((8, both), F32),
            pltpu.VMEM((8, both), F32),
            pltpu.VMEM((8, both), F32),
            pltpu.VMEM((HD, both), F32),
            pltpu.VMEM((HD, both), F32),
            pltpu.VMEM((nh, 2, 3, 4, bq, HD), BF16),
            pltpu.VMEM((nh, 2, 2, 3, bq, HD), BF16),
            pltpu.VMEM((nh, 2, 2, 2, bq, HD), BF16),
            pltpu.VMEM((nh, 4, both, HD), BF16),
            pltpu.VMEM((2, HD, words), F32),
            pltpu.VMEM((8, words), F32),
            pltpu.VMEM((nh + 2, words, HD), F32),
            pltpu.VMEM((2 * ny - 1, nh + 2, words // (2 * ny), HD), F32),
            pltpu.VMEM((nx - 1, nh + 2, words // (2 * ny), HD), F32),
            pltpu.VMEM((nh + 2, words, HD), F32),
            pltpu.VMEM((3 * nh, words, HD), F32),
            pltpu.VMEM((3 * nh, words, HD), BF16),
            pltpu.VMEM((2 * ny - 1, 3 * nh, words // (2 * ny), HD), BF16),
            pltpu.VMEM((nx - 1, 3 * nh, words // (2 * ny), HD), F32),
            pltpu.VMEM((3 * nh, words, HD), BF16),
            pltpu.VMEM((nh, 2, both, HD), F32),
            pltpu.VMEM((4, nh, words, HD), BF16),
            dma((nh, 4)),
            dma((nh, 4)),
            dma((nh, 4)),
            dma((3,)),
            dma((nh, 2, 2)),
            dma((nh, 2, 2)),
            dma((nh, 3, 2)),
            dma((nh, 3, 2)),
            dma((nh, 3, 2)),
            dma((nh, 3, 2)),
            dma((nh, 2)),
            dma((nh, 2)),
            dma((nh, 4)),
            dma((nh, 4)),
            dma((nh, 4)),
            dma((3, 3, 2 * ny - 1)),
            dma((3, 3, 2 * ny - 1)),
            dma((4, nh)),
            dma((4, nh)),
            dma((4, nh)),
        ],
        compiler_params=pltpu.CompilerParams(
            collective_id=0, has_side_effects=True, vmem_limit_bytes=62 * 2**20
        ),
        name="window",
    )(query, key, value, grad, mask, text_query, text_key, text_value, text_grad, text_mask)


def settle_kernel(*refs):
    n = (len(refs) - 2) // 3
    sems_in, sems_out = refs[-2:]
    ins = [pltpu.make_async_copy(refs[j], refs[2 * n + j], sems_in.at[j]) for j in range(n)]
    outs = [pltpu.make_async_copy(refs[2 * n + j], refs[n + j], sems_out.at[j]) for j in range(n)]
    for copy in ins:
        copy.start()
    for j in range(n):
        ins[j].wait()
        outs[j].start()
    for copy in outs:
        copy.wait()


def settle(arrays):
    hbm = pl.BlockSpec(memory_space=pl.ANY)
    n = len(arrays)
    return pl.pallas_call(
        settle_kernel,
        out_shape=[jax.ShapeDtypeStruct(a.shape, a.dtype) for a in arrays],
        in_specs=[hbm] * n,
        out_specs=[hbm] * n,
        scratch_shapes=[pltpu.VMEM(a.shape, a.dtype) for a in arrays]
        + [pltpu.SemaphoreType.DMA((n,)), pltpu.SemaphoreType.DMA((n,))],
        compiler_params=pltpu.CompilerParams(vmem_limit_bytes=62 * 2**20),
        name="settle",
    )(*arrays)


def edge_mask(tile_lists, tile, slot):
    lists = tile_lists.reshape(4, 3, 3, 3)
    rows = []
    for col in (0, 3):
        on = jnp.any((lists >= 0) & (lists % 4 == col), axis=-1)
        rows.append(on)
    on = jnp.stack(rows, -1)
    on = jnp.transpose(on, (1, 2, 3, 0)).reshape(18, 4).astype(F32)
    on = jnp.repeat(on, tile, axis=1)
    pad = jnp.zeros((6, on.shape[1]), F32)
    return jnp.where(
        slot == 0, jnp.concatenate([on, pad]), jnp.concatenate([pad, on])
    )


def body(
    query_latent,
    key_latent,
    value_latent,
    grad_latent,
    tile_lists,
    text_query,
    text_key,
    text_value,
    grad_text,
    text_mask,
):
    frames, rows, width_tiles, tile, channels = query_latent.shape
    flat = [
        a.reshape(width_tiles * tile, channels)
        for a in (query_latent, key_latent, value_latent, grad_latent)
    ]
    mask = edge_mask(tile_lists, tile, lax.axis_index("tm") % 2)
    text_on = jnp.broadcast_to(
        (text_mask > 0).astype(F32)[:, None], (text_mask.shape[0], HD)
    )
    outs = window_pass(*flat, mask, text_query, text_key, text_value, grad_text, text_on)
    outs = settle(outs)
    return tuple(a.reshape(query_latent.shape) for a in outs[:4]) + tuple(outs[4:])


def solution(mesh):
    latent = P("tm", "height", None, None, "heads")
    text = P(None, "heads")
    in_specs = (latent,) * 4 + (P("tm", "height", None, None),) + (text,) * 4 + (P(),)
    out_specs = (latent,) * 4 + (text,) * 4
    return jax.shard_map(body, mesh=mesh, in_specs=in_specs, out_specs=out_specs, check_vma=False)
```

```python
import functools
import math

import jax
import jax.numpy as jnp
from jax import lax
from jax.experimental import pallas as pl
from jax.experimental.pallas import tpu as pltpu
from jax.sharding import PartitionSpec as P

HD = 128
NEG = -1e30
F32 = jnp.float32
BF16 = jnp.bfloat16
MESH = pl.DeviceIdType.MESH


def mm_nt(a, b):
    return lax.dot_general(a, b, (((1,), (1,)), ((), ())), preferred_element_type=F32)


def mm_tn(a, b):
    return lax.dot_general(a, b, (((0,), (0,)), ((), ())), preferred_element_type=F32)


def mm_nn(a, b):
    return jnp.dot(a, b, preferred_element_type=F32)


def window_kernel(
    nx,
    ny,
    q_ref,
    k_ref,
    v_ref,
    g_ref,
    mask_ref,
    tq_ref,
    tk_ref,
    tv_ref,
    tg_ref,
    tm_ref,
    out_ref,
    dq_ref,
    dk_ref,
    dv_ref,
    tout_ref,
    tdq_ref,
    tdk_ref,
    tdv_ref,
    kv,
    qg,
    mask,
    p_mid,
    p_side,
    p_text,
    m_saved,
    m_run,
    l_run,
    d_row,
    o_t,
    dq_t,
    share,
    g1r,
    g2r,
    fin,
    st,
    lse,
    part0,
    gh0,
    gx0,
    whole0,
    part,
    part_b,
    gh,
    gx,
    whole,
    t_kv,
    t_fin,
    sem_loc,
    sem_r1s,
    sem_r1r,
    sem_mask,
    sem_r2s,
    sem_r2r,
    sem_r3s,
    sem_r3r,
    sem_g1s,
    sem_g1r,
    sem_g2s,
    sem_g2r,
    sem_g3s,
    sem_g3r,
    sem_out,
    sem_txs,
    sem_txr,
    sem_tfs,
    sem_tfr,
    sem_tfl,
):
    bq = q_ref.shape[0]
    tile = bq // 4
    heads = q_ref.shape[1] // HD
    nh = heads // 2
    both = 2 * bq
    scale = 1.0 / math.sqrt(HD)
    c2 = scale * math.log2(math.e)

    t = lax.axis_index("tm")
    h = lax.axis_index("height")
    c = lax.axis_index("heads")
    x = t // 2
    zl = t % 2
    zh = h // ny
    half = (zl + zh) % 2
    other = 1 - half
    rows_all = 2 * ny

    def at_grid(xx, hh):
        return (2 * xx + (half + hh // ny) % 2, hh, c)

    partner = (2 * x + 1 - zl, h, c)
    left = (t - 2, h, c)
    right = (t + 2, h, c)
    up = at_grid(x, h - 1)
    down = at_grid(x, h + 1)
    has_left = x > 0
    has_right = x < nx - 1
    has_up = h > 0
    has_down = h < rows_all - 1

    words_n = tq_ref.shape[0]
    h_peers = [(j, (h + j + 1) % rows_all) for j in range(rows_all - 1)]
    x_peers = [(j, (x + j + 1) % nx) for j in range(nx - 1)]

    barrier = pltpu.get_barrier_semaphore()
    pl.semaphore_signal(barrier, inc=1, device_id=partner, device_id_type=MESH)
    for _, to in h_peers:
        pl.semaphore_signal(barrier, inc=1, device_id=at_grid(x, to), device_id_type=MESH)
    for _, to in x_peers:
        pl.semaphore_signal(barrier, inc=1, device_id=at_grid(to, h), device_id_type=MESH)
    pl.semaphore_wait(barrier, nx + rows_all - 1)

    def remote(src, dst, ssem, rsem, dev):
        return pltpu.make_async_remote_copy(
            src_ref=src, dst_ref=dst, send_sem=ssem, recv_sem=rsem,
            device_id=dev, device_id_type=MESH,
        )

    def head_cols(which, i):
        return pl.ds(pl.multiple_of((which * nh + i) * HD, HD), HD)

    ins = (q_ref, k_ref, v_ref, g_ref)
    outs = (out_ref, dq_ref, dk_ref, dv_ref)

    def landing(i, j):
        if j == 0:
            return qg.at[i, 0, pl.ds(pl.multiple_of(zl * bq, bq), bq)]
        if j == 3:
            return qg.at[i, 1, pl.ds(pl.multiple_of(zl * bq, bq), bq)]
        return kv.at[i, j - 1, 1, 1 + zl]

    def r1(i, j):
        return remote(
            ins[j].at[:, head_cols(other, i)], landing(i, j),
            sem_r1s.at[i, j], sem_r1r.at[i, j], partner,
        )

    def local_in(i, j):
        return pltpu.make_async_copy(
            ins[j].at[:, head_cols(half, i)], landing(i, j), sem_loc.at[i, j]
        )

    mask_cols = pl.ds(pl.multiple_of(zl * bq, bq), bq)
    mask_out = remote(mask_ref, mask.at[:, mask_cols], sem_mask.at[0], sem_mask.at[1], partner)
    mask_own = pltpu.make_async_copy(mask_ref, mask.at[:, mask_cols], sem_mask.at[2])

    def r2(i, d, s):
        return remote(
            kv.at[i, :, 1, 1 + s], kv.at[i, :, 2 - 2 * d, 1 + s],
            sem_r2s.at[i, d, s], sem_r2r.at[i, d, s], (up, down)[d],
        )

    def r3(i, r, d):
        return remote(
            kv.at[i, :, r, 1 + d], kv.at[i, :, r, 3 - 3 * d],
            sem_r3s.at[i, r, d], sem_r3r.at[i, r, d], (left, right)[d],
        )

    def g1(i, r, d):
        return remote(
            share.at[i, :, r, 3 * d], g1r.at[i, d, :, r],
            sem_g1s.at[i, r, d], sem_g1r.at[i, r, d], (left, right)[d],
        )

    def g2(i, d):
        return remote(
            share.at[i, :, 2 * d, pl.ds(1, 2)], g2r.at[i, d],
            sem_g2s.at[i, d], sem_g2r.at[i, d], (up, down)[d],
        )

    def g3(i, j):
        return remote(
            fin.at[i, j, pl.ds(pl.multiple_of((1 - zl) * bq, bq), bq)],
            outs[j].at[:, head_cols(half, i)],
            sem_g3s.at[i, j], sem_g3r.at[i, j], partner,
        )

    def local_out(i, j):
        return pltpu.make_async_copy(
            fin.at[i, j, pl.ds(pl.multiple_of(zl * bq, bq), bq)],
            outs[j].at[:, head_cols(half, i)], sem_out.at[i, j],
        )

    def row_on(r):
        return (h + r - 1 >= 0) & (h + r - 1 < rows_all)

    side_on = (has_left, has_right)
    vert_on = (has_up, has_down)

    def wait_in(i, which):
        for j in which:
            r1(i, j).wait_recv()

    def wait_local(i, which):
        for j in which:
            local_in(i, j).wait()

    def start_r2(i, s):
        for d in range(2):
            pl.when(vert_on[d])(lambda d=d: r2(i, d, s).start())

    def wait_r2(i):
        for d in range(2):
            @pl.when(vert_on[1 - d])
            def _(d=d):
                r2(i, d, 0).wait_recv()
                r2(i, d, 1).wait_recv()

    def start_own(i):
        wait_local(i, (1, 2))
        start_r2(i, zl)
        for d in range(2):
            pl.when((zl == d) & side_on[d])(lambda d=d: r3(i, 1, d).start())

    def start_traded(i):
        wait_in(i, (1, 2))
        start_r2(i, 1 - zl)
        for d in range(2):
            pl.when((zl != d) & side_on[d])(lambda d=d: r3(i, 1, d).start())

    def for_sides(i, rows, act, flip):
        for r in rows:
            for d in range(2):
                on = side_on[1 - d] if flip else side_on[d]
                if r != 1:
                    on = on & row_on(r)
                pl.when(on)(lambda r=r, d=d: act(i, r, d))

    def start_r3(i, rows):
        for_sides(i, rows, lambda i, r, d: r3(i, r, d).start(), False)

    def wait_r3(i):
        for_sides(i, (0, 1, 2), lambda i, r, d: r3(i, r, d).wait_recv(), True)

    first = (x == 0) & (h == 0)

    band = words_n // rows_all

    def band_of(hh):
        return pl.ds(pl.multiple_of(hh * band, 8), band)

    own_band = band_of(h)

    class Round:
        def __init__(self, n, first_src, src, got_h, got_x, dst, lo, hi):
            self.n, self.first_src, self.src, self.dst = n, first_src, src, dst
            self.got_h, self.got_x = got_h, got_x
            self.lo, self.hi, self.tiles = lo, hi, pl.ds(lo, hi - lo)

        def copies(self, stage):
            if stage == 0:
                trips = [
                    (self.first_src.at[self.tiles, band_of(to)], self.got_h.at[j, self.tiles], (x, to))
                    for j, to in h_peers
                ]
            elif stage == 1:
                own = self.src.at[self.tiles, own_band]
                trips = [(own, self.got_x.at[j, self.tiles], (to, h)) for j, to in x_peers]
            else:
                own = self.dst.at[self.tiles, own_band]
                trips = [(own, own, (x, to)) for j, to in h_peers]
            return [
                remote(
                    a, b, sem_txs.at[self.n, stage, j], sem_txr.at[self.n, stage, j], at_grid(*to)
                )
                for j, (a, b, to) in enumerate(trips)
            ]

        def send(self, stage):
            for copy in self.copies(stage):
                copy.start()

        def got(self, stage):
            for copy in self.copies(stage):
                copy.wait_recv()

        def sent(self):
            for stage in range(3):
                for copy in self.copies(stage):
                    copy.wait_send()

    round0 = Round(0, part0, part0, gh0, gx0, whole0, 0, nh + 2)
    round1 = Round(1, part_b, part, gh, gx, whole, 0, 3 * nh - 2)
    round2 = Round(2, part_b, part, gh, gx, whole, 3 * nh - 2, 3 * nh)

    def merged(own, parts):
        peak = own(nh)
        for p in parts:
            peak = jnp.maximum(peak, p[nh])
        f = jnp.exp2(own(nh) - peak)
        total = own(nh + 1) * f
        values = [own(i) * f[:, i : i + 1] for i in range(nh)]
        for p in parts:
            f = jnp.exp2(p[nh] - peak)
            total = total + p[nh + 1] * f
            values = [v + p[i] * f[:, i : i + 1] for i, v in enumerate(values)]
        return values, peak, total

    def merge0_h():
        round0.got(0)
        values, peak, total = merged(
            lambda a: part0[a, own_band], [gh0.at[j] for j, _ in h_peers]
        )
        for i in range(nh):
            part0[i, own_band] = values[i]
        part0[nh, own_band] = peak
        part0[nh + 1, own_band] = total
        round0.send(1)

    def merge0_x():
        round0.got(1)
        values, peak, total = merged(
            lambda a: part0[a, own_band], [gx0.at[j] for j, _ in x_peers]
        )
        for i in range(nh):
            value = values[i] / total[:, i : i + 1]
            whole0[i, own_band] = value.astype(BF16).astype(F32)
        whole0[nh, own_band] = peak + jnp.log2(total)
        whole0[nh + 1, own_band] = total
        round0.send(2)

    def launch(rnd):
        for a in range(rnd.lo, rnd.hi):
            part_b[a] = part[a].astype(BF16)
        rnd.send(0)

    def merge_h(rnd):
        rnd.got(0)
        for a in range(rnd.lo, rnd.hi):
            total = part[a, own_band]
            for j, _ in h_peers:
                total = total + gh[j, a].astype(F32)
            part[a, own_band] = total
        rnd.send(1)

    def merge_x(rnd):
        rnd.got(1)
        for a in range(rnd.lo, rnd.hi):
            total = part[a, own_band]
            for j, _ in x_peers:
                total = total + gx[j, a]
            whole[a, own_band] = total.astype(BF16)
        rnd.send(2)

    def text_scores(i):
        keys = kv[i, 0, 1, 1:3].reshape(both, HD)
        return mm_nt(keys, tq_ref[:, head_cols(half, i)]) * c2

    def words_scores(i):
        cols = head_cols(half, i)
        s = mm_nt(tk_ref[:, cols], tq_ref[:, cols]) * c2
        return jnp.where(tm_ref[:, 0:1] > 0.5, s, NEG)

    def text_partial(i):
        def one(s, v, old):
            peak = jnp.max(s, 0, keepdims=True)
            if old is not None:
                peak = jnp.maximum(peak, old[0])
            e = jnp.exp2(s - peak)
            total = jnp.sum(e, 0, keepdims=True)
            value = mm_tn(v, e.astype(BF16))
            if old is not None:
                f = jnp.exp2(old[0] - peak)
                total = total + old[1] * f
                value = value + old[2].T * f
            st[0, pl.ds(i, 1)] = peak
            st[1, pl.ds(i, 1)] = total
            part0[i] = value.T

        one(text_scores(i), kv[i, 1, 1, 1:3].reshape(both, HD), None)

        @pl.when(first)
        def _():
            old = (st[0, pl.ds(i, 1)], st[1, pl.ds(i, 1)], part0[i])
            one(words_scores(i), tv_ref[:, head_cols(half, i)], old)

    def text_start():
        part0[nh] = st[0].T
        part0[nh + 1] = st[1].T
        round0.send(0)

    def text_backward(i):
        cols = head_cols(half, i)
        row = lse[pl.ds(i, 1)]
        q = tq_ref[:, cols]
        g = tg_ref[:, cols]
        o_round = whole0[i]
        t_fin[0, i] = o_round.astype(BF16)
        delta = jnp.sum((o_round * g.astype(F32)).T, 0, keepdims=True)

        def one(s, k, v):
            p = jnp.exp2(s - row)
            ds = (p * (mm_nt(v, g) - delta)).astype(BF16)
            return (
                (mm_tn(k, ds) * scale).T,
                mm_nn(ds, q) * scale,
                mm_nn(p.astype(BF16), g),
            )

        a_q, a_k, a_v = one(
            text_scores(i), kv[i, 0, 1, 1:3].reshape(both, HD), kv[i, 1, 1, 1:3].reshape(both, HD)
        )
        part[i] = a_q
        t_kv[i, 0] = a_k
        t_kv[i, 1] = a_v

        @pl.when(first)
        def _():
            b_q, b_k, b_v = one(words_scores(i), tk_ref[:, cols], tv_ref[:, cols])
            part[i] += b_q
            part[nh + 2 * i] += b_k
            part[nh + 2 * i + 1] += b_v

    t_outs = (tout_ref, tdq_ref, tdk_ref, tdv_ref)

    def t_out(j, i):
        return remote(
            t_fin.at[j, i], t_outs[j].at[:, head_cols(half, i)],
            sem_tfs.at[j, i], sem_tfr.at[j, i], partner,
        )

    def t_loc(j, i):
        return pltpu.make_async_copy(
            t_fin.at[j, i], t_outs[j].at[:, head_cols(half, i)], sem_tfl.at[j, i]
        )

    def send_text(j, i):
        t_out(j, i).start()
        t_loc(j, i).start()

    def finish_td(i):
        for a in range(2):
            t_fin[2 + a, i] = whole[nh + 2 * i + a]
            send_text(2 + a, i)

    mask_out.start()
    mask_own.start()
    for i in range(nh):
        for j in (1, 2):
            local_in(i, j).start()
    for i, js in ((0, (1, 2)), (0, (0, 3)), (1, (1, 2)), (2, (1, 2)), (1, (0, 3)), (2, (0, 3))):
        for j in js:
            r1(i, j).start()
    for i in range(nh):
        for j in (0, 3):
            local_in(i, j).start()
    start_own(0)


    @pl.loop(0, nh)
    def _(i):
        @pl.when(jnp.logical_not(has_right))
        def _():
            g1r[i, 0] = jnp.zeros(g1r.shape[2:], BF16)

        @pl.when(jnp.logical_not(has_left))
        def _():
            g1r[i, 1] = jnp.zeros(g1r.shape[2:], BF16)

        @pl.when(jnp.logical_not(has_down))
        def _():
            g2r[i, 0] = jnp.zeros(g2r.shape[2:], BF16)

        @pl.when(jnp.logical_not(has_up))
        def _():
            g2r[i, 1] = jnp.zeros(g2r.shape[2:], BF16)

    @pl.loop(nh, 3 * nh)
    def _(a):
        part[a] = jnp.zeros(part.shape[1:], F32)

    st[...] = jnp.zeros(st.shape, F32)
    start_traded(0)
    text_partial(0)
    mask_own.wait()
    mask_out.wait_recv()

    def online(s, v, save, qs, keep):
        m_old = m_run[0:1, qs]
        m_new = jnp.maximum(m_old, jnp.max(s, 0, keepdims=True))
        alpha = jnp.exp2(m_old - m_new)
        e = jnp.exp2(s - m_new)
        l_run[0:1, qs] = l_run[0:1, qs] * alpha + jnp.sum(e, 0, keepdims=True)
        m_run[0:1, qs] = m_new
        m_saved[pl.ds(save, 1), qs] = m_new
        w = e.astype(BF16)
        keep(w)
        o_t[:, qs] = o_t[:, qs] * alpha + mm_tn(v, w)

    def fwd(i, row, col, qs, keep):
        s = mm_nt(kv[i, 0, row, col], qg[i, 0, qs]) * c2
        at = (col * 3 + row) * 2
        first = mask[pl.ds(at, 1), qs]
        last = mask[pl.ds(at + 1, 1), qs]
        s = jnp.concatenate(
            [
                jnp.where(first > 0.5, s[:tile], NEG),
                s[tile : 3 * tile],
                jnp.where(last > 0.5, s[3 * tile :], NEG),
            ],
            axis=0,
        )
        online(s, kv[i, 1, row, col], col * 3 + row, qs, keep)

    def fwd_mid(i, row, col):
        def keep(w):
            p_mid[row, col - 1] = w

        fwd(i, row, col, pl.ds(0, both), keep)

    def fwd_side(i, row, d):
        def keep(w):
            p_side[row, d] = w

        fwd(i, row, 3 * d, pl.ds(d * bq, bq), keep)

    def back(w0, k, v, q, g, save, qs):
        f = jnp.exp2(m_saved[pl.ds(save, 1), qs] - m_run[0:1, qs]) * l_run[0:1, qs]
        dp = mm_nt(v, g)
        w = w0.astype(F32) * f
        ds = (w * (dp - d_row[0:1, qs])).astype(BF16)
        d_k = mm_nn(ds, q) * scale
        d_v = mm_nn(w.astype(BF16), g)
        dq_t[:, qs] += mm_tn(k, ds)
        return d_k, d_v

    def bwd(i, row, col, qs, w0):
        d_k, d_v = back(
            w0, kv[i, 0, row, col], kv[i, 1, row, col], qg[i, 0, qs], qg[i, 1, qs],
            col * 3 + row, qs,
        )
        share[i, 0, row, col] = d_k.astype(BF16)
        share[i, 1, row, col] = d_v.astype(BF16)

    def add_g1(i):
        for_sides(i, (0, 2), lambda i, r, d: g1(i, r, d).wait_recv(), True)
        for r in (0, 2):
            @pl.when(row_on(r))
            def _(r=r):
                for a in range(2):
                    for d in range(2):
                        col = 2 - d
                        share[i, a, r, col] = (
                            share[i, a, r, col].astype(F32) + g1r[i, d, a, r].astype(F32)
                        ).astype(BF16)
        for d in range(2):
            pl.when(vert_on[d])(lambda d=d: g2(i, d).start())

    def add_g2(i):
        for_sides(i, (1,), lambda i, r, d: g1(i, r, d).wait_recv(), True)
        for d in range(2):
            pl.when(vert_on[1 - d])(lambda d=d: g2(i, d).wait_recv())
        for a in range(2):
            for s in range(2):
                total = (
                    share[i, a, 1, 1 + s].astype(F32)
                    + g1r[i, 1 - s, a, 1].astype(F32)
                    + g2r[i, 0, a, s].astype(F32)
                    + g2r[i, 1, a, s].astype(F32)
                    + t_kv[i, a, s * bq : (s + 1) * bq]
                )
                fin[i, 2 + a, s * bq : (s + 1) * bq] = total.astype(BF16)
        for j in (2, 3):
            g3(i, j).start()
            local_out(i, j).start()

    @pl.loop(0, nh)
    def _(i):
        m_run[0:1, :] = jnp.full((1, both), NEG, F32)
        l_run[0:1, :] = jnp.zeros((1, both), F32)
        o_t[...] = jnp.zeros(o_t.shape, F32)
        dq_t[...] = jnp.zeros(dq_t.shape, F32)

        wait_local(i, (0, 3))
        wait_in(i, (0, 3))

        @pl.loop(1, 3)
        def _(col):
            fwd_mid(i, 1, col)

        @pl.when(i == 0)
        def _():
            wait_r2(0)
            start_r3(0, (0, 2))
            start_own(1)
            start_traded(1)
            text_partial(1)

        @pl.when(i == 1)
        def _():
            merge0_x()

        @pl.loop(0, 4)
        def _(n):
            row = (n // 2) * 2

            @pl.when(row_on(row))
            def _():
                fwd_mid(i, row, 1 + n % 2)

        @pl.when(i == 0)
        def _():
            start_own(2)
            start_traded(2)
            text_partial(2)
            text_start()
            wait_r2(1)
            start_r3(1, (0, 2))

        @pl.when(i == 2)
        def _():
            merge_x(round1)

        words = head_cols(half, i)
        s_text = jnp.where(
            tm_ref[:, 0:1] > 0.5, mm_nt(tk_ref[:, words], qg[i, 0]) * c2, NEG
        )

        def keep_text(w):
            p_text[...] = w

        online(s_text, tv_ref[:, words], 12, pl.ds(0, both), keep_text)

        wait_r3(i)
        for d in range(2):
            @pl.when(side_on[d])
            def _(d=d):
                @pl.loop(0, 3)
                def _(row):
                    @pl.when(row_on(row))
                    def _():
                        fwd_side(i, row, d)

        @pl.when(i == 0)
        def _():
            wait_r2(2)
            start_r3(2, (0, 2))
            merge0_h()

        inv = 1.0 / l_run[0:1, :]
        l_run[0:1, :] = inv
        o_round = (o_t[...] * inv).astype(BF16).astype(F32)
        fin[i, 0] = o_round.T.astype(BF16)
        g_t = qg[i, 1].astype(F32).T
        d_row[0:1, :] = jnp.sum(o_round * g_t, 0, keepdims=True)
        g3(i, 0).start()
        local_out(i, 0).start()

        d_k, d_v = back(
            p_text[...], tk_ref[:, words], tv_ref[:, words], qg[i, 0], qg[i, 1],
            12, pl.ds(0, both),
        )
        part[nh + 2 * i] += d_k
        part[nh + 2 * i + 1] += d_v

        @pl.when(i == 2)
        def _():
            launch(round2)

        for d in range(2):
            @pl.when(side_on[d])
            def _(d=d):
                @pl.loop(0, 3)
                def _(n):
                    row = (2 * n) % 3

                    @pl.when(row_on(row))
                    def _():
                        bwd(i, row, 3 * d, pl.ds(d * bq, bq), p_side[row, d])

            if d == 0:
                @pl.when(i == 2)
                def _():
                    merge_h(round2)

            for row in (0, 2, 1):
                pl.when(side_on[d] & row_on(row))(lambda row=row, d=d: g1(i, row, d).start())

        @pl.when(i == 1)
        def _():
            round0.got(2)
            lse[...] = whole0[nh].T[0:8]

            @pl.loop(0, nh)
            def _(j):
                text_backward(j)
                send_text(0, j)

            launch(round1)

        @pl.when(i > 0)
        def _():
            add_g1(i - 1)

        for row in (0, 2, 1):
            @pl.when(row_on(row))
            def _(row=row):
                @pl.loop(1, 3)
                def _(col):
                    bwd(i, row, col, pl.ds(0, both), p_mid[row, col - 1])

            if row == 2:
                @pl.when(i == 2)
                def _():
                    merge_x(round2)

        @pl.when(i == 1)
        def _():
            merge_h(round1)

        @pl.when(i == 2)
        def _():
            round1.got(2)
            for j in range(nh):
                t_fin[1, j] = whole[j]
                send_text(1, j)
            for j in range(nh - 1):
                finish_td(j)

        @pl.when(i > 0)
        def _():
            add_g2(i - 1)

        fin[i, 1] = (dq_t[...] * scale).T.astype(BF16)
        g3(i, 1).start()
        local_out(i, 1).start()

    add_g1(nh - 1)
    round2.got(2)
    finish_td(nh - 1)
    add_g2(nh - 1)

    for rnd in (round0, round1, round2):
        rnd.sent()

    for n in range(4):
        for j in range(nh):
            t_out(n, j).wait_send()
            t_out(n, j).wait_recv()
            t_loc(n, j).wait()

    mask_out.wait_send()

    @pl.loop(0, nh)
    def _(i):
        for j in range(4):
            r1(i, j).wait_send()
            g3(i, j).wait_send()
            g3(i, j).wait_recv()
            local_out(i, j).wait()
        for d in range(2):
            @pl.when(vert_on[d])
            def _(d=d):
                r2(i, d, 0).wait_send()
                r2(i, d, 1).wait_send()
                g2(i, d).wait_send()
        for_sides(i, (0, 1, 2), lambda i, r, d: r3(i, r, d).wait_send(), False)
        for_sides(i, (0, 1, 2), lambda i, r, d: g1(i, r, d).wait_send(), False)


def window_pass(
    query, key, value, grad, mask, text_query, text_key, text_value, text_grad, text_mask
):
    nx = lax.axis_size("tm") // 2
    ny = lax.axis_size("height") // 2
    bq, channels = query.shape
    nh = channels // HD // 2
    words = text_key.shape[0]
    both = 2 * bq
    sds = jax.ShapeDtypeStruct
    hbm = pl.BlockSpec(memory_space=pl.ANY)
    vmem = pl.BlockSpec(memory_space=pltpu.VMEM)
    dma = pltpu.SemaphoreType.DMA
    return pl.pallas_call(
        functools.partial(window_kernel, nx, ny),
        out_shape=[sds((bq, channels), BF16)] * 4 + [sds((words, channels), BF16)] * 4,
        in_specs=[hbm] * 4 + [vmem] * 6,
        out_specs=[hbm] * 8,
        scratch_shapes=[
            pltpu.VMEM((nh, 2, 3, 4, bq, HD), BF16),
            pltpu.VMEM((nh, 2, both, HD), BF16),
            pltpu.VMEM((24, both), F32),
            pltpu.VMEM((3, 2, bq, both), BF16),
            pltpu.VMEM((3, 2, bq, bq), BF16),
            pltpu.VMEM((words, both), BF16),
            pltpu.VMEM((16, both), F32),
            pltpu.VMEM((8, both), F32),
            pltpu.VMEM((8, both), F32),
            pltpu.VMEM((8, both), F32),
            pltpu.VMEM((HD, both), F32),
            pltpu.VMEM((HD, both), F32),
            pltpu.VMEM((nh, 2, 3, 4, bq, HD), BF16),
            pltpu.VMEM((nh, 2, 2, 3, bq, HD), BF16),
            pltpu.VMEM((nh, 2, 2, 2, bq, HD), BF16),
            pltpu.VMEM((nh, 4, both, HD), BF16),
            pltpu.VMEM((2, HD, words), F32),
            pltpu.VMEM((8, words), F32),
            pltpu.VMEM((nh + 2, words, HD), F32),
            pltpu.VMEM((2 * ny - 1, nh + 2, words // (2 * ny), HD), F32),
            pltpu.VMEM((nx - 1, nh + 2, words // (2 * ny), HD), F32),
            pltpu.VMEM((nh + 2, words, HD), F32),
            pltpu.VMEM((3 * nh, words, HD), F32),
            pltpu.VMEM((3 * nh, words, HD), BF16),
            pltpu.VMEM((2 * ny - 1, 3 * nh, words // (2 * ny), HD), BF16),
            pltpu.VMEM((nx - 1, 3 * nh, words // (2 * ny), HD), F32),
            pltpu.VMEM((3 * nh, words, HD), BF16),
            pltpu.VMEM((nh, 2, both, HD), F32),
            pltpu.VMEM((4, nh, words, HD), BF16),
            dma((nh, 4)),
            dma((nh, 4)),
            dma((nh, 4)),
            dma((3,)),
            dma((nh, 2, 2)),
            dma((nh, 2, 2)),
            dma((nh, 3, 2)),
            dma((nh, 3, 2)),
            dma((nh, 3, 2)),
            dma((nh, 3, 2)),
            dma((nh, 2)),
            dma((nh, 2)),
            dma((nh, 4)),
            dma((nh, 4)),
            dma((nh, 4)),
            dma((3, 3, 2 * ny - 1)),
            dma((3, 3, 2 * ny - 1)),
            dma((4, nh)),
            dma((4, nh)),
            dma((4, nh)),
        ],
        compiler_params=pltpu.CompilerParams(
            collective_id=0, has_side_effects=True, vmem_limit_bytes=62 * 2**20
        ),
        name="window",
    )(query, key, value, grad, mask, text_query, text_key, text_value, text_grad, text_mask)


def settle_kernel(*refs):
    n = (len(refs) - 2) // 3
    sems_in, sems_out = refs[-2:]
    ins = [pltpu.make_async_copy(refs[j], refs[2 * n + j], sems_in.at[j]) for j in range(n)]
    outs = [pltpu.make_async_copy(refs[2 * n + j], refs[n + j], sems_out.at[j]) for j in range(n)]
    for copy in ins:
        copy.start()
    for j in range(n):
        ins[j].wait()
        outs[j].start()
    for copy in outs:
        copy.wait()


def settle(arrays):
    hbm = pl.BlockSpec(memory_space=pl.ANY)
    n = len(arrays)
    return pl.pallas_call(
        settle_kernel,
        out_shape=[jax.ShapeDtypeStruct(a.shape, a.dtype) for a in arrays],
        in_specs=[hbm] * n,
        out_specs=[hbm] * n,
        scratch_shapes=[pltpu.VMEM(a.shape, a.dtype) for a in arrays]
        + [pltpu.SemaphoreType.DMA((n,)), pltpu.SemaphoreType.DMA((n,))],
        compiler_params=pltpu.CompilerParams(vmem_limit_bytes=62 * 2**20),
        name="settle",
    )(*arrays)


def edge_mask(tile_lists, tile, slot):
    lists = tile_lists.reshape(4, 3, 3, 3)
    rows = []
    for col in (0, 3):
        on = jnp.any((lists >= 0) & (lists % 4 == col), axis=-1)
        rows.append(on)
    on = jnp.stack(rows, -1)
    on = jnp.transpose(on, (1, 2, 3, 0)).reshape(18, 4).astype(F32)
    on = jnp.repeat(on, tile, axis=1)
    pad = jnp.zeros((6, on.shape[1]), F32)
    return jnp.where(
        slot == 0, jnp.concatenate([on, pad]), jnp.concatenate([pad, on])
    )


def body(
    query_latent,
    key_latent,
    value_latent,
    grad_latent,
    tile_lists,
    text_query,
    text_key,
    text_value,
    grad_text,
    text_mask,
):
    frames, rows, width_tiles, tile, channels = query_latent.shape
    flat = [
        a.reshape(width_tiles * tile, channels)
        for a in (query_latent, key_latent, value_latent, grad_latent)
    ]
    mask = edge_mask(tile_lists, tile, lax.axis_index("tm") % 2)
    text_on = jnp.broadcast_to(
        (text_mask > 0).astype(F32)[:, None], (text_mask.shape[0], HD)
    )
    outs = window_pass(*flat, mask, text_query, text_key, text_value, grad_text, text_on)
    outs = settle(outs)
    return tuple(a.reshape(query_latent.shape) for a in outs[:4]) + tuple(outs[4:])


def solution(mesh):
    latent = P("tm", "height", None, None, "heads")
    text = P(None, "heads")
    in_specs = (latent,) * 4 + (P("tm", "height", None, None),) + (text,) * 4 + (P(),)
    out_specs = (latent,) * 4 + (text,) * 4
    return jax.shard_map(body, mesh=mesh, in_specs=in_specs, out_specs=out_specs, check_vma=False)
```

```python
import functools
import math

import jax
import jax.numpy as jnp
from jax import lax
from jax.experimental import pallas as pl
from jax.experimental.pallas import tpu as pltpu
from jax.sharding import PartitionSpec as P

HD = 128
NEG = -1e30
F32 = jnp.float32
BF16 = jnp.bfloat16
MESH = pl.DeviceIdType.MESH


def mm_nt(a, b):
    return lax.dot_general(a, b, (((1,), (1,)), ((), ())), preferred_element_type=F32)


def mm_tn(a, b):
    return lax.dot_general(a, b, (((0,), (0,)), ((), ())), preferred_element_type=F32)


def mm_nn(a, b):
    return jnp.dot(a, b, preferred_element_type=F32)


def window_kernel(
    nx,
    ny,
    q_ref,
    k_ref,
    v_ref,
    g_ref,
    mask_ref,
    tq_ref,
    tk_ref,
    tv_ref,
    tg_ref,
    tm_ref,
    out_ref,
    dq_ref,
    dk_ref,
    dv_ref,
    tout_ref,
    tdq_ref,
    tdk_ref,
    tdv_ref,
    kv,
    qg,
    mask,
    p_mid,
    p_side,
    p_text,
    m_saved,
    m_run,
    l_run,
    d_row,
    o_t,
    dq_t,
    share,
    g1r,
    g2r,
    fin,
    st,
    lse,
    part0,
    gh0,
    gx0,
    whole0,
    part,
    part_b,
    gh,
    gx,
    whole,
    t_kv,
    t_fin,
    sem_loc,
    sem_r1s,
    sem_r1r,
    sem_mask,
    sem_r2s,
    sem_r2r,
    sem_r3s,
    sem_r3r,
    sem_g1s,
    sem_g1r,
    sem_g2s,
    sem_g2r,
    sem_g3s,
    sem_g3r,
    sem_out,
    sem_txs,
    sem_txr,
    sem_tfs,
    sem_tfr,
    sem_tfl,
):
    bq = q_ref.shape[0]
    tile = bq // 4
    heads = q_ref.shape[1] // HD
    nh = heads // 2
    both = 2 * bq
    scale = 1.0 / math.sqrt(HD)
    c2 = scale * math.log2(math.e)

    t = lax.axis_index("tm")
    h = lax.axis_index("height")
    c = lax.axis_index("heads")
    x = t // 2
    zl = t % 2
    zh = h // ny
    half = (zl + zh) % 2
    other = 1 - half
    rows_all = 2 * ny

    def at_grid(xx, hh):
        return (2 * xx + (half + hh // ny) % 2, hh, c)

    partner = (2 * x + 1 - zl, h, c)
    left = (t - 2, h, c)
    right = (t + 2, h, c)
    up = at_grid(x, h - 1)
    down = at_grid(x, h + 1)
    has_left = x > 0
    has_right = x < nx - 1
    has_up = h > 0
    has_down = h < rows_all - 1

    words_n = tq_ref.shape[0]
    h_peers = [(j, (h + j + 1) % rows_all) for j in range(rows_all - 1)]
    x_peers = [(j, (x + j + 1) % nx) for j in range(nx - 1)]

    barrier = pltpu.get_barrier_semaphore()
    pl.semaphore_signal(barrier, inc=1, device_id=partner, device_id_type=MESH)
    for _, to in h_peers:
        pl.semaphore_signal(barrier, inc=1, device_id=at_grid(x, to), device_id_type=MESH)
    for _, to in x_peers:
        pl.semaphore_signal(barrier, inc=1, device_id=at_grid(to, h), device_id_type=MESH)
    pl.semaphore_wait(barrier, nx + rows_all - 1)

    def remote(src, dst, ssem, rsem, dev):
        return pltpu.make_async_remote_copy(
            src_ref=src, dst_ref=dst, send_sem=ssem, recv_sem=rsem,
            device_id=dev, device_id_type=MESH,
        )

    def head_cols(which, i):
        return pl.ds(pl.multiple_of((which * nh + i) * HD, HD), HD)

    ins = (q_ref, k_ref, v_ref, g_ref)
    outs = (out_ref, dq_ref, dk_ref, dv_ref)

    def landing(i, j):
        if j == 0:
            return qg.at[i, 0, pl.ds(pl.multiple_of(zl * bq, bq), bq)]
        if j == 3:
            return qg.at[i, 1, pl.ds(pl.multiple_of(zl * bq, bq), bq)]
        return kv.at[i, j - 1, 1, 1 + zl]

    def r1(i, j):
        return remote(
            ins[j].at[:, head_cols(other, i)], landing(i, j),
            sem_r1s.at[i, j], sem_r1r.at[i, j], partner,
        )

    def local_in(i, j):
        return pltpu.make_async_copy(
            ins[j].at[:, head_cols(half, i)], landing(i, j), sem_loc.at[i, j]
        )

    mask_cols = pl.ds(pl.multiple_of(zl * bq, bq), bq)
    mask_out = remote(mask_ref, mask.at[:, mask_cols], sem_mask.at[0], sem_mask.at[1], partner)
    mask_own = pltpu.make_async_copy(mask_ref, mask.at[:, mask_cols], sem_mask.at[2])

    def r2(i, d, s):
        return remote(
            kv.at[i, :, 1, 1 + s], kv.at[i, :, 2 - 2 * d, 1 + s],
            sem_r2s.at[i, d, s], sem_r2r.at[i, d, s], (up, down)[d],
        )

    def r3(i, r, d):
        return remote(
            kv.at[i, :, r, 1 + d], kv.at[i, :, r, 3 - 3 * d],
            sem_r3s.at[i, r, d], sem_r3r.at[i, r, d], (left, right)[d],
        )

    def g1(i, r, d):
        return remote(
            share.at[i, :, r, 3 * d], g1r.at[i, d, :, r],
            sem_g1s.at[i, r, d], sem_g1r.at[i, r, d], (left, right)[d],
        )

    def g2(i, d):
        return remote(
            share.at[i, :, 2 * d, pl.ds(1, 2)], g2r.at[i, d],
            sem_g2s.at[i, d], sem_g2r.at[i, d], (up, down)[d],
        )

    def g3(i, j):
        return remote(
            fin.at[i, j, pl.ds(pl.multiple_of((1 - zl) * bq, bq), bq)],
            outs[j].at[:, head_cols(half, i)],
            sem_g3s.at[i, j], sem_g3r.at[i, j], partner,
        )

    def local_out(i, j):
        return pltpu.make_async_copy(
            fin.at[i, j, pl.ds(pl.multiple_of(zl * bq, bq), bq)],
            outs[j].at[:, head_cols(half, i)], sem_out.at[i, j],
        )

    def row_on(r):
        return (h + r - 1 >= 0) & (h + r - 1 < rows_all)

    side_on = (has_left, has_right)
    vert_on = (has_up, has_down)

    def wait_in(i, which):
        for j in which:
            r1(i, j).wait_recv()

    def wait_local(i, which):
        for j in which:
            local_in(i, j).wait()

    def start_r2(i, s):
        for d in range(2):
            pl.when(vert_on[d])(lambda d=d: r2(i, d, s).start())

    def wait_r2(i):
        for d in range(2):
            @pl.when(vert_on[1 - d])
            def _(d=d):
                r2(i, d, 0).wait_recv()
                r2(i, d, 1).wait_recv()

    def start_own(i):
        wait_local(i, (1, 2))
        start_r2(i, zl)
        for d in range(2):
            pl.when((zl == d) & side_on[d])(lambda d=d: r3(i, 1, d).start())

    def start_traded(i):
        wait_in(i, (1, 2))
        start_r2(i, 1 - zl)
        for d in range(2):
            pl.when((zl != d) & side_on[d])(lambda d=d: r3(i, 1, d).start())

    def for_sides(i, rows, act, flip):
        for r in rows:
            for d in range(2):
                on = side_on[1 - d] if flip else side_on[d]
                if r != 1:
                    on = on & row_on(r)
                pl.when(on)(lambda r=r, d=d: act(i, r, d))

    def start_r3(i, rows):
        for_sides(i, rows, lambda i, r, d: r3(i, r, d).start(), False)

    def wait_r3(i):
        for_sides(i, (0, 1, 2), lambda i, r, d: r3(i, r, d).wait_recv(), True)

    first = (x == 0) & (h == 0)

    band = words_n // rows_all

    def band_of(hh):
        return pl.ds(pl.multiple_of(hh * band, 8), band)

    own_band = band_of(h)

    class Round:
        def __init__(self, n, first_src, src, got_h, got_x, dst, lo, hi):
            self.n, self.first_src, self.src, self.dst = n, first_src, src, dst
            self.got_h, self.got_x = got_h, got_x
            self.lo, self.hi, self.tiles = lo, hi, pl.ds(lo, hi - lo)

        def copies(self, stage):
            if stage == 0:
                trips = [
                    (self.first_src.at[self.tiles, band_of(to)], self.got_h.at[j, self.tiles], (x, to))
                    for j, to in h_peers
                ]
            elif stage == 1:
                own = self.src.at[self.tiles, own_band]
                trips = [(own, self.got_x.at[j, self.tiles], (to, h)) for j, to in x_peers]
            else:
                own = self.dst.at[self.tiles, own_band]
                trips = [(own, own, (x, to)) for j, to in h_peers]
            return [
                remote(
                    a, b, sem_txs.at[self.n, stage, j], sem_txr.at[self.n, stage, j], at_grid(*to)
                )
                for j, (a, b, to) in enumerate(trips)
            ]

        def send(self, stage):
            for copy in self.copies(stage):
                copy.start()

        def got(self, stage):
            for copy in self.copies(stage):
                copy.wait_recv()

        def sent(self):
            for stage in range(3):
                for copy in self.copies(stage):
                    copy.wait_send()

    round0 = Round(0, part0, part0, gh0, gx0, whole0, 0, nh + 2)
    round1 = Round(1, part_b, part, gh, gx, whole, 0, 3 * nh - 2)
    round2 = Round(2, part_b, part, gh, gx, whole, 3 * nh - 2, 3 * nh)

    def merged(own, parts):
        peak = own(nh)
        for p in parts:
            peak = jnp.maximum(peak, p[nh])
        f = jnp.exp2(own(nh) - peak)
        total = own(nh + 1) * f
        values = [own(i) * f[:, i : i + 1] for i in range(nh)]
        for p in parts:
            f = jnp.exp2(p[nh] - peak)
            total = total + p[nh + 1] * f
            values = [v + p[i] * f[:, i : i + 1] for i, v in enumerate(values)]
        return values, peak, total

    def merge0_h():
        round0.got(0)
        values, peak, total = merged(
            lambda a: part0[a, own_band], [gh0.at[j] for j, _ in h_peers]
        )
        for i in range(nh):
            part0[i, own_band] = values[i]
        part0[nh, own_band] = peak
        part0[nh + 1, own_band] = total
        round0.send(1)

    def merge0_x():
        round0.got(1)
        values, peak, total = merged(
            lambda a: part0[a, own_band], [gx0.at[j] for j, _ in x_peers]
        )
        for i in range(nh):
            value = values[i] / total[:, i : i + 1]
            whole0[i, own_band] = value.astype(BF16).astype(F32)
        whole0[nh, own_band] = peak + jnp.log2(total)
        whole0[nh + 1, own_band] = total
        round0.send(2)

    def launch(rnd):
        for a in range(rnd.lo, rnd.hi):
            part_b[a] = part[a].astype(BF16)
        rnd.send(0)

    def merge_h(rnd):
        rnd.got(0)
        for a in range(rnd.lo, rnd.hi):
            total = part[a, own_band]
            for j, _ in h_peers:
                total = total + gh[j, a].astype(F32)
            part[a, own_band] = total
        rnd.send(1)

    def merge_x(rnd):
        rnd.got(1)
        for a in range(rnd.lo, rnd.hi):
            total = part[a, own_band]
            for j, _ in x_peers:
                total = total + gx[j, a]
            whole[a, own_band] = total.astype(BF16)
        rnd.send(2)

    def text_scores(i):
        keys = kv[i, 0, 1, 1:3].reshape(both, HD)
        return mm_nt(keys, tq_ref[:, head_cols(half, i)]) * c2

    def words_scores(i):
        cols = head_cols(half, i)
        s = mm_nt(tk_ref[:, cols], tq_ref[:, cols]) * c2
        return jnp.where(tm_ref[:, 0:1] > 0.5, s, NEG)

    def text_partial(i):
        def one(s, v, old):
            peak = jnp.max(s, 0, keepdims=True)
            if old is not None:
                peak = jnp.maximum(peak, old[0])
            e = jnp.exp2(s - peak)
            total = jnp.sum(e, 0, keepdims=True)
            value = mm_tn(v, e.astype(BF16))
            if old is not None:
                f = jnp.exp2(old[0] - peak)
                total = total + old[1] * f
                value = value + old[2].T * f
            st[0, pl.ds(i, 1)] = peak
            st[1, pl.ds(i, 1)] = total
            part0[i] = value.T

        one(text_scores(i), kv[i, 1, 1, 1:3].reshape(both, HD), None)

        @pl.when(first)
        def _():
            old = (st[0, pl.ds(i, 1)], st[1, pl.ds(i, 1)], part0[i])
            one(words_scores(i), tv_ref[:, head_cols(half, i)], old)

    def text_start():
        part0[nh] = st[0].T
        part0[nh + 1] = st[1].T
        round0.send(0)

    def text_backward(i):
        cols = head_cols(half, i)
        row = lse[pl.ds(i, 1)]
        q = tq_ref[:, cols]
        g = tg_ref[:, cols]
        o_round = whole0[i]
        t_fin[0, i] = o_round.astype(BF16)
        delta = jnp.sum((o_round * g.astype(F32)).T, 0, keepdims=True)

        def one(s, k, v):
            p = jnp.exp2(s - row)
            ds = (p * (mm_nt(v, g) - delta)).astype(BF16)
            return (
                (mm_tn(k, ds) * scale).T,
                mm_nn(ds, q) * scale,
                mm_nn(p.astype(BF16), g),
            )

        a_q, a_k, a_v = one(
            text_scores(i), kv[i, 0, 1, 1:3].reshape(both, HD), kv[i, 1, 1, 1:3].reshape(both, HD)
        )
        part[i] = a_q
        t_kv[i, 0] = a_k
        t_kv[i, 1] = a_v

        @pl.when(first)
        def _():
            b_q, b_k, b_v = one(words_scores(i), tk_ref[:, cols], tv_ref[:, cols])
            part[i] += b_q
            part[nh + 2 * i] += b_k
            part[nh + 2 * i + 1] += b_v

    t_outs = (tout_ref, tdq_ref, tdk_ref, tdv_ref)

    def t_out(j, i):
        return remote(
            t_fin.at[j, i], t_outs[j].at[:, head_cols(half, i)],
            sem_tfs.at[j, i], sem_tfr.at[j, i], partner,
        )

    def t_loc(j, i):
        return pltpu.make_async_copy(
            t_fin.at[j, i], t_outs[j].at[:, head_cols(half, i)], sem_tfl.at[j, i]
        )

    def send_text(j, i):
        t_out(j, i).start()
        t_loc(j, i).start()

    def finish_td(i):
        for a in range(2):
            t_fin[2 + a, i] = whole[nh + 2 * i + a]
            send_text(2 + a, i)

    mask_out.start()
    mask_own.start()
    for i in range(nh):
        for j in (1, 2):
            local_in(i, j).start()
    for i, js in ((0, (1, 2)), (0, (0, 3)), (1, (1, 2)), (2, (1, 2)), (1, (0, 3)), (2, (0, 3))):
        for j in js:
            r1(i, j).start()
    for i in range(nh):
        for j in (0, 3):
            local_in(i, j).start()
    start_own(0)


    @pl.loop(0, nh)
    def _(i):
        @pl.when(jnp.logical_not(has_right))
        def _():
            g1r[i, 0] = jnp.zeros(g1r.shape[2:], BF16)

        @pl.when(jnp.logical_not(has_left))
        def _():
            g1r[i, 1] = jnp.zeros(g1r.shape[2:], BF16)

        @pl.when(jnp.logical_not(has_down))
        def _():
            g2r[i, 0] = jnp.zeros(g2r.shape[2:], BF16)

        @pl.when(jnp.logical_not(has_up))
        def _():
            g2r[i, 1] = jnp.zeros(g2r.shape[2:], BF16)

    @pl.loop(nh, 3 * nh)
    def _(a):
        part[a] = jnp.zeros(part.shape[1:], F32)

    st[...] = jnp.zeros(st.shape, F32)
    start_traded(0)
    text_partial(0)
    mask_own.wait()
    mask_out.wait_recv()

    def online(s, v, save, qs, keep):
        m_old = m_run[0:1, qs]
        m_new = jnp.maximum(m_old, jnp.max(s, 0, keepdims=True))
        alpha = jnp.exp2(m_old - m_new)
        e = jnp.exp2(s - m_new)
        l_run[0:1, qs] = l_run[0:1, qs] * alpha + jnp.sum(e, 0, keepdims=True)
        m_run[0:1, qs] = m_new
        m_saved[pl.ds(save, 1), qs] = m_new
        w = e.astype(BF16)
        keep(w)
        o_t[:, qs] = o_t[:, qs] * alpha + mm_tn(v, w)

    def fwd(i, row, col, qs, keep):
        s = mm_nt(kv[i, 0, row, col], qg[i, 0, qs]) * c2
        at = (col * 3 + row) * 2
        first = mask[pl.ds(at, 1), qs]
        last = mask[pl.ds(at + 1, 1), qs]
        s = jnp.concatenate(
            [
                jnp.where(first > 0.5, s[:tile], NEG),
                s[tile : 3 * tile],
                jnp.where(last > 0.5, s[3 * tile :], NEG),
            ],
            axis=0,
        )
        online(s, kv[i, 1, row, col], col * 3 + row, qs, keep)

    def fwd_mid(i, row, col):
        def keep(w):
            p_mid[row, col - 1] = w

        fwd(i, row, col, pl.ds(0, both), keep)

    def fwd_side(i, row, d):
        def keep(w):
            p_side[row, d] = w

        fwd(i, row, 3 * d, pl.ds(d * bq, bq), keep)

    def back(w0, k, v, q, g, save, qs):
        f = jnp.exp2(m_saved[pl.ds(save, 1), qs] - m_run[0:1, qs]) * l_run[0:1, qs]
        dp = mm_nt(v, g)
        w = w0.astype(F32) * f
        ds = (w * (dp - d_row[0:1, qs])).astype(BF16)
        d_k = mm_nn(ds, q) * scale
        d_v = mm_nn(w.astype(BF16), g)
        dq_t[:, qs] += mm_tn(k, ds)
        return d_k, d_v

    def bwd(i, row, col, qs, w0):
        d_k, d_v = back(
            w0, kv[i, 0, row, col], kv[i, 1, row, col], qg[i, 0, qs], qg[i, 1, qs],
            col * 3 + row, qs,
        )
        share[i, 0, row, col] = d_k.astype(BF16)
        share[i, 1, row, col] = d_v.astype(BF16)

    def add_g1(i):
        for_sides(i, (0, 2), lambda i, r, d: g1(i, r, d).wait_recv(), True)
        for r in (0, 2):
            @pl.when(row_on(r))
            def _(r=r):
                for a in range(2):
                    for d in range(2):
                        col = 2 - d
                        share[i, a, r, col] = (
                            share[i, a, r, col].astype(F32) + g1r[i, d, a, r].astype(F32)
                        ).astype(BF16)
        for d in range(2):
            pl.when(vert_on[d])(lambda d=d: g2(i, d).start())

    def add_g2(i):
        for_sides(i, (1,), lambda i, r, d: g1(i, r, d).wait_recv(), True)
        for d in range(2):
            pl.when(vert_on[1 - d])(lambda d=d: g2(i, d).wait_recv())
        for a in range(2):
            for s in range(2):
                total = (
                    share[i, a, 1, 1 + s].astype(F32)
                    + g1r[i, 1 - s, a, 1].astype(F32)
                    + g2r[i, 0, a, s].astype(F32)
                    + g2r[i, 1, a, s].astype(F32)
                    + t_kv[i, a, s * bq : (s + 1) * bq]
                )
                fin[i, 2 + a, s * bq : (s + 1) * bq] = total.astype(BF16)
        for j in (2, 3):
            g3(i, j).start()
            local_out(i, j).start()

    @pl.loop(0, nh)
    def _(i):
        m_run[0:1, :] = jnp.full((1, both), NEG, F32)
        l_run[0:1, :] = jnp.zeros((1, both), F32)
        o_t[...] = jnp.zeros(o_t.shape, F32)
        dq_t[...] = jnp.zeros(dq_t.shape, F32)

        wait_local(i, (0, 3))
        wait_in(i, (0, 3))

        @pl.loop(1, 3)
        def _(col):
            fwd_mid(i, 1, col)

        @pl.when(i == 0)
        def _():
            wait_r2(0)
            start_r3(0, (0, 2))
            start_own(1)
            start_traded(1)
            text_partial(1)

        @pl.when(i == 1)
        def _():
            merge0_x()

        @pl.loop(0, 4)
        def _(n):
            row = (n // 2) * 2

            @pl.when(row_on(row))
            def _():
                fwd_mid(i, row, 1 + n % 2)

        @pl.when(i == 0)
        def _():
            start_own(2)
            start_traded(2)
            text_partial(2)
            text_start()
            wait_r2(1)
            start_r3(1, (0, 2))

        @pl.when(i == 2)
        def _():
            merge_x(round1)

        words = head_cols(half, i)
        s_text = jnp.where(
            tm_ref[:, 0:1] > 0.5, mm_nt(tk_ref[:, words], qg[i, 0]) * c2, NEG
        )

        def keep_text(w):
            p_text[...] = w

        online(s_text, tv_ref[:, words], 12, pl.ds(0, both), keep_text)

        wait_r3(i)
        for d in range(2):
            @pl.when(side_on[d])
            def _(d=d):
                @pl.loop(0, 3)
                def _(row):
                    @pl.when(row_on(row))
                    def _():
                        fwd_side(i, row, d)

        @pl.when(i == 0)
        def _():
            wait_r2(2)
            start_r3(2, (0, 2))
            merge0_h()

        inv = 1.0 / l_run[0:1, :]
        l_run[0:1, :] = inv
        o_round = (o_t[...] * inv).astype(BF16).astype(F32)
        fin[i, 0] = o_round.T.astype(BF16)
        g_t = qg[i, 1].astype(F32).T
        d_row[0:1, :] = jnp.sum(o_round * g_t, 0, keepdims=True)
        g3(i, 0).start()
        local_out(i, 0).start()

        d_k, d_v = back(
            p_text[...], tk_ref[:, words], tv_ref[:, words], qg[i, 0], qg[i, 1],
            12, pl.ds(0, both),
        )
        part[nh + 2 * i] += d_k
        part[nh + 2 * i + 1] += d_v

        @pl.when(i == 2)
        def _():
            launch(round2)

        for d in range(2):
            @pl.when(side_on[d])
            def _(d=d):
                @pl.loop(0, 3)
                def _(n):
                    row = (2 * n) % 3

                    @pl.when(row_on(row))
                    def _():
                        bwd(i, row, 3 * d, pl.ds(d * bq, bq), p_side[row, d])
                        if d == 1:
                            g1(i, row, d).start()

            if d == 0:
                @pl.when(i == 2)
                def _():
                    merge_h(round2)

                for row in (0, 2, 1):
                    pl.when(side_on[0] & row_on(row))(lambda row=row: g1(i, row, 0).start())

        @pl.when(i == 1)
        def _():
            round0.got(2)
            lse[...] = whole0[nh].T[0:8]

            @pl.loop(0, nh)
            def _(j):
                text_backward(j)
                send_text(0, j)

            launch(round1)

        @pl.when(i > 0)
        def _():
            add_g1(i - 1)

        for row in (0, 2, 1):
            @pl.when(row_on(row))
            def _(row=row):
                @pl.loop(1, 3)
                def _(col):
                    bwd(i, row, col, pl.ds(0, both), p_mid[row, col - 1])

            if row == 2:
                @pl.when(i == 2)
                def _():
                    merge_x(round2)

        @pl.when(i == 1)
        def _():
            merge_h(round1)

        @pl.when(i == 2)
        def _():
            round1.got(2)
            for j in range(nh):
                t_fin[1, j] = whole[j]
                send_text(1, j)
            for j in range(nh - 1):
                finish_td(j)

        @pl.when(i > 0)
        def _():
            add_g2(i - 1)

        fin[i, 1] = (dq_t[...] * scale).T.astype(BF16)
        g3(i, 1).start()
        local_out(i, 1).start()

    add_g1(nh - 1)
    round2.got(2)
    finish_td(nh - 1)
    add_g2(nh - 1)

    for rnd in (round0, round1, round2):
        rnd.sent()

    for n in range(4):
        for j in range(nh):
            t_out(n, j).wait_send()
            t_out(n, j).wait_recv()
            t_loc(n, j).wait()

    mask_out.wait_send()

    @pl.loop(0, nh)
    def _(i):
        for j in range(4):
            r1(i, j).wait_send()
            g3(i, j).wait_send()
            g3(i, j).wait_recv()
            local_out(i, j).wait()
        for d in range(2):
            @pl.when(vert_on[d])
            def _(d=d):
                r2(i, d, 0).wait_send()
                r2(i, d, 1).wait_send()
                g2(i, d).wait_send()
        for_sides(i, (0, 1, 2), lambda i, r, d: r3(i, r, d).wait_send(), False)
        for_sides(i, (0, 1, 2), lambda i, r, d: g1(i, r, d).wait_send(), False)


def window_pass(
    query, key, value, grad, mask, text_query, text_key, text_value, text_grad, text_mask
):
    nx = lax.axis_size("tm") // 2
    ny = lax.axis_size("height") // 2
    bq, channels = query.shape
    nh = channels // HD // 2
    words = text_key.shape[0]
    both = 2 * bq
    sds = jax.ShapeDtypeStruct
    hbm = pl.BlockSpec(memory_space=pl.ANY)
    vmem = pl.BlockSpec(memory_space=pltpu.VMEM)
    dma = pltpu.SemaphoreType.DMA
    return pl.pallas_call(
        functools.partial(window_kernel, nx, ny),
        out_shape=[sds((bq, channels), BF16)] * 4 + [sds((words, channels), BF16)] * 4,
        in_specs=[hbm] * 4 + [vmem] * 6,
        out_specs=[hbm] * 8,
        scratch_shapes=[
            pltpu.VMEM((nh, 2, 3, 4, bq, HD), BF16),
            pltpu.VMEM((nh, 2, both, HD), BF16),
            pltpu.VMEM((24, both), F32),
            pltpu.VMEM((3, 2, bq, both), BF16),
            pltpu.VMEM((3, 2, bq, bq), BF16),
            pltpu.VMEM((words, both), BF16),
            pltpu.VMEM((16, both), F32),
            pltpu.VMEM((8, both), F32),
            pltpu.VMEM((8, both), F32),
            pltpu.VMEM((8, both), F32),
            pltpu.VMEM((HD, both), F32),
            pltpu.VMEM((HD, both), F32),
            pltpu.VMEM((nh, 2, 3, 4, bq, HD), BF16),
            pltpu.VMEM((nh, 2, 2, 3, bq, HD), BF16),
            pltpu.VMEM((nh, 2, 2, 2, bq, HD), BF16),
            pltpu.VMEM((nh, 4, both, HD), BF16),
            pltpu.VMEM((2, HD, words), F32),
            pltpu.VMEM((8, words), F32),
            pltpu.VMEM((nh + 2, words, HD), F32),
            pltpu.VMEM((2 * ny - 1, nh + 2, words // (2 * ny), HD), F32),
            pltpu.VMEM((nx - 1, nh + 2, words // (2 * ny), HD), F32),
            pltpu.VMEM((nh + 2, words, HD), F32),
            pltpu.VMEM((3 * nh, words, HD), F32),
            pltpu.VMEM((3 * nh, words, HD), BF16),
            pltpu.VMEM((2 * ny - 1, 3 * nh, words // (2 * ny), HD), BF16),
            pltpu.VMEM((nx - 1, 3 * nh, words // (2 * ny), HD), F32),
            pltpu.VMEM((3 * nh, words, HD), BF16),
            pltpu.VMEM((nh, 2, both, HD), F32),
            pltpu.VMEM((4, nh, words, HD), BF16),
            dma((nh, 4)),
            dma((nh, 4)),
            dma((nh, 4)),
            dma((3,)),
            dma((nh, 2, 2)),
            dma((nh, 2, 2)),
            dma((nh, 3, 2)),
            dma((nh, 3, 2)),
            dma((nh, 3, 2)),
            dma((nh, 3, 2)),
            dma((nh, 2)),
            dma((nh, 2)),
            dma((nh, 4)),
            dma((nh, 4)),
            dma((nh, 4)),
            dma((3, 3, 2 * ny - 1)),
            dma((3, 3, 2 * ny - 1)),
            dma((4, nh)),
            dma((4, nh)),
            dma((4, nh)),
        ],
        compiler_params=pltpu.CompilerParams(
            collective_id=0, has_side_effects=True, vmem_limit_bytes=62 * 2**20
        ),
        name="window",
    )(query, key, value, grad, mask, text_query, text_key, text_value, text_grad, text_mask)


def settle_kernel(*refs):
    n = (len(refs) - 2) // 3
    sems_in, sems_out = refs[-2:]
    ins = [pltpu.make_async_copy(refs[j], refs[2 * n + j], sems_in.at[j]) for j in range(n)]
    outs = [pltpu.make_async_copy(refs[2 * n + j], refs[n + j], sems_out.at[j]) for j in range(n)]
    for copy in ins:
        copy.start()
    for j in range(n):
        ins[j].wait()
        outs[j].start()
    for copy in outs:
        copy.wait()


def settle(arrays):
    hbm = pl.BlockSpec(memory_space=pl.ANY)
    n = len(arrays)
    return pl.pallas_call(
        settle_kernel,
        out_shape=[jax.ShapeDtypeStruct(a.shape, a.dtype) for a in arrays],
        in_specs=[hbm] * n,
        out_specs=[hbm] * n,
        scratch_shapes=[pltpu.VMEM(a.shape, a.dtype) for a in arrays]
        + [pltpu.SemaphoreType.DMA((n,)), pltpu.SemaphoreType.DMA((n,))],
        compiler_params=pltpu.CompilerParams(vmem_limit_bytes=62 * 2**20),
        name="settle",
    )(*arrays)


def edge_mask(tile_lists, tile, slot):
    lists = tile_lists.reshape(4, 3, 3, 3)
    rows = []
    for col in (0, 3):
        on = jnp.any((lists >= 0) & (lists % 4 == col), axis=-1)
        rows.append(on)
    on = jnp.stack(rows, -1)
    on = jnp.transpose(on, (1, 2, 3, 0)).reshape(18, 4).astype(F32)
    on = jnp.repeat(on, tile, axis=1)
    pad = jnp.zeros((6, on.shape[1]), F32)
    return jnp.where(
        slot == 0, jnp.concatenate([on, pad]), jnp.concatenate([pad, on])
    )


def body(
    query_latent,
    key_latent,
    value_latent,
    grad_latent,
    tile_lists,
    text_query,
    text_key,
    text_value,
    grad_text,
    text_mask,
):
    frames, rows, width_tiles, tile, channels = query_latent.shape
    flat = [
        a.reshape(width_tiles * tile, channels)
        for a in (query_latent, key_latent, value_latent, grad_latent)
    ]
    mask = edge_mask(tile_lists, tile, lax.axis_index("tm") % 2)
    text_on = jnp.broadcast_to(
        (text_mask > 0).astype(F32)[:, None], (text_mask.shape[0], HD)
    )
    outs = window_pass(*flat, mask, text_query, text_key, text_value, grad_text, text_on)
    outs = settle(outs)
    return tuple(a.reshape(query_latent.shape) for a in outs[:4]) + tuple(outs[4:])


def solution(mesh):
    latent = P("tm", "height", None, None, "heads")
    text = P(None, "heads")
    in_specs = (latent,) * 4 + (P("tm", "height", None, None),) + (text,) * 4 + (P(),)
    out_specs = (latent,) * 4 + (text,) * 4
    return jax.shard_map(body, mesh=mesh, in_specs=in_specs, out_specs=out_specs, check_vma=False)
```
